32 devices in a mesh: patch: 16 (over z, y, core), fsdp: 2 (over x).
Axes of the slice: x: 2, y: 2, z: 4, core: 2. Of those that a mesh axis runs over, the one named last changes fastest.
Arguments:
- image: bfloat16 [2048, 3072], P('patch'), may hold values from -6 to 6
- mod_shift: float32 [3072], replicated, may hold values from -3 to 3
- mod_scale: float32 [3072], replicated, may hold values from -2.5 to 2.5
- mod_gate: float32 [3072], replicated, may hold values from -4 to 4
- w_query: bfloat16 [3072, 2048], P('patch', 'fsdp'), may hold values from -0.109375 to 0.109375
- w_key: bfloat16 [3072, 2048], P('patch', 'fsdp'), may hold values from -0.109375 to 0.109375
- w_value: bfloat16 [3072, 2048], P('patch', 'fsdp'), may hold values from -0.109375 to 0.109375
- query_gain: float32 [128], replicated, may hold values from 1.5 to 160
- key_gain: float32 [128], replicated, may hold values from 0.1 to 1.9
- text_keys: bfloat16 [512, 2048], P(None, 'fsdp'), may hold values from -6 to 6
- text_values: bfloat16 [512, 2048], P(None, 'fsdp'), may hold values from -6 to 6
- stale_keys: bfloat16 [2048, 2048], P('patch', 'fsdp'), may hold values from -6 to 6
- stale_values: bfloat16 [2048, 2048], P('patch', 'fsdp'), may hold values from -6 to 6
- w_out: bfloat16 [2048, 3072], P('fsdp', 'patch'), may hold values from -0.125 to 0.125
Outputs:
- hidden: bfloat16 [2048, 3072], P('patch', 'fsdp')
- fresh_keys: bfloat16 [2048, 2048], P('patch', 'fsdp')
- fresh_values: bfloat16 [2048, 2048], P('patch', 'fsdp')
The draws below stay inside these ranges and needn't reach their ends.
All inputs are finite; a program needn't handle non-finite values.
Results may differ from the reference program's by a relative error of at most 0.013.
Values may be sent and summed in bfloat16 or wider, within the bound.
No kernel may reach another device: no remote copies, remote signals or barrier semaphores. Data moves between devices by JAX's collectives and lax.ppermute only.
A program may use at most 128 MiB of HBM per device.

```python
import math
import jax
import jax.numpy as jnp
from jax import lax

D = 3072
HEADS = 16
HD = 128
TXT = 512
IMG_DEV = 128
IMG = 2048
N_PATCH = 16


def draw_query_gain(key, part):
    key = jax.random.fold_in(key, 7)
    return jax.random.uniform(key, (HD,), jnp.float32, 1.5, 3.0)


def draw_stale_keys(key, part):
    key = jax.random.fold_in(key, 13)
    base_key = jax.random.fold_in(key, 0)
    return jnp.clip(jax.random.normal(base_key, (IMG, HEADS * HD), jnp.float32), -6.0, 6.0).astype(jnp.bfloat16)


def levels(stream_key, dims, cuts, least, high):
    factor_of, own = 1.0, jax.random.fold_in(stream_key, 6)
    for position, parts in cuts:
        steps = jnp.exp(jax.random.uniform(jax.random.fold_in(own, position), (parts,), jnp.float32, least / len(cuts), high / len(cuts)))
        factor_of = factor_of * jnp.repeat(steps, dims[position] // parts).reshape([-1 if axis == position else 1 for axis in range(len(dims))])
    return factor_of


def noise(own_key, extent, scale, limit, pieces=(), held_as=jnp.bfloat16):
    entries = jax.random.normal(own_key, extent, jnp.float32) * scale
    if len(pieces) > 0:
        entries = levels(own_key, extent, pieces, -0.22, 0.18) * entries
    return jnp.clip(entries, min=-limit, max=limit).astype(held_as)


def setup_inputs(seed: int = 0) -> dict:
    arg_keys = jax.random.split(jax.random.key(seed), 15)
    image = noise(arg_keys[0], (IMG, D), 1.0, 6.0, ((0, 16),))
    mod_shift = noise(arg_keys[1], (D,), 0.5, 3.0, (), jnp.float32)
    mod_scale = noise(arg_keys[2], (D,), 0.4, 2.5, (), jnp.float32)
    mod_gate = noise(arg_keys[3], (D,), 1.0, 4.0, (), jnp.float32)
    w_query = noise(arg_keys[4], (D, HEADS * HD), D ** -0.5, 0.109375, ((0, 16), (1, 2)))
    w_key = noise(arg_keys[5], (D, HEADS * HD), D ** -0.5, 0.109375, ((0, 16), (1, 2)))
    w_value = noise(arg_keys[6], (D, HEADS * HD), D ** -0.5, 0.109375, ((0, 16), (1, 2)))
    query_gain = draw_query_gain(jax.random.fold_in(arg_keys[14], 71), 0)
    key_gain = jnp.clip(1.0 + 0.18 * jax.random.normal(arg_keys[8], (HD,), jnp.float32), 0.1, 1.9)
    text_keys = noise(arg_keys[9], (TXT, HEADS * HD), 1.0, 6.0, ((1, 2),))
    text_values = noise(arg_keys[10], (TXT, HEADS * HD), 1.0, 6.0, ((1, 2),))
    stale_keys = draw_stale_keys(jax.random.fold_in(arg_keys[14], 71), 0)
    stale_values = noise(arg_keys[12], (IMG, HEADS * HD), 1.0, 6.0, ((0, 16), (1, 2)))
    w_out = noise(arg_keys[13], (HEADS * HD, D), (HEADS * HD) ** -0.5, 0.125, ((0, 2), (1, 16)))
    return {"image": image, "mod_shift": mod_shift, "mod_scale": mod_scale, "mod_gate": mod_gate, "w_query": w_query, "w_key": w_key, "w_value": w_value, "query_gain": query_gain, "key_gain": key_gain, "text_keys": text_keys, "text_values": text_values, "stale_keys": stale_keys, "stale_values": stale_values, "w_out": w_out}


def modulate(image, mod_shift, mod_scale):
    values = image.astype(jnp.float32)
    center = lax.optimization_barrier(jnp.mean(values, axis=-1, keepdims=True))
    spread = lax.optimization_barrier(jnp.mean(jnp.square(values - center), axis=-1, keepdims=True))
    normed = (values - center) * lax.rsqrt(spread + 1e-06)
    return ((1.0 + mod_scale) * normed + mod_shift).astype(jnp.bfloat16)

def head_norm(projected, gain, head_size):
    count = projected.shape[0]
    shaped = projected.reshape(count, -1, head_size)
    power = lax.optimization_barrier(jnp.mean(shaped * shaped, axis=-1, keepdims=True))
    return (shaped * lax.rsqrt(power + 1e-06) * gain).astype(jnp.bfloat16).reshape(count, -1)

def reference(image, mod_shift, mod_scale, mod_gate, w_query, w_key, w_value, query_gain, key_gain, text_keys, text_values, stale_keys, stale_values, w_out):
    modded = modulate(image, mod_shift, mod_scale)
    queries = head_norm(jnp.dot(modded, w_query, preferred_element_type=jnp.float32), query_gain, HD)
    key_new = head_norm(jnp.dot(modded, w_key, preferred_element_type=jnp.float32), key_gain, HD)
    value_new = jnp.dot(modded, w_value, preferred_element_type=jnp.float32).astype(jnp.bfloat16)
    factor = 1.0 / math.sqrt(HD)

    def attend(patch_index):
        start = (patch_index * IMG_DEV).astype(jnp.int32)
        query_block = lax.dynamic_slice_in_dim(queries, start, IMG_DEV, 0).astype(jnp.float32).reshape(IMG_DEV, HEADS, HD)
        key_image = lax.dynamic_update_slice_in_dim(stale_keys, lax.dynamic_slice_in_dim(key_new, start, IMG_DEV, 0), start, 0)
        value_image = lax.dynamic_update_slice_in_dim(stale_values, lax.dynamic_slice_in_dim(value_new, start, IMG_DEV, 0), start, 0)
        key_all = jnp.concatenate([text_keys, key_image], axis=0).astype(jnp.float32).reshape(-1, HEADS, HD)
        value_all = jnp.concatenate([text_values, value_image], axis=0).astype(jnp.float32).reshape(-1, HEADS, HD)
        scores = jnp.einsum('rhd,khd->hrk', query_block, key_all) * factor
        largest = lax.optimization_barrier(jnp.max(scores, axis=-1, keepdims=True))
        expos = jnp.exp(scores - largest)
        weights = (expos / lax.optimization_barrier(jnp.sum(expos, axis=-1, keepdims=True))).astype(jnp.bfloat16)
        mixture = jnp.einsum('hrk,khd->rhd', weights.astype(jnp.float32), value_all)
        return mixture.astype(jnp.bfloat16).reshape(IMG_DEV, HEADS * HD)
    blocks = lax.map(attend, jnp.arange(N_PATCH, dtype=jnp.int32))
    attended = blocks.reshape(IMG, HEADS * HD)
    projected = jnp.dot(attended, w_out, preferred_element_type=jnp.float32)
    hidden = (image.astype(jnp.float32) + mod_gate * projected).astype(jnp.bfloat16)
    return (hidden, key_new, value_new)
```

```python
import functools
import math

import jax
import jax.numpy as jnp
from jax import lax
from jax.experimental import pallas as pl
from jax.experimental.pallas import tpu as pltpu
from jax.sharding import PartitionSpec as P

INNER = 4
VMEM_BYTES = 60 * 1024 * 1024


def modulate(image, mod_shift, mod_scale):
    values = image.astype(jnp.float32)
    center = jnp.mean(values, axis=-1, keepdims=True)
    spread = jnp.mean(jnp.square(values - center), axis=-1, keepdims=True)
    normed = (values - center) * lax.rsqrt(spread + 1e-06)
    return ((1.0 + mod_scale) * normed + mod_shift).astype(jnp.bfloat16)


def after(x, *deps):
    return lax.optimization_barrier((x,) + deps)[0]


def nt_dot(a, b):
    return lax.dot_general(a, b, (((1,), (1,)), ((), ())), preferred_element_type=jnp.float32)


def patch_kernel(depth, head_size, n_pieces, counts, where_ref, *refs):
    n_shares, n_patches = sum(counts), len(counts)
    shares, refs = refs[:n_shares], refs[n_shares:]
    tk_ref, tv_ref, qg_ref, kg_ref = refs[:4]
    pieces, refs = refs[4 : 4 + n_pieces], refs[4 + n_pieces :]
    att_refs, kv_refs = refs[:n_patches], refs[n_patches : 2 * n_patches]
    held, scores, expos, sems = refs[2 * n_patches :]
    rows, width = att_refs[0].shape
    groups = [slice(g * rows, (g + 1) * rows) for g in range(n_patches)]
    owns, firsts, at = [], [], 1 + n_pieces
    for count in counts:
        owns.append(where_ref[at])
        firsts.append([where_ref[at + 1 + i] for i in range(count)])
        at += 1 + count
    copies = [
        pltpu.make_async_copy(piece, held.at[where_ref[1 + i]], sems.at[i])
        for i, piece in enumerate(pieces)
    ]
    for copy in copies:
        copy.start()

    def put(refs, cols, value):
        for g, group in enumerate(groups):
            share = rows // counts[g]
            for i, first in enumerate(firsts[g]):
                start = group.start + i * share
                refs[g][pl.ds(pl.multiple_of(first, 16), share), cols] = value[start : start + share]

    chunk = INNER * depth
    proj = [jnp.zeros((n_patches * rows, width), jnp.float32) for _ in range(3)]
    if chunk % 128 == 0:
        for first in range(0, n_pieces, INNER):
            for copy in copies[first : first + INNER]:
                copy.wait()
            place = where_ref[1 + first] // INNER
            cols = pl.ds(pl.multiple_of(place * chunk, 128), chunk)
            part = jnp.concatenate([x[:, cols] for x in shares], axis=0)
            for i in range(3):
                weight = held[pl.ds(place * INNER, INNER), i * depth : (i + 1) * depth, :]
                proj[i] += jnp.dot(
                    part, weight.reshape(chunk, width), preferred_element_type=jnp.float32
                )
    else:
        for copy in copies:
            copy.wait()
        part = jnp.concatenate([x[...] for x in shares], axis=0)
        for i in range(3):
            weight = held[:, i * depth : (i + 1) * depth, :]
            proj[i] += jnp.dot(
                part, weight.reshape(n_pieces * depth, width), preferred_element_type=jnp.float32
            )
    q_proj, k_proj, v_proj = proj

    def norm(x, gain):
        power = jnp.mean(x * x, axis=-1, keepdims=True)
        return (x * lax.rsqrt(power + 1e-06) * gain).astype(jnp.bfloat16)

    v_new = v_proj.astype(jnp.bfloat16)
    put(kv_refs, slice(width, 2 * width), v_new)
    k0, v0 = 3 * depth, 3 * depth + rows
    scale = math.log2(math.e) / math.sqrt(head_size)
    for h in range(width // head_size):
        cols = slice(h * head_size, (h + 1) * head_size)
        key = norm(k_proj[:, cols], kg_ref[...])
        put(kv_refs, cols, key)
        query = norm(q_proj[:, cols], qg_ref[...])
        value = v_new[:, cols]
        keys = held[:, k0 : k0 + rows, cols].reshape(n_pieces * rows, head_size)
        values = held[:, v0 : v0 + rows, cols].reshape(n_pieces * rows, head_size)
        scores[...] = nt_dot(query, keys)
        own_cols = [pl.ds(pl.multiple_of(own * rows, 128), rows) for own in owns]
        for g, group in enumerate(groups):
            scores[group, own_cols[g]] = nt_dot(query[group], key[group])
        text_s = nt_dot(query, tk_ref[:, cols])
        image_s = scores[...]
        largest = jnp.maximum(
            jnp.max(text_s, axis=-1, keepdims=True), jnp.max(image_s, axis=-1, keepdims=True)
        )
        text_e = jnp.exp2((text_s - largest) * scale)
        image_e = jnp.exp2((image_s - largest) * scale)
        total = jnp.sum(text_e, axis=-1, keepdims=True) + jnp.sum(image_e, axis=-1, keepdims=True)
        expos[...] = image_e.astype(jnp.bfloat16)
        fresh_mix = []
        for g, group in enumerate(groups):
            fresh_mix.append(
                jnp.dot(expos[group, own_cols[g]], value[group], preferred_element_type=jnp.float32)
            )
            expos[group, own_cols[g]] = jnp.zeros((rows, rows), jnp.bfloat16)
        mixture = (
            jnp.dot(text_e.astype(jnp.bfloat16), tv_ref[:, cols], preferred_element_type=jnp.float32)
            + jnp.dot(expos[...], values, preferred_element_type=jnp.float32)
            + jnp.concatenate(fresh_mix, axis=0)
        )
        put(att_refs, cols, (mixture / total).astype(jnp.bfloat16))


def attend_patches(where, patches, text_keys, text_values, query_gain, key_gain, pieces, depth, width):
    shares = [x for patch in patches for x in patch]
    model_width = shares[0].shape[1]
    rows = sum(x.shape[0] for x in patches[0])
    n = len(patches)
    head_size = query_gain.shape[0]
    texts = text_keys.shape[0]
    n_pieces = len(pieces)
    whole = lambda i, w: (0, 0)
    outs = [width] * n + [2 * width] * n
    out = pl.pallas_call(
        functools.partial(patch_kernel, depth, head_size, n_pieces, [len(x) for x in patches]),
        grid_spec=pltpu.PrefetchScalarGridSpec(
            num_scalar_prefetch=1,
            grid=(1,),
            in_specs=[pl.BlockSpec(x.shape, whole) for x in shares]
            + [
                pl.BlockSpec((texts, width), lambda i, w: (0, w[0])),
                pl.BlockSpec((texts, width), lambda i, w: (0, w[0])),
                pl.BlockSpec((1, head_size), whole),
                pl.BlockSpec((1, head_size), whole),
            ]
            + [pl.BlockSpec(memory_space=pl.ANY)] * n_pieces,
            out_specs=[pl.BlockSpec((rows, x), whole) for x in outs],
            scratch_shapes=[
                pltpu.VMEM((n_pieces,) + pieces[0].shape, jnp.bfloat16),
                pltpu.VMEM((n * rows, n_pieces * rows), jnp.float32),
                pltpu.VMEM((n * rows, n_pieces * rows), jnp.bfloat16),
                pltpu.SemaphoreType.DMA((n_pieces,)),
            ],
        ),
        out_shape=[jax.ShapeDtypeStruct((rows, x), jnp.bfloat16) for x in outs],
        compiler_params=pltpu.CompilerParams(vmem_limit_bytes=VMEM_BYTES),
        cost_estimate=pl.CostEstimate(
            flops=2 * n * rows * (model_width * 3 * width + 2 * (texts + n_pieces * rows) * width),
            bytes_accessed=2 * n_pieces * pieces[0].size,
            transcendentals=n * rows * (texts + n_pieces * rows) * (width // head_size),
        ),
    )(
        where,
        *shares,
        text_keys,
        text_values,
        query_gain.reshape(1, -1),
        key_gain.reshape(1, -1),
        *pieces,
    )
    return out[:n], out[n:]


def deal_kernel(n_arrays, team, member_ref, *refs):
    arrays, outs = refs[:n_arrays], refs[n_arrays:]
    width = outs[0].shape[1]
    for k in range(team):
        at = lax.rem(member_ref[0] + k, team)
        cols = pl.ds(pl.multiple_of(at * width, 128), width)
        first = 0
        for x in arrays:
            rows = x.shape[0]
            outs[k][first : first + rows, :] = x[:, cols]
            first += rows


def deal(member, arrays, team):
    width = arrays[0].shape[1] // team
    shape = jax.ShapeDtypeStruct((sum(x.shape[0] for x in arrays), width), jnp.bfloat16)
    return pl.pallas_call(
        functools.partial(deal_kernel, len(arrays), team),
        in_specs=[pl.BlockSpec(memory_space=pltpu.SMEM)]
        + [pl.BlockSpec(memory_space=pltpu.VMEM)] * len(arrays),
        out_specs=[pl.BlockSpec(memory_space=pltpu.VMEM)] * team,
        out_shape=[shape] * team,
        compiler_params=pltpu.CompilerParams(vmem_limit_bytes=VMEM_BYTES),
    )(member.reshape(1), *arrays)


def collect_kernel(team, member_ref, *refs):
    packs, outs = refs[:team], refs[team:]
    width = outs[0].shape[1] // team
    for s in range(team):
        at = lax.rem(member_ref[0] + s, team)
        cols = pl.ds(pl.multiple_of(at * width, 128), width)
        for i, out in enumerate(outs):
            out[:, cols] = packs[s][:, i * width : (i + 1) * width]


def collect(member, packs):
    team = len(packs)
    rows, double = packs[0].shape
    shape = jax.ShapeDtypeStruct((rows, double // 2 * team), jnp.bfloat16)
    return pl.pallas_call(
        functools.partial(collect_kernel, team),
        in_specs=[pl.BlockSpec(memory_space=pltpu.SMEM)]
        + [pl.BlockSpec(memory_space=pltpu.VMEM)] * team,
        out_specs=[pl.BlockSpec(memory_space=pltpu.VMEM)] * 2,
        out_shape=[shape, shape],
        compiler_params=pltpu.CompilerParams(vmem_limit_bytes=VMEM_BYTES),
    )(member.reshape(1), *packs)


def project_kernel(team, where_ref, *refs):
    packs, w_ref, out_ref = refs[:team], refs[team], refs[team + 1]
    width = w_ref.shape[1] // team
    total = jnp.zeros(out_ref.shape, jnp.float32)
    for s in range(team):
        at = lax.rem(where_ref[0] + s, team)
        cols = pl.ds(pl.multiple_of(at * width, 128), width)
        total += nt_dot(packs[s][...], w_ref[:, cols])
    out_ref[...] = total.astype(out_ref.dtype)


def project(where, packs, w_rows, share, dtype):
    rows, width = packs[0].shape
    local_width = w_rows.shape[1]
    steps = 3 if share % (3 * 256) == 0 else 1
    block = share // steps
    return pl.pallas_call(
        functools.partial(project_kernel, len(packs)),
        grid_spec=pltpu.PrefetchScalarGridSpec(
            num_scalar_prefetch=1,
            grid=(steps,),
            in_specs=[pl.BlockSpec((rows, width), lambda i, w: (0, 0))] * len(packs)
            + [pl.BlockSpec((block, local_width), lambda i, w: (w[1] * steps + i, 0))],
            out_specs=pl.BlockSpec((rows, block), lambda i, w: (0, i)),
        ),
        out_shape=jax.ShapeDtypeStruct((rows, share), dtype),
        compiler_params=pltpu.CompilerParams(vmem_limit_bytes=VMEM_BYTES),
        cost_estimate=pl.CostEstimate(
            flops=2 * rows * share * local_width,
            bytes_accessed=2 * share * local_width,
            transcendentals=0,
        ),
    )(where, *packs, w_rows)


def on_device(
    image,
    mod_shift,
    mod_scale,
    mod_gate,
    w_query,
    w_key,
    w_value,
    query_gain,
    key_gain,
    text_keys,
    text_values,
    stale_keys,
    stale_values,
    w_out,
):
    head_size = query_gain.shape[0]
    rows, model_width = image.shape
    depth, local_width = w_query.shape
    heads = local_width // head_size
    patches = lax.axis_size("patch")
    fsdp = lax.axis_size("fsdp")
    outer = patches // INNER
    team = math.gcd(outer, heads)
    width = local_width // team
    me = lax.axis_index("patch")
    mine = lax.axis_index("fsdp")
    place, seat = me // INNER, me % INNER
    member = place % team

    def along_outer(x, step):
        return lax.ppermute(
            x, "patch", [(p, (p + step * INNER) % patches) for p in range(patches)]
        )

    def along_team(x, step):
        pairs = []
        for p in range(patches):
            z = p // INNER
            to = z - z % team + (z % team + step) % team
            pairs.append((p, to * INNER + p % INNER))
        return lax.ppermute(x, "patch", pairs)

    def flip(x, bit):
        return lax.ppermute(x, "patch", [(p, p ^ bit) for p in range(patches)])

    def along_fsdp(x, step):
        return lax.ppermute(x, "fsdp", [(i, (i + step) % fsdp) for i in range(fsdp)])

    def steps_of(count):
        return sorted(range(1, count), key=lambda s: (min(s, count - s), s))

    w_rows = lax.all_gather(w_out.T, "patch", axis=0, tiled=True)
    dealt = deal(member, (w_query, w_key, w_value, stale_keys, stale_values), team)
    modded = modulate(image, mod_shift, mod_scale)
    share = rows // fsdp
    part = lax.dynamic_slice_in_dim(modded, mine * share, share, axis=0)

    pieces, origins, sent, incoming = {}, {}, [], {0: [modded]}

    def send_rows(s):
        got = along_team(after(part, *sent[-2:-1]), s)
        sent.append(got)
        incoming[s] = [got] + [along_fsdp(got, i) for i in range(1, fsdp)]

    def spread(s, piece):
        side = flip(piece, 2)
        pieces[s] = [piece, side, flip(piece, 1), flip(side, 1)]
        source = (place + (outer - s)) % outer
        origins[s] = [source * INNER + (seat ^ bits) for bits in (0, 2, 1, 3)]

    team_order, order = steps_of(team), steps_of(outer)
    for s in team_order[:-1]:
        send_rows(s)
    spread(0, dealt[0])
    for s in order:
        piece = along_outer(after(dealt[s % team], *sent[-2:-1]), s)
        sent.append(piece)
        spread(s, piece)
    for s in team_order[-1:]:
        send_rows(s)

    all_pieces = [x for s in [0] + order for x in pieces[s]]
    all_origins = [o for s in [0] + order for o in origins[s]]
    attended, fresh = {}, {}
    last = []
    for batch in ([0] + team_order[:-1], team_order[-1:]):
        if not batch:
            continue
        where = [member] + all_origins
        for s in batch:
            where.append((place - member + (member + team - s) % team) * INNER + seat)
            where += [((mine + (fsdp - i)) % fsdp) * share for i in range(fsdp)] if s else [0 * mine]
        att, kv = attend_patches(
            after(jnp.stack(where).astype(jnp.int32), *last),
            [incoming[s] for s in batch],
            text_keys,
            text_values,
            query_gain,
            key_gain,
            all_pieces,
            depth,
            width,
        )
        for s, a, f in zip(batch, att, kv):
            attended[s] = along_team(a, team - s) if s else a
            fresh[s] = along_team(f, team - s) if s else f
            last += [attended[s], fresh[s]]
    packs = [attended[s] for s in range(team)]
    out_share = model_width // fsdp
    received = []
    for i in range(1, fsdp):
        where = jnp.stack([member, (mine + i) % fsdp]).astype(jnp.int32)
        received.append(along_fsdp(project(where, packs, w_rows, out_share, jnp.bfloat16), i))
    where = jnp.stack([member, mine]).astype(jnp.int32)
    summed = project(where, packs, w_rows, out_share, jnp.float32)
    fresh = [fresh[s] for s in range(team)]
    key_out, value_out = collect(member, [after(fresh[0], summed)] + fresh[1:])
    for x in received:
        summed = summed + x.astype(jnp.float32)
    col_start = mine * out_share
    image_part = lax.dynamic_slice_in_dim(image, col_start, out_share, 1).astype(jnp.float32)
    gate_part = lax.dynamic_slice_in_dim(mod_gate, col_start, out_share, 0)
    hidden = (image_part + gate_part * summed).astype(jnp.bfloat16)
    return (hidden, key_out, value_out)


def solution(mesh):
    return jax.shard_map(
        on_device,
        mesh=mesh,
        in_specs=(
            P("patch", None),
            P(),
            P(),
            P(),
            P("patch", "fsdp"),
            P("patch", "fsdp"),
            P("patch", "fsdp"),
            P(),
            P(),
            P(None, "fsdp"),
            P(None, "fsdp"),
            P("patch", "fsdp"),
            P("patch", "fsdp"),
            P("fsdp", "patch"),
        ),
        out_specs=(P("patch", "fsdp"), P("patch", "fsdp"), P("patch", "fsdp")),
        check_vma=False,
    )
```

```python
import functools
import math

import jax
import jax.numpy as jnp
from jax import lax
from jax.experimental import pallas as pl
from jax.experimental.pallas import tpu as pltpu
from jax.sharding import PartitionSpec as P

INNER = 4
VMEM_BYTES = 60 * 1024 * 1024


def modulate(image, mod_shift, mod_scale):
    values = image.astype(jnp.float32)
    center = jnp.mean(values, axis=-1, keepdims=True)
    spread = jnp.mean(jnp.square(values - center), axis=-1, keepdims=True)
    normed = (values - center) * lax.rsqrt(spread + 1e-06)
    return ((1.0 + mod_scale) * normed + mod_shift).astype(jnp.bfloat16)


def after(x, *deps):
    return lax.optimization_barrier((x,) + deps)[0]


def nt_dot(a, b):
    return lax.dot_general(a, b, (((1,), (1,)), ((), ())), preferred_element_type=jnp.float32)


def patch_kernel(depth, head_size, n_pieces, counts, where_ref, *refs):
    n_shares, n_patches = sum(counts), len(counts)
    shares, refs = refs[:n_shares], refs[n_shares:]
    tk_ref, tv_ref, qg_ref, kg_ref = refs[:4]
    pieces, refs = refs[4 : 4 + n_pieces], refs[4 + n_pieces :]
    att_refs, refs = refs[: n_patches // 2], refs[n_patches // 2 :]
    kv_refs, (held, scores, expos, sems) = refs[:n_patches], refs[n_patches:]
    rows, width = kv_refs[0].shape[0], kv_refs[0].shape[1] // 2
    groups = [slice(g * rows, (g + 1) * rows) for g in range(n_patches)]
    owns, firsts, at = [], [], 1 + n_pieces
    for count in counts:
        owns.append(where_ref[at])
        firsts.append([where_ref[at + 1 + i] for i in range(count)])
        at += 1 + count
    copies = [
        pltpu.make_async_copy(piece, held.at[where_ref[1 + i]], sems.at[i])
        for i, piece in enumerate(pieces)
    ]
    for copy in copies:
        copy.start()

    def put(ref_of, cols, value):
        for g, group in enumerate(groups):
            ref, base = ref_of(g)
            share = rows // counts[g]
            for i, first in enumerate(firsts[g]):
                start = group.start + i * share
                to = pl.ds(pl.multiple_of(base + first, 16), share)
                ref[to, cols] = value[start : start + share]

    def kv_of(g):
        return kv_refs[g], 0

    def att_of(g):
        return att_refs[g // 2], lax.rem(owns[g] // INNER, 2) * rows

    def rows_of(cols):
        return jnp.concatenate([x[:, cols] for x in shares], axis=0)

    chunk = INNER * depth
    proj = [jnp.zeros((n_patches * rows, width), jnp.float32) for _ in range(3)]
    if chunk % 128 == 0:
        for first in range(0, n_pieces, INNER):
            for copy in copies[first : first + INNER]:
                copy.wait()
            place = where_ref[1 + first] // INNER
            cols = pl.ds(pl.multiple_of(place * chunk, 128), chunk)
            part = rows_of(cols)
            for i in range(3):
                weight = held[pl.ds(place * INNER, INNER), i * depth : (i + 1) * depth, :]
                proj[i] += jnp.dot(
                    part, weight.reshape(chunk, width), preferred_element_type=jnp.float32
                )
    else:
        for copy in copies:
            copy.wait()
        part = rows_of(slice(None))
        for i in range(3):
            weight = held[:, i * depth : (i + 1) * depth, :]
            proj[i] += jnp.dot(
                part, weight.reshape(n_pieces * depth, width), preferred_element_type=jnp.float32
            )
    q_proj, k_proj, v_proj = proj

    def norm(x, gain):
        power = jnp.mean(x * x, axis=-1, keepdims=True)
        return (x * lax.rsqrt(power + 1e-06) * gain).astype(jnp.bfloat16)

    v_new = v_proj.astype(jnp.bfloat16)
    put(kv_of, slice(width, 2 * width), v_new)
    k0, v0 = 3 * depth, 3 * depth + rows
    scale = math.log2(math.e) / math.sqrt(head_size)
    for h in range(width // head_size):
        cols = slice(h * head_size, (h + 1) * head_size)
        key = norm(k_proj[:, cols], kg_ref[...])
        put(kv_of, cols, key)
        query = norm(q_proj[:, cols], qg_ref[...])
        value = v_new[:, cols]
        keys = held[:, k0 : k0 + rows, cols].reshape(n_pieces * rows, head_size)
        values = held[:, v0 : v0 + rows, cols].reshape(n_pieces * rows, head_size)
        scores[...] = nt_dot(query, keys)
        own_cols = [pl.ds(pl.multiple_of(own * rows, 128), rows) for own in owns]
        for g, group in enumerate(groups):
            scores[group, own_cols[g]] = nt_dot(query[group], key[group])
        text_s = nt_dot(query, tk_ref[:, cols])
        image_s = scores[...]
        largest = jnp.maximum(
            jnp.max(text_s, axis=-1, keepdims=True), jnp.max(image_s, axis=-1, keepdims=True)
        )
        text_e = jnp.exp2((text_s - largest) * scale)
        image_e = jnp.exp2((image_s - largest) * scale)
        total = jnp.sum(text_e, axis=-1, keepdims=True) + jnp.sum(image_e, axis=-1, keepdims=True)
        expos[...] = image_e.astype(jnp.bfloat16)
        fresh_mix = []
        for g, group in enumerate(groups):
            fresh_mix.append(
                jnp.dot(expos[group, own_cols[g]], value[group], preferred_element_type=jnp.float32)
            )
            expos[group, own_cols[g]] = jnp.zeros((rows, rows), jnp.bfloat16)
        mixture = (
            jnp.dot(text_e.astype(jnp.bfloat16), tv_ref[:, cols], preferred_element_type=jnp.float32)
            + jnp.dot(expos[...], values, preferred_element_type=jnp.float32)
            + jnp.concatenate(fresh_mix, axis=0)
        )
        put(att_of, cols, (mixture / total).astype(jnp.bfloat16))


def attend_patches(where, patches, text_keys, text_values, query_gain, key_gain, pieces, depth, width):
    shares = [x for patch in patches for x in patch]
    model_width = shares[0].shape[1]
    rows = sum(x.shape[0] for x in patches[0])
    n = len(patches)
    head_size = query_gain.shape[0]
    texts = text_keys.shape[0]
    n_pieces = len(pieces)
    whole = lambda i, w: (0, 0)
    outs = [(2 * rows, width)] * (n // 2) + [(rows, 2 * width)] * n
    out = pl.pallas_call(
        functools.partial(patch_kernel, depth, head_size, n_pieces, [len(x) for x in patches]),
        grid_spec=pltpu.PrefetchScalarGridSpec(
            num_scalar_prefetch=1,
            grid=(1,),
            in_specs=[pl.BlockSpec(x.shape, whole) for x in shares]
            + [
                pl.BlockSpec((texts, width), lambda i, w: (0, w[0])),
                pl.BlockSpec((texts, width), lambda i, w: (0, w[0])),
                pl.BlockSpec((1, head_size), whole),
                pl.BlockSpec((1, head_size), whole),
            ]
            + [pl.BlockSpec(memory_space=pl.ANY)] * n_pieces,
            out_specs=[pl.BlockSpec(x, whole) for x in outs],
            scratch_shapes=[
                pltpu.VMEM((n_pieces,) + pieces[0].shape, jnp.bfloat16),
                pltpu.VMEM((n * rows, n_pieces * rows), jnp.float32),
                pltpu.VMEM((n * rows, n_pieces * rows), jnp.bfloat16),
                pltpu.SemaphoreType.DMA((n_pieces,)),
            ],
        ),
        out_shape=[jax.ShapeDtypeStruct(x, jnp.bfloat16) for x in outs],
        compiler_params=pltpu.CompilerParams(vmem_limit_bytes=VMEM_BYTES),
        cost_estimate=pl.CostEstimate(
            flops=2 * n * rows * (model_width * 3 * width + 2 * (texts + n_pieces * rows) * width),
            bytes_accessed=2 * n_pieces * pieces[0].size,
            transcendentals=n * rows * (texts + n_pieces * rows) * (width // head_size),
        ),
    )(
        where,
        *shares,
        text_keys,
        text_values,
        query_gain.reshape(1, -1),
        key_gain.reshape(1, -1),
        *pieces,
    )
    return out[: n // 2], out[n // 2 :]


def deal_kernel(n_arrays, team, member_ref, *refs):
    arrays, outs = refs[:n_arrays], refs[n_arrays:]
    width = outs[0].shape[1]
    for k in range(team):
        at = member_ref[0] ^ k
        cols = pl.ds(pl.multiple_of(at * width, 128), width)
        first = 0
        for x in arrays:
            rows = x.shape[0]
            outs[k][first : first + rows, :] = x[:, cols]
            first += rows


def deal(member, arrays, team):
    width = arrays[0].shape[1] // team
    shape = jax.ShapeDtypeStruct((sum(x.shape[0] for x in arrays), width), jnp.bfloat16)
    return pl.pallas_call(
        functools.partial(deal_kernel, len(arrays), team),
        in_specs=[pl.BlockSpec(memory_space=pltpu.SMEM)]
        + [pl.BlockSpec(memory_space=pltpu.VMEM)] * len(arrays),
        out_specs=[pl.BlockSpec(memory_space=pltpu.VMEM)] * team,
        out_shape=[shape] * team,
        compiler_params=pltpu.CompilerParams(vmem_limit_bytes=VMEM_BYTES),
    )(member.reshape(1), *arrays)


def collect_kernel(team, member_ref, *refs):
    packs, outs = refs[:team], refs[team:]
    width = outs[0].shape[1] // team
    for s in range(team):
        at = member_ref[0] ^ s
        cols = pl.ds(pl.multiple_of(at * width, 128), width)
        for i, out in enumerate(outs):
            out[:, cols] = packs[s][:, i * width : (i + 1) * width]


def collect(member, packs):
    team = len(packs)
    rows, double = packs[0].shape
    shape = jax.ShapeDtypeStruct((rows, double // 2 * team), jnp.bfloat16)
    return pl.pallas_call(
        functools.partial(collect_kernel, team),
        in_specs=[pl.BlockSpec(memory_space=pltpu.SMEM)]
        + [pl.BlockSpec(memory_space=pltpu.VMEM)] * team,
        out_specs=[pl.BlockSpec(memory_space=pltpu.VMEM)] * 2,
        out_shape=[shape, shape],
        compiler_params=pltpu.CompilerParams(vmem_limit_bytes=VMEM_BYTES),
    )(member.reshape(1), *packs)


def project_kernel(n_packs, n_pieces, n_shares, where_ref, *refs):
    packs, pieces = refs[:n_packs], refs[n_packs : n_packs + n_pieces]
    refs = refs[n_packs + n_pieces :]
    outs, held, sems = refs[:-2], refs[-2], refs[-1]
    rows, width = packs[0].shape[0] // 2, packs[0].shape[1]
    depth = held.shape[1]
    copies = [
        pltpu.make_async_copy(piece, held.at[where_ref[2 + n_shares + i]], sems.at[i])
        for i, piece in enumerate(pieces)
    ]
    for copy in copies:
        copy.start()
    own = pl.multiple_of(where_ref[1] * rows, 16)
    other = pl.multiple_of((1 - where_ref[1]) * rows, 16)
    attended = [
        jnp.concatenate([x[pl.ds(own, rows), :], x[pl.ds(other, rows), :]], axis=0) for x in packs
    ]
    for copy in copies:
        copy.wait()
    for i in reversed(range(n_shares)):
        block = pl.ds(where_ref[2 + i] * INNER, INNER)
        total = jnp.zeros((2 * rows, INNER * depth), jnp.float32)
        for s in range(n_packs):
            cols = pl.ds(pl.multiple_of((where_ref[0] ^ s) * width, 128), width)
            total += nt_dot(attended[s], held[block, :, cols].reshape(INNER * depth, width))
        outs[2 * i][...] = total[:rows].astype(outs[2 * i].dtype)
        outs[2 * i + 1][...] = total[rows:].astype(outs[2 * i + 1].dtype)


def project(where, packs, pieces, n_shares):
    rows, width = packs[0].shape[0] // 2, packs[0].shape[1]
    depth, local_width = pieces[0].shape
    block = INNER * depth
    whole = lambda i, w: (0, 0)
    types = [jnp.float32] + [jnp.bfloat16] * (2 * n_shares - 1)
    return pl.pallas_call(
        functools.partial(project_kernel, len(packs), len(pieces), n_shares),
        grid_spec=pltpu.PrefetchScalarGridSpec(
            num_scalar_prefetch=1,
            grid=(1,),
            in_specs=[pl.BlockSpec((2 * rows, width), whole)] * len(packs)
            + [pl.BlockSpec(memory_space=pl.ANY)] * len(pieces),
            out_specs=[pl.BlockSpec((rows, block), whole)] * len(types),
            scratch_shapes=[
                pltpu.VMEM((len(pieces), depth, local_width), jnp.bfloat16),
                pltpu.SemaphoreType.DMA((len(pieces),)),
            ],
        ),
        out_shape=[jax.ShapeDtypeStruct((rows, block), t) for t in types],
        compiler_params=pltpu.CompilerParams(vmem_limit_bytes=VMEM_BYTES),
        cost_estimate=pl.CostEstimate(
            flops=4 * rows * block * n_shares * local_width,
            bytes_accessed=2 * block * n_shares * local_width,
            transcendentals=0,
        ),
    )(where, *packs, *pieces)


def on_device(
    image,
    mod_shift,
    mod_scale,
    mod_gate,
    w_query,
    w_key,
    w_value,
    query_gain,
    key_gain,
    text_keys,
    text_values,
    stale_keys,
    stale_values,
    w_out,
):
    head_size = query_gain.shape[0]
    rows, model_width = image.shape
    depth, local_width = w_query.shape
    heads = local_width // head_size
    patches = lax.axis_size("patch")
    fsdp = lax.axis_size("fsdp")
    outer = patches // INNER
    team = math.gcd(outer, heads)
    width = local_width // team
    assert outer == 2 * fsdp and team > 1 and team & (team - 1) == 0 and outer & (outer - 1) == 0
    me = lax.axis_index("patch")
    mine = lax.axis_index("fsdp")
    place, seat = me // INNER, me % INNER
    member, parity = place % team, place % 2
    chain = []

    def over_outer(x, pairs):
        if len(chain) >= 3:
            x = after(x, chain[-3])
        seats = range(INNER)
        pairs = [(a * INNER + k, b * INNER + k) for a, b in pairs for k in seats]
        chain.append(lax.ppermute(x, "patch", pairs))
        return chain[-1]

    def to_partner(x, bits):
        return over_outer(x, [(z, z ^ bits) for z in range(outer)])

    def flip(x, bits):
        return lax.ppermute(x, "patch", [(p, p ^ bits) for p in range(patches)])

    def along_fsdp(x, step):
        return lax.ppermute(x, "fsdp", [(i, (i + step) % fsdp) for i in range(fsdp)])

    def along_both(x, bits, step):
        pairs = [
            (p * fsdp + f, (p ^ (bits * INNER)) * fsdp + (f + step) % fsdp)
            for p in range(patches)
            for f in range(fsdp)
        ]
        return lax.ppermute(x, ("patch", "fsdp"), pairs)

    def spread(piece):
        side = flip(piece, 2)
        return [piece, side, flip(piece, 1), flip(side, 1)]

    def seats_of(position):
        return [position * INNER + (seat ^ bits) for bits in (0, 2, 1, 3)]

    modded = modulate(image, mod_shift, mod_scale)
    share = rows // fsdp
    part = lax.dynamic_slice_in_dim(modded, mine * share, share, axis=0)
    dealt = deal(member, (w_query, w_key, w_value, stale_keys, stale_values), team)
    pieces = {0: dealt[0]}
    row_shares = {}
    if outer == 4 and team == 4:
        ends = [(1, 0), (2, 3)]
        middle = [(1, 2), (2, 1)]
        inside = jnp.logical_or(place == 1, place == 2)
        near = to_partner(part, 1)
        across = over_outer(part, middle)
        pieces[1] = to_partner(dealt[1], 1)
        far = over_outer(near, middle)
        pieces[2] = to_partner(dealt[2], 2)
        end_across = over_outer(across, ends)
        pieces[3] = to_partner(dealt[3], 3)
        end_far = over_outer(far, ends)
        row_shares[1] = near
        row_shares[2] = jnp.where(inside, far, end_across)
        row_shares[3] = jnp.where(inside, across, end_far)
    else:
        for k in range(1, team):
            row_shares[k] = to_partner(part, k)
        for k in range(1, outer):
            pieces[k] = to_partner(dealt[k % team], k)
    out_pieces = [w_out.T] + [to_partner(w_out.T, 2 * k) for k in range(1, fsdp)]

    pieces = [x for k in range(outer) for x in spread(pieces[k])]
    origins = [o for k in range(outer) for o in seats_of(place ^ k)]
    patch_rows = [[modded]]
    for k in range(1, team):
        got = row_shares[k]
        patch_rows.append([got] + [along_fsdp(got, i) for i in range(1, fsdp)])
    out_pieces = [x for piece in out_pieces for x in spread(piece)]
    out_places = [o for k in range(fsdp) for o in seats_of((place ^ (2 * k)) // 2)]

    where = [member] + origins
    for k in range(team):
        where.append((place ^ k) * INNER + seat)
        where += [((mine + (fsdp - i)) % fsdp) * share for i in range(fsdp)] if k else [0 * mine]
    att, kv = attend_patches(
        jnp.stack(where).astype(jnp.int32),
        patch_rows,
        text_keys,
        text_values,
        query_gain,
        key_gain,
        pieces,
        depth,
        width,
    )
    def give(x, bits):
        return lax.ppermute(x, "patch", [(p, p ^ (bits * INNER)) for p in range(patches)])

    packs = [att[0]] + [give(att[k // 2], k) for k in range(1, team)]
    where = [member, parity] + [(mine + i) % fsdp for i in range(fsdp)] + out_places
    partial = project(jnp.stack(where).astype(jnp.int32), packs, out_pieces, fsdp)
    own, partner = partial[0], [along_both(partial[1], 1, 0)]
    for i in range(1, fsdp):
        own = own + along_fsdp(partial[2 * i], i).astype(jnp.float32)
        partner.append(along_both(partial[2 * i + 1], 1, i))
    other = sum(x.astype(jnp.float32) for x in partner)
    summed = jnp.where(
        parity == 0,
        jnp.concatenate([own, other], axis=1),
        jnp.concatenate([other, own], axis=1),
    )
    fresh = [kv[0]] + [give(kv[k], k) for k in range(1, team)]
    key_out, value_out = collect(member, [after(fresh[0], partial[0])] + fresh[1:])

    out_share = model_width // fsdp
    col_start = mine * out_share
    image_part = lax.dynamic_slice_in_dim(image, col_start, out_share, 1).astype(jnp.float32)
    gate_part = lax.dynamic_slice_in_dim(mod_gate, col_start, out_share, 0)
    hidden = (image_part + gate_part * summed).astype(jnp.bfloat16)
    return (hidden, key_out, value_out)


def solution(mesh):
    return jax.shard_map(
        on_device,
        mesh=mesh,
        in_specs=(
            P("patch", None),
            P(),
            P(),
            P(),
            P("patch", "fsdp"),
            P("patch", "fsdp"),
            P("patch", "fsdp"),
            P(),
            P(),
            P(None, "fsdp"),
            P(None, "fsdp"),
            P("patch", "fsdp"),
            P("patch", "fsdp"),
            P("fsdp", "patch"),
        ),
        out_specs=(P("patch", "fsdp"), P("patch", "fsdp"), P("patch", "fsdp")),
        check_vma=False,
    )
```

```python
import functools
import math

import jax
import jax.numpy as jnp
from jax import lax
from jax.experimental import pallas as pl
from jax.experimental.pallas import tpu as pltpu
from jax.sharding import PartitionSpec as P

INNER = 4
VMEM_BYTES = 60 * 1024 * 1024


def modulate(image, mod_shift, mod_scale):
    values = image.astype(jnp.float32)
    center = jnp.mean(values, axis=-1, keepdims=True)
    spread = jnp.mean(jnp.square(values - center), axis=-1, keepdims=True)
    normed = (values - center) * lax.rsqrt(spread + 1e-06)
    return ((1.0 + mod_scale) * normed + mod_shift).astype(jnp.bfloat16)


def after(x, *deps):
    return lax.optimization_barrier((x,) + deps)[0]


def nt_dot(a, b):
    return lax.dot_general(a, b, (((1,), (1,)), ((), ())), preferred_element_type=jnp.float32)


def norm_heads(x, gain):
    power = jnp.mean(x * x, axis=-1, keepdims=True)
    return (x * lax.rsqrt(power + 1e-06) * gain).astype(jnp.bfloat16)


def rows_kernel(depth, head_size, n_pieces, counts, where_ref, *refs):
    n_shares, n_patches = sum(counts), len(counts)
    shares, refs = refs[:n_shares], refs[n_shares:]
    qg_ref, kg_ref = refs[:2]
    pieces, refs = refs[2 : 2 + n_pieces], refs[2 + n_pieces :]
    q_refs, kv_refs, (held, sems) = refs[: n_patches // 2], refs[n_patches // 2 : -2], refs[-2:]
    rows, width = kv_refs[0].shape[0], kv_refs[0].shape[1] // 2
    copies = [
        pltpu.make_async_copy(
            piece.at[pl.ds(0, 3 * depth)], held.at[where_ref[i]], sems.at[i]
        )
        for i, piece in enumerate(pieces)
    ]
    for copy in copies:
        copy.start()

    def put(ref_of, cols, value):
        at = 0
        for g, count in enumerate(counts):
            share = rows // count
            ref, base = ref_of(g)
            for i in range(count):
                first = pl.multiple_of(base + where_ref[n_pieces + at], 16)
                start = g * rows + i * share
                ref[pl.ds(first, share), cols] = value[start : start + share]
                at += 1

    def rows_of(cols):
        return jnp.concatenate([x[:, cols] for x in shares], axis=0)

    chunk = INNER * depth
    proj = [jnp.zeros((n_patches * rows, width), jnp.float32) for _ in range(3)]
    if chunk % 128 == 0:
        for first in range(0, n_pieces, INNER):
            for copy in copies[first : first + INNER]:
                copy.wait()
            place = where_ref[first] // INNER
            part = rows_of(pl.ds(pl.multiple_of(place * chunk, 128), chunk))
            for i in range(3):
                weight = held[pl.ds(place * INNER, INNER), i * depth : (i + 1) * depth, :]
                proj[i] += jnp.dot(
                    part, weight.reshape(chunk, width), preferred_element_type=jnp.float32
                )
    else:
        for copy in copies:
            copy.wait()
        part = rows_of(slice(None))
        for i in range(3):
            weight = held[:, i * depth : (i + 1) * depth, :]
            proj[i] += jnp.dot(
                part, weight.reshape(n_pieces * depth, width), preferred_element_type=jnp.float32
            )
    q_proj, k_proj, v_proj = proj
    put(lambda g: (kv_refs[g], 0), slice(width, 2 * width), v_proj.astype(jnp.bfloat16))
    for h in range(width // head_size):
        cols = slice(h * head_size, (h + 1) * head_size)
        put(lambda g: (kv_refs[g], 0), cols, norm_heads(k_proj[:, cols], kg_ref[...]))
        put(
            lambda g: (q_refs[g // 2], g % 2 * rows),
            cols,
            norm_heads(q_proj[:, cols], qg_ref[...]),
        )


def project_rows(where, patches, query_gain, key_gain, pieces, depth, width):
    shares = [x for patch in patches for x in patch]
    model_width = shares[0].shape[1]
    rows = sum(x.shape[0] for x in patches[0])
    n, n_pieces, head_size = len(patches), len(pieces), query_gain.shape[0]
    whole = lambda i, w: (0, 0)
    outs = [(2 * rows, width)] * (n // 2) + [(rows, 2 * width)] * n
    out = pl.pallas_call(
        functools.partial(rows_kernel, depth, head_size, n_pieces, [len(x) for x in patches]),
        grid_spec=pltpu.PrefetchScalarGridSpec(
            num_scalar_prefetch=1,
            grid=(1,),
            in_specs=[pl.BlockSpec(x.shape, whole) for x in shares]
            + [pl.BlockSpec((1, head_size), whole)] * 2
            + [pl.BlockSpec(memory_space=pl.ANY)] * n_pieces,
            out_specs=[pl.BlockSpec(x, whole) for x in outs],
            scratch_shapes=[
                pltpu.VMEM((n_pieces, 3 * depth, width), jnp.bfloat16),
                pltpu.SemaphoreType.DMA((n_pieces,)),
            ],
        ),
        out_shape=[jax.ShapeDtypeStruct(x, jnp.bfloat16) for x in outs],
        compiler_params=pltpu.CompilerParams(vmem_limit_bytes=VMEM_BYTES),
        cost_estimate=pl.CostEstimate(
            flops=2 * n * rows * model_width * 3 * width,
            bytes_accessed=6 * n_pieces * depth * width,
            transcendentals=0,
        ),
    )(where, *shares, query_gain.reshape(1, -1), key_gain.reshape(1, -1), *pieces)
    return out[: n // 2], out[n // 2 :]


def attend_kernel(depth, head_size, n_pieces, n_patches, where_ref, *refs):
    q_refs, refs = refs[: n_patches // 2], refs[n_patches // 2 :]
    kv_refs, refs = refs[:n_patches], refs[n_patches:]
    tk_ref, tv_ref, pieces, refs = refs[0], refs[1], refs[2 : 2 + n_pieces], refs[2 + n_pieces :]
    att_refs, (held, scores, expos, sems) = refs[:n_patches], refs[n_patches:]
    rows, width = kv_refs[0].shape[0], kv_refs[0].shape[1] // 2
    groups = [slice(g * rows, (g + 1) * rows) for g in range(n_patches)]
    owns = [where_ref[1 + n_pieces + g] for g in range(n_patches)]
    copies = [
        pltpu.make_async_copy(
            piece.at[pl.ds(3 * depth, 2 * rows)], held.at[where_ref[1 + i]], sems.at[i]
        )
        for i, piece in enumerate(pieces)
    ]
    for copy in copies:
        copy.start()
    scale = math.log2(math.e) / math.sqrt(head_size)
    own_cols = [pl.ds(pl.multiple_of(own * rows, 128), rows) for own in owns]
    for copy in copies:
        copy.wait()
    for h in range(width // head_size):
        cols = slice(h * head_size, (h + 1) * head_size)
        query = jnp.concatenate([x[:, cols] for x in q_refs], axis=0)
        keys = held[:, :rows, cols].reshape(n_pieces * rows, head_size)
        values = held[:, rows:, cols].reshape(n_pieces * rows, head_size)
        scores[...] = nt_dot(query, keys)
        for g, group in enumerate(groups):
            scores[group, own_cols[g]] = nt_dot(query[group], kv_refs[g][:, cols])
        text_s = nt_dot(query, tk_ref[:, cols])
        image_s = scores[...]
        largest = jnp.maximum(
            jnp.max(text_s, axis=-1, keepdims=True), jnp.max(image_s, axis=-1, keepdims=True)
        )
        text_e = jnp.exp2((text_s - largest) * scale)
        image_e = jnp.exp2((image_s - largest) * scale)
        total = jnp.sum(text_e, axis=-1, keepdims=True) + jnp.sum(image_e, axis=-1, keepdims=True)
        expos[...] = image_e.astype(jnp.bfloat16)
        fresh_mix = []
        for g, group in enumerate(groups):
            value = kv_refs[g][:, width + cols.start : width + cols.stop]
            fresh_mix.append(
                jnp.dot(expos[group, own_cols[g]], value, preferred_element_type=jnp.float32)
            )
            expos[group, own_cols[g]] = jnp.zeros((rows, rows), jnp.bfloat16)
        mixture = (
            jnp.dot(text_e.astype(jnp.bfloat16), tv_ref[:, cols], preferred_element_type=jnp.float32)
            + jnp.dot(expos[...], values, preferred_element_type=jnp.float32)
            + jnp.concatenate(fresh_mix, axis=0)
        )
        attended = (mixture / total).astype(jnp.bfloat16)
        for g, group in enumerate(groups):
            first = pl.multiple_of(lax.rem(owns[g] // INNER, 2) * rows, 16)
            for att_ref in att_refs[g // 2 * 2 : g // 2 * 2 + 2]:
                att_ref[pl.ds(first, rows), cols] = attended[group]


def attend_rows(where, queries, kv, text_keys, text_values, pieces, depth, head_size):
    pair_rows, width = queries[0].shape
    rows, texts, n_pieces, n = pair_rows // 2, text_keys.shape[0], len(pieces), len(kv)
    whole = lambda i, w: (0, 0)
    return pl.pallas_call(
        functools.partial(attend_kernel, depth, head_size, n_pieces, n),
        grid_spec=pltpu.PrefetchScalarGridSpec(
            num_scalar_prefetch=1,
            grid=(1,),
            in_specs=[pl.BlockSpec((pair_rows, width), whole)] * (n // 2)
            + [pl.BlockSpec((rows, 2 * width), whole)] * n
            + [pl.BlockSpec((texts, width), lambda i, w: (0, w[0]))] * 2
            + [pl.BlockSpec(memory_space=pl.ANY)] * n_pieces,
            out_specs=[pl.BlockSpec((pair_rows, width), whole)] * n,
            scratch_shapes=[
                pltpu.VMEM((n_pieces, 2 * rows, width), jnp.bfloat16),
                pltpu.VMEM((n * rows, n_pieces * rows), jnp.float32),
                pltpu.VMEM((n * rows, n_pieces * rows), jnp.bfloat16),
                pltpu.SemaphoreType.DMA((n_pieces,)),
            ],
        ),
        out_shape=[jax.ShapeDtypeStruct((pair_rows, width), jnp.bfloat16)] * n,
        compiler_params=pltpu.CompilerParams(vmem_limit_bytes=VMEM_BYTES),
        cost_estimate=pl.CostEstimate(
            flops=4 * n * rows * (texts + n_pieces * rows) * width,
            bytes_accessed=4 * n_pieces * rows * width,
            transcendentals=n * rows * (texts + n_pieces * rows) * (width // head_size),
        ),
    )(where, *queries, *kv, text_keys, text_values, *pieces)


def deal_kernel(n_arrays, team, member_ref, *refs):
    arrays, outs = refs[:n_arrays], refs[n_arrays:]
    width = outs[0].shape[1]
    for k in range(team):
        at = member_ref[0] ^ k
        cols = pl.ds(pl.multiple_of(at * width, 128), width)
        first = 0
        for x in arrays:
            rows = x.shape[0]
            outs[k][first : first + rows, :] = x[:, cols]
            first += rows


def deal(member, arrays, team):
    width = arrays[0].shape[1] // team
    shape = jax.ShapeDtypeStruct((sum(x.shape[0] for x in arrays), width), jnp.bfloat16)
    return pl.pallas_call(
        functools.partial(deal_kernel, len(arrays), team),
        in_specs=[pl.BlockSpec(memory_space=pltpu.SMEM)]
        + [pl.BlockSpec(memory_space=pltpu.VMEM)] * len(arrays),
        out_specs=[pl.BlockSpec(memory_space=pltpu.VMEM)] * team,
        out_shape=[shape] * team,
        compiler_params=pltpu.CompilerParams(vmem_limit_bytes=VMEM_BYTES),
    )(member.reshape(1), *arrays)


def collect_kernel(team, member_ref, *refs):
    packs, outs = refs[:team], refs[team:]
    width = outs[0].shape[1] // team
    for s in range(team):
        at = member_ref[0] ^ s
        cols = pl.ds(pl.multiple_of(at * width, 128), width)
        for i, out in enumerate(outs):
            out[:, cols] = packs[s][:, i * width : (i + 1) * width]


def collect(member, packs):
    team = len(packs)
    rows, double = packs[0].shape
    shape = jax.ShapeDtypeStruct((rows, double // 2 * team), jnp.bfloat16)
    return pl.pallas_call(
        functools.partial(collect_kernel, team),
        in_specs=[pl.BlockSpec(memory_space=pltpu.SMEM)]
        + [pl.BlockSpec(memory_space=pltpu.VMEM)] * team,
        out_specs=[pl.BlockSpec(memory_space=pltpu.VMEM)] * 2,
        out_shape=[shape, shape],
        compiler_params=pltpu.CompilerParams(vmem_limit_bytes=VMEM_BYTES),
    )(member.reshape(1), *packs)


def project_kernel(n_packs, n_pieces, n_shares, where_ref, *refs):
    packs, pieces = refs[:n_packs], refs[n_packs : n_packs + n_pieces]
    refs = refs[n_packs + n_pieces :]
    outs, held, sems = refs[:-2], refs[-2], refs[-1]
    rows, width = packs[0].shape[0] // 2, packs[0].shape[1]
    depth = held.shape[1]
    copies = [
        pltpu.make_async_copy(piece, held.at[where_ref[2 + n_shares + i]], sems.at[i])
        for i, piece in enumerate(pieces)
    ]
    for copy in copies:
        copy.start()
    own = pl.multiple_of(where_ref[1] * rows, 16)
    other = pl.multiple_of((1 - where_ref[1]) * rows, 16)
    attended = [
        jnp.concatenate([x[pl.ds(own, rows), :], x[pl.ds(other, rows), :]], axis=0) for x in packs
    ]
    for copy in copies:
        copy.wait()
    for i in reversed(range(n_shares)):
        block = pl.ds(where_ref[2 + i] * INNER, INNER)
        total = jnp.zeros((2 * rows, INNER * depth), jnp.float32)
        for s in range(n_packs):
            cols = pl.ds(pl.multiple_of((where_ref[0] ^ s) * width, 128), width)
            total += nt_dot(attended[s], held[block, :, cols].reshape(INNER * depth, width))
        outs[2 * i][...] = total[:rows].astype(outs[2 * i].dtype)
        outs[2 * i + 1][...] = total[rows:].astype(outs[2 * i + 1].dtype)


def project(where, packs, pieces, n_shares):
    rows, width = packs[0].shape[0] // 2, packs[0].shape[1]
    depth, local_width = pieces[0].shape
    block = INNER * depth
    whole = lambda i, w: (0, 0)
    types = [jnp.float32] + [jnp.bfloat16] * (2 * n_shares - 1)
    return pl.pallas_call(
        functools.partial(project_kernel, len(packs), len(pieces), n_shares),
        grid_spec=pltpu.PrefetchScalarGridSpec(
            num_scalar_prefetch=1,
            grid=(1,),
            in_specs=[pl.BlockSpec((2 * rows, width), whole)] * len(packs)
            + [pl.BlockSpec(memory_space=pl.ANY)] * len(pieces),
            out_specs=[pl.BlockSpec((rows, block), whole)] * len(types),
            scratch_shapes=[
                pltpu.VMEM((len(pieces), depth, local_width), jnp.bfloat16),
                pltpu.SemaphoreType.DMA((len(pieces),)),
            ],
        ),
        out_shape=[jax.ShapeDtypeStruct((rows, block), t) for t in types],
        compiler_params=pltpu.CompilerParams(vmem_limit_bytes=VMEM_BYTES),
        cost_estimate=pl.CostEstimate(
            flops=4 * rows * block * n_shares * local_width,
            bytes_accessed=2 * block * n_shares * local_width,
            transcendentals=0,
        ),
    )(where, *packs, *pieces)


def on_device(
    image,
    mod_shift,
    mod_scale,
    mod_gate,
    w_query,
    w_key,
    w_value,
    query_gain,
    key_gain,
    text_keys,
    text_values,
    stale_keys,
    stale_values,
    w_out,
):
    head_size = query_gain.shape[0]
    rows, model_width = image.shape
    depth, local_width = w_query.shape
    heads = local_width // head_size
    patches = lax.axis_size("patch")
    fsdp = lax.axis_size("fsdp")
    outer = patches // INNER
    team = math.gcd(outer, heads)
    width = local_width // team
    assert outer == 2 * fsdp and team > 1 and team & (team - 1) == 0 and outer & (outer - 1) == 0
    me = lax.axis_index("patch")
    mine = lax.axis_index("fsdp")
    place, seat = me // INNER, me % INNER
    member, parity = place % team, place % 2
    def over_outer(x, pairs):
        pairs = [(a * INNER + k, b * INNER + k) for a, b in pairs for k in range(INNER)]
        return lax.ppermute(x, "patch", pairs)

    def to_partner(x, bits):
        return over_outer(x, [(z, z ^ bits) for z in range(outer)])

    def flip(x, bits):
        return lax.ppermute(x, "patch", [(p, p ^ bits) for p in range(patches)])

    def along_fsdp(x, step):
        return lax.ppermute(x, "fsdp", [(i, (i + step) % fsdp) for i in range(fsdp)])

    def along_both(x, bits, step):
        pairs = [
            (p * fsdp + f, (p ^ (bits * INNER)) * fsdp + (f + step) % fsdp)
            for p in range(patches)
            for f in range(fsdp)
        ]
        return lax.ppermute(x, ("patch", "fsdp"), pairs)

    def spread(piece):
        side = flip(piece, 2)
        return [piece, side, flip(piece, 1), flip(side, 1)]

    def seats_of(position):
        return [position * INNER + (seat ^ bits) for bits in (0, 2, 1, 3)]

    modded = modulate(image, mod_shift, mod_scale)
    share = rows // fsdp
    part = lax.dynamic_slice_in_dim(modded, mine * share, share, axis=0)
    dealt = deal(member, (w_query, w_key, w_value, stale_keys, stale_values), team)
    pieces = {0: dealt[0]}
    row_shares = {}
    if outer == 4 and team == 4:
        ends = [(1, 0), (2, 3)]
        middle = [(1, 2), (2, 1)]
        inside = jnp.logical_or(place == 1, place == 2)
        near = to_partner(part, 1)
        across = over_outer(part, middle)
        far = over_outer(near, middle)
        pieces[2] = to_partner(after(dealt[2], near), 2)
        pieces[1] = to_partner(after(dealt[1], near), 1)
        end_across = over_outer(across, ends)
        end_far = over_outer(far, ends)
        pieces[3] = to_partner(after(dealt[3], far), 3)
        row_shares[1] = near
        row_shares[2] = jnp.where(inside, far, end_across)
        row_shares[3] = jnp.where(inside, across, end_far)
    else:
        for k in range(1, team):
            row_shares[k] = to_partner(part, k)
        for k in range(1, outer):
            pieces[k] = to_partner(dealt[k % team], k)
    out_piece = after(w_out.T, pieces[outer - 1])
    out_pieces = [out_piece] + [to_partner(out_piece, 2 * k) for k in range(1, fsdp)]

    pieces = [x for k in range(outer) for x in spread(pieces[k])]
    origins = [o for k in range(outer) for o in seats_of(place ^ k)]
    patch_rows = [[modded]]
    firsts = [0 * mine]
    for k in range(1, team):
        got = row_shares[k]
        patch_rows.append([got] + [along_fsdp(got, i) for i in range(1, fsdp)])
        firsts += [((mine + (fsdp - i)) % fsdp) * share for i in range(fsdp)]
    queries, kv = project_rows(
        jnp.stack(origins + firsts).astype(jnp.int32),
        patch_rows,
        query_gain,
        key_gain,
        pieces,
        depth,
        width,
    )
    out_pieces = [x for piece in out_pieces for x in spread(after(piece, queries[0]))]
    out_places = [o for k in range(fsdp) for o in seats_of((place ^ (2 * k)) // 2)]

    def give(x, bits):
        return lax.ppermute(x, "patch", [(p, p ^ (bits * INNER)) for p in range(patches)])

    fresh = [kv[0]] + [give(kv[k], k) for k in range(1, team)]
    where = [member] + origins + [(place ^ k) * INNER + seat for k in range(team)]
    att = attend_rows(
        jnp.stack(where).astype(jnp.int32),
        queries,
        kv,
        text_keys,
        text_values,
        pieces,
        depth,
        head_size,
    )
    packs = [att[0]] + [give(att[k], k) for k in range(1, team)]
    where = [member, parity] + [(mine + i) % fsdp for i in range(fsdp)] + out_places
    where = after(jnp.stack(where).astype(jnp.int32), *fresh)
    partial = project(where, packs, out_pieces, fsdp)
    own, partner = partial[0], [along_both(partial[1], 1, 0)]
    for i in range(1, fsdp):
        own = own + along_fsdp(partial[2 * i], i).astype(jnp.float32)
        partner.append(along_both(partial[2 * i + 1], 1, i))
    other = sum(x.astype(jnp.float32) for x in partner)
    summed = jnp.where(
        parity == 0,
        jnp.concatenate([own, other], axis=1),
        jnp.concatenate([other, own], axis=1),
    )
    key_out, value_out = collect(member, [after(fresh[0], partial[0])] + fresh[1:])

    out_share = model_width // fsdp
    col_start = mine * out_share
    image_part = lax.dynamic_slice_in_dim(image, col_start, out_share, 1).astype(jnp.float32)
    gate_part = lax.dynamic_slice_in_dim(mod_gate, col_start, out_share, 0)
    hidden = (image_part + gate_part * summed).astype(jnp.bfloat16)
    return (hidden, key_out, value_out)


def solution(mesh):
    return jax.shard_map(
        on_device,
        mesh=mesh,
        in_specs=(
            P("patch", None),
            P(),
            P(),
            P(),
            P("patch", "fsdp"),
            P("patch", "fsdp"),
            P("patch", "fsdp"),
            P(),
            P(),
            P(None, "fsdp"),
            P(None, "fsdp"),
            P("patch", "fsdp"),
            P("patch", "fsdp"),
            P("fsdp", "patch"),
        ),
        out_specs=(P("patch", "fsdp"), P("patch", "fsdp"), P("patch", "fsdp")),
        check_vma=False,
    )
```

```python
import functools
import math

import jax
import jax.numpy as jnp
from jax import lax
from jax.experimental import pallas as pl
from jax.experimental.pallas import tpu as pltpu
from jax.sharding import PartitionSpec as P

INNER = 4
VMEM_BYTES = 60 * 1024 * 1024


def modulate(image, mod_shift, mod_scale):
    values = image.astype(jnp.float32)
    center = jnp.mean(values, axis=-1, keepdims=True)
    spread = jnp.mean(jnp.square(values - center), axis=-1, keepdims=True)
    normed = (values - center) * lax.rsqrt(spread + 1e-06)
    return ((1.0 + mod_scale) * normed + mod_shift).astype(jnp.bfloat16)


def after(x, *deps):
    return lax.optimization_barrier((x,) + deps)[0]


def nt_dot(a, b):
    return lax.dot_general(a, b, (((1,), (1,)), ((), ())), preferred_element_type=jnp.float32)


def norm_heads(x, gain):
    power = jnp.mean(x * x, axis=-1, keepdims=True)
    return (x * lax.rsqrt(power + 1e-06) * gain).astype(jnp.bfloat16)


def rows_kernel(depth, head_size, n_pieces, counts, where_ref, *refs):
    n_shares, n_patches = sum(counts), len(counts)
    shares, refs = refs[:n_shares], refs[n_shares:]
    qg_ref, kg_ref = refs[:2]
    pieces, refs = refs[2 : 2 + n_pieces], refs[2 + n_pieces :]
    q_refs, kv_refs, (held, sems) = refs[: n_patches // 2], refs[n_patches // 2 : -2], refs[-2:]
    rows, width = kv_refs[0].shape[0], kv_refs[0].shape[1] // 2
    copies = [
        pltpu.make_async_copy(
            piece.at[pl.ds(0, 3 * depth)], held.at[where_ref[i]], sems.at[i]
        )
        for i, piece in enumerate(pieces)
    ]
    for copy in copies:
        copy.start()

    def put(ref_of, cols, value):
        at = 0
        for g, count in enumerate(counts):
            share = rows // count
            ref, base = ref_of(g)
            for i in range(count):
                first = pl.multiple_of(base + where_ref[n_pieces + at], 16)
                start = g * rows + i * share
                ref[pl.ds(first, share), cols] = value[start : start + share]
                at += 1

    def rows_of(cols):
        return jnp.concatenate([x[:, cols] for x in shares], axis=0)

    chunk = INNER * depth
    proj = [jnp.zeros((n_patches * rows, width), jnp.float32) for _ in range(3)]
    if chunk % 128 == 0:
        for first in range(0, n_pieces, INNER):
            for copy in copies[first : first + INNER]:
                copy.wait()
            place = where_ref[first] // INNER
            part = rows_of(pl.ds(pl.multiple_of(place * chunk, 128), chunk))
            for i in range(3):
                weight = held[pl.ds(place * INNER, INNER), i * depth : (i + 1) * depth, :]
                proj[i] += jnp.dot(
                    part, weight.reshape(chunk, width), preferred_element_type=jnp.float32
                )
    else:
        for copy in copies:
            copy.wait()
        part = rows_of(slice(None))
        for i in range(3):
            weight = held[:, i * depth : (i + 1) * depth, :]
            proj[i] += jnp.dot(
                part, weight.reshape(n_pieces * depth, width), preferred_element_type=jnp.float32
            )
    q_proj, k_proj, v_proj = proj
    put(lambda g: (kv_refs[g], 0), slice(width, 2 * width), v_proj.astype(jnp.bfloat16))
    for h in range(width // head_size):
        cols = slice(h * head_size, (h + 1) * head_size)
        put(lambda g: (kv_refs[g], 0), cols, norm_heads(k_proj[:, cols], kg_ref[...]))
        put(
            lambda g: (q_refs[g // 2], g % 2 * rows),
            cols,
            norm_heads(q_proj[:, cols], qg_ref[...]),
        )


def project_rows(where, patches, query_gain, key_gain, pieces, depth, width):
    shares = [x for patch in patches for x in patch]
    model_width = shares[0].shape[1]
    rows = sum(x.shape[0] for x in patches[0])
    n, n_pieces, head_size = len(patches), len(pieces), query_gain.shape[0]
    whole = lambda i, w: (0, 0)
    outs = [(2 * rows, width)] * (n // 2) + [(rows, 2 * width)] * n
    out = pl.pallas_call(
        functools.partial(rows_kernel, depth, head_size, n_pieces, [len(x) for x in patches]),
        grid_spec=pltpu.PrefetchScalarGridSpec(
            num_scalar_prefetch=1,
            grid=(1,),
            in_specs=[pl.BlockSpec(x.shape, whole) for x in shares]
            + [pl.BlockSpec((1, head_size), whole)] * 2
            + [pl.BlockSpec(memory_space=pl.ANY)] * n_pieces,
            out_specs=[pl.BlockSpec(x, whole) for x in outs],
            scratch_shapes=[
                pltpu.VMEM((n_pieces, 3 * depth, width), jnp.bfloat16),
                pltpu.SemaphoreType.DMA((n_pieces,)),
            ],
        ),
        out_shape=[jax.ShapeDtypeStruct(x, jnp.bfloat16) for x in outs],
        compiler_params=pltpu.CompilerParams(vmem_limit_bytes=VMEM_BYTES),
        cost_estimate=pl.CostEstimate(
            flops=2 * n * rows * model_width * 3 * width,
            bytes_accessed=6 * n_pieces * depth * width,
            transcendentals=0,
        ),
    )(where, *shares, query_gain.reshape(1, -1), key_gain.reshape(1, -1), *pieces)
    return out[: n // 2], out[n // 2 :]


def attend_kernel(depth, head_size, n_pieces, n_patches, where_ref, *refs):
    q_refs, refs = refs[: n_patches // 2], refs[n_patches // 2 :]
    kv_refs, refs = refs[:n_patches], refs[n_patches:]
    tk_ref, tv_ref, pieces, refs = refs[0], refs[1], refs[2 : 2 + n_pieces], refs[2 + n_pieces :]
    att_refs, (held, scores, expos, sems) = refs[:n_patches], refs[n_patches:]
    rows, width = kv_refs[0].shape[0], kv_refs[0].shape[1] // 2
    groups = [slice(g * rows, (g + 1) * rows) for g in range(n_patches)]
    owns = [where_ref[1 + n_pieces + g] for g in range(n_patches)]
    copies = [
        pltpu.make_async_copy(
            piece.at[pl.ds(3 * depth, 2 * rows)], held.at[where_ref[1 + i]], sems.at[i]
        )
        for i, piece in enumerate(pieces)
    ]
    for copy in copies:
        copy.start()
    scale = math.log2(math.e) / math.sqrt(head_size)
    own_cols = [pl.ds(pl.multiple_of(own * rows, 128), rows) for own in owns]
    for copy in copies:
        copy.wait()
    for h in range(width // head_size):
        cols = slice(h * head_size, (h + 1) * head_size)
        query = jnp.concatenate([x[:, cols] for x in q_refs], axis=0)
        keys = held[:, :rows, cols].reshape(n_pieces * rows, head_size)
        values = held[:, rows:, cols].reshape(n_pieces * rows, head_size)
        scores[h] = nt_dot(query, keys)
        for g, group in enumerate(groups):
            scores[h, group, own_cols[g]] = nt_dot(query[group], kv_refs[g][:, cols])
        text_s = nt_dot(query, tk_ref[:, cols])
        image_s = scores[h]
        largest = jnp.maximum(
            jnp.max(text_s, axis=-1, keepdims=True), jnp.max(image_s, axis=-1, keepdims=True)
        )
        text_e = jnp.exp2((text_s - largest) * scale)
        image_e = jnp.exp2((image_s - largest) * scale)
        total = jnp.sum(text_e, axis=-1, keepdims=True) + jnp.sum(image_e, axis=-1, keepdims=True)
        expos[h] = image_e.astype(jnp.bfloat16)
        fresh_mix = []
        for g, group in enumerate(groups):
            value = kv_refs[g][:, width + cols.start : width + cols.stop]
            fresh_mix.append(
                jnp.dot(expos[h, group, own_cols[g]], value, preferred_element_type=jnp.float32)
            )
            expos[h, group, own_cols[g]] = jnp.zeros((rows, rows), jnp.bfloat16)
        mixture = (
            jnp.dot(text_e.astype(jnp.bfloat16), tv_ref[:, cols], preferred_element_type=jnp.float32)
            + jnp.dot(expos[h], values, preferred_element_type=jnp.float32)
            + jnp.concatenate(fresh_mix, axis=0)
        )
        attended = (mixture / total).astype(jnp.bfloat16)
        for g, group in enumerate(groups):
            first = pl.multiple_of(lax.rem(owns[g] // INNER, 2) * rows, 16)
            for att_ref in att_refs[g // 2 * 2 : g // 2 * 2 + 2]:
                att_ref[pl.ds(first, rows), cols] = attended[group]


def attend_rows(where, queries, kv, text_keys, text_values, pieces, depth, head_size):
    pair_rows, width = queries[0].shape
    rows, texts, n_pieces, n = pair_rows // 2, text_keys.shape[0], len(pieces), len(kv)
    whole = lambda i, w: (0, 0)
    return pl.pallas_call(
        functools.partial(attend_kernel, depth, head_size, n_pieces, n),
        grid_spec=pltpu.PrefetchScalarGridSpec(
            num_scalar_prefetch=1,
            grid=(1,),
            in_specs=[pl.BlockSpec((pair_rows, width), whole)] * (n // 2)
            + [pl.BlockSpec((rows, 2 * width), whole)] * n
            + [pl.BlockSpec((texts, width), lambda i, w: (0, w[0]))] * 2
            + [pl.BlockSpec(memory_space=pl.ANY)] * n_pieces,
            out_specs=[pl.BlockSpec((pair_rows, width), whole)] * n,
            scratch_shapes=[
                pltpu.VMEM((n_pieces, 2 * rows, width), jnp.bfloat16),
                pltpu.VMEM((width // head_size, n * rows, n_pieces * rows), jnp.float32),
                pltpu.VMEM((width // head_size, n * rows, n_pieces * rows), jnp.bfloat16),
                pltpu.SemaphoreType.DMA((n_pieces,)),
            ],
        ),
        out_shape=[jax.ShapeDtypeStruct((pair_rows, width), jnp.bfloat16)] * n,
        compiler_params=pltpu.CompilerParams(vmem_limit_bytes=VMEM_BYTES),
        cost_estimate=pl.CostEstimate(
            flops=4 * n * rows * (texts + n_pieces * rows) * width,
            bytes_accessed=4 * n_pieces * rows * width,
            transcendentals=n * rows * (texts + n_pieces * rows) * (width // head_size),
        ),
    )(where, *queries, *kv, text_keys, text_values, *pieces)


def deal_kernel(n_arrays, team, member_ref, *refs):
    arrays, outs = refs[:n_arrays], refs[n_arrays:]
    width = outs[0].shape[1]
    for k in range(team):
        at = member_ref[0] ^ k
        cols = pl.ds(pl.multiple_of(at * width, 128), width)
        first = 0
        for x in arrays:
            rows = x.shape[0]
            outs[k][first : first + rows, :] = x[:, cols]
            first += rows


def deal(member, arrays, team):
    width = arrays[0].shape[1] // team
    shape = jax.ShapeDtypeStruct((sum(x.shape[0] for x in arrays), width), jnp.bfloat16)
    return pl.pallas_call(
        functools.partial(deal_kernel, len(arrays), team),
        in_specs=[pl.BlockSpec(memory_space=pltpu.SMEM)]
        + [pl.BlockSpec(memory_space=pltpu.VMEM)] * len(arrays),
        out_specs=[pl.BlockSpec(memory_space=pltpu.VMEM)] * team,
        out_shape=[shape] * team,
        compiler_params=pltpu.CompilerParams(vmem_limit_bytes=VMEM_BYTES),
    )(member.reshape(1), *arrays)


def collect_kernel(team, member_ref, *refs):
    packs, outs = refs[:team], refs[team:]
    width = outs[0].shape[1] // team
    for s in range(team):
        at = member_ref[0] ^ s
        cols = pl.ds(pl.multiple_of(at * width, 128), width)
        for i, out in enumerate(outs):
            out[:, cols] = packs[s][:, i * width : (i + 1) * width]


def collect(member, packs):
    team = len(packs)
    rows, double = packs[0].shape
    shape = jax.ShapeDtypeStruct((rows, double // 2 * team), jnp.bfloat16)
    return pl.pallas_call(
        functools.partial(collect_kernel, team),
        in_specs=[pl.BlockSpec(memory_space=pltpu.SMEM)]
        + [pl.BlockSpec(memory_space=pltpu.VMEM)] * team,
        out_specs=[pl.BlockSpec(memory_space=pltpu.VMEM)] * 2,
        out_shape=[shape, shape],
        compiler_params=pltpu.CompilerParams(vmem_limit_bytes=VMEM_BYTES),
    )(member.reshape(1), *packs)


def project_kernel(n_packs, n_pieces, n_shares, where_ref, *refs):
    packs, pieces = refs[:n_packs], refs[n_packs : n_packs + n_pieces]
    refs = refs[n_packs + n_pieces :]
    outs, held, sems = refs[:-2], refs[-2], refs[-1]
    rows, width = packs[0].shape[0] // 2, packs[0].shape[1]
    depth = held.shape[1]
    copies = [
        pltpu.make_async_copy(piece, held.at[where_ref[2 + n_shares + i]], sems.at[i])
        for i, piece in enumerate(pieces)
    ]
    for copy in copies:
        copy.start()
    own = pl.multiple_of(where_ref[1] * rows, 16)
    other = pl.multiple_of((1 - where_ref[1]) * rows, 16)
    attended = [
        jnp.concatenate([x[pl.ds(own, rows), :], x[pl.ds(other, rows), :]], axis=0) for x in packs
    ]
    for copy in copies:
        copy.wait()
    for i in reversed(range(n_shares)):
        block = pl.ds(where_ref[2 + i] * INNER, INNER)
        total = jnp.zeros((2 * rows, INNER * depth), jnp.float32)
        for s in range(n_packs):
            cols = pl.ds(pl.multiple_of((where_ref[0] ^ s) * width, 128), width)
            total += nt_dot(attended[s], held[block, :, cols].reshape(INNER * depth, width))
        outs[2 * i][...] = total[:rows].astype(outs[2 * i].dtype)
        outs[2 * i + 1][...] = total[rows:].astype(outs[2 * i + 1].dtype)


def project(where, packs, pieces, n_shares):
    rows, width = packs[0].shape[0] // 2, packs[0].shape[1]
    depth, local_width = pieces[0].shape
    block = INNER * depth
    whole = lambda i, w: (0, 0)
    types = [jnp.float32] + [jnp.bfloat16] * (2 * n_shares - 1)
    return pl.pallas_call(
        functools.partial(project_kernel, len(packs), len(pieces), n_shares),
        grid_spec=pltpu.PrefetchScalarGridSpec(
            num_scalar_prefetch=1,
            grid=(1,),
            in_specs=[pl.BlockSpec((2 * rows, width), whole)] * len(packs)
            + [pl.BlockSpec(memory_space=pl.ANY)] * len(pieces),
            out_specs=[pl.BlockSpec((rows, block), whole)] * len(types),
            scratch_shapes=[
                pltpu.VMEM((len(pieces), depth, local_width), jnp.bfloat16),
                pltpu.SemaphoreType.DMA((len(pieces),)),
            ],
        ),
        out_shape=[jax.ShapeDtypeStruct((rows, block), t) for t in types],
        compiler_params=pltpu.CompilerParams(vmem_limit_bytes=VMEM_BYTES),
        cost_estimate=pl.CostEstimate(
            flops=4 * rows * block * n_shares * local_width,
            bytes_accessed=2 * block * n_shares * local_width,
            transcendentals=0,
        ),
    )(where, *packs, *pieces)


def on_device(
    image,
    mod_shift,
    mod_scale,
    mod_gate,
    w_query,
    w_key,
    w_value,
    query_gain,
    key_gain,
    text_keys,
    text_values,
    stale_keys,
    stale_values,
    w_out,
):
    head_size = query_gain.shape[0]
    rows, model_width = image.shape
    depth, local_width = w_query.shape
    heads = local_width // head_size
    patches = lax.axis_size("patch")
    fsdp = lax.axis_size("fsdp")
    outer = patches // INNER
    team = math.gcd(outer, heads)
    width = local_width // team
    assert outer == 2 * fsdp and team > 1 and team & (team - 1) == 0 and outer & (outer - 1) == 0
    me = lax.axis_index("patch")
    mine = lax.axis_index("fsdp")
    place, seat = me // INNER, me % INNER
    member, parity = place % team, place % 2
    def over_outer(x, pairs):
        pairs = [(a * INNER + k, b * INNER + k) for a, b in pairs for k in range(INNER)]
        return lax.ppermute(x, "patch", pairs)

    def to_partner(x, bits):
        return over_outer(x, [(z, z ^ bits) for z in range(outer)])

    def flip(x, bits):
        return lax.ppermute(x, "patch", [(p, p ^ bits) for p in range(patches)])

    def along_fsdp(x, step):
        return lax.ppermute(x, "fsdp", [(i, (i + step) % fsdp) for i in range(fsdp)])

    def along_both(x, bits, step):
        pairs = [
            (p * fsdp + f, (p ^ (bits * INNER)) * fsdp + (f + step) % fsdp)
            for p in range(patches)
            for f in range(fsdp)
        ]
        return lax.ppermute(x, ("patch", "fsdp"), pairs)

    def spread(piece, side=None, *deps):
        side = flip(piece, 2) if side is None else side
        return [piece, side, flip(after(piece, *deps), 1), flip(after(side, *deps), 1)]

    def seats_of(position):
        return [position * INNER + (seat ^ bits) for bits in (0, 2, 1, 3)]

    modded = modulate(image, mod_shift, mod_scale)
    share = rows // fsdp
    part = lax.dynamic_slice_in_dim(modded, mine * share, share, axis=0)
    dealt = deal(member, (w_query, w_key, w_value, stale_keys, stale_values), team)
    pieces, sides = {0: dealt[0]}, {}
    row_shares = {}
    if outer == 4 and team == 4:
        ends = [(1, 0), (2, 3)]
        middle = [(1, 2), (2, 1)]
        inside = jnp.logical_or(place == 1, place == 2)
        near = to_partner(part, 1)
        across = over_outer(part, middle)
        sides[0] = flip(pieces[0], 2)
        far = over_outer(near, middle)
        pieces[2] = to_partner(after(dealt[2], near, across), 2)
        pieces[1] = to_partner(after(dealt[1], near, across), 1)
        end_across = over_outer(across, ends)
        end_far = over_outer(after(far, sides[0]), ends)
        sides[1] = flip(after(pieces[1], far), 2)
        pieces[3] = to_partner(after(dealt[3], far), 3)
        sides[2] = flip(after(pieces[2], end_far, sides[1]), 2)
        row_shares[1] = after(near, sides[1])
        row_shares[2] = jnp.where(inside, far, end_across)
        row_shares[3] = jnp.where(inside, across, end_far)
    else:
        for k in range(1, team):
            row_shares[k] = to_partner(part, k)
        for k in range(1, outer):
            pieces[k] = to_partner(dealt[k % team], k)
    out_piece = after(w_out.T, pieces[outer - 1])
    out_pieces = [out_piece] + [to_partner(out_piece, 2 * k) for k in range(1, fsdp)]

    late = list(sides.values())[-1:]
    pieces = [x for k in range(outer) for x in spread(pieces[k], sides.get(k), *late)]
    origins = [o for k in range(outer) for o in seats_of(place ^ k)]
    patch_rows = [[modded]]
    firsts = [0 * mine]
    for k in range(1, team):
        got = row_shares[k]
        patch_rows.append([got] + [along_fsdp(got, i) for i in range(1, fsdp)])
        firsts += [((mine + (fsdp - i)) % fsdp) * share for i in range(fsdp)]
    queries, kv = project_rows(
        jnp.stack(origins + firsts).astype(jnp.int32),
        patch_rows,
        query_gain,
        key_gain,
        pieces,
        depth,
        width,
    )
    out_places = [o for k in range(fsdp) for o in seats_of((place ^ (2 * k)) // 2)]

    def give(x, bits):
        return lax.ppermute(x, "patch", [(p, p ^ (bits * INNER)) for p in range(patches)])

    fresh = [kv[0]] + [give(kv[k], k) for k in range(1, team)]
    where = [member] + origins + [(place ^ k) * INNER + seat for k in range(team)]
    att = attend_rows(
        jnp.stack(where).astype(jnp.int32),
        queries,
        kv,
        text_keys,
        text_values,
        pieces,
        depth,
        head_size,
    )
    packs = [att[0]] + [give(att[k], k) for k in range(1, team)]
    out_sides = [flip(after(out_pieces[0], queries[0]), 2)]
    out_sides += [flip(after(piece, att[0], *fresh[1:]), 2) for piece in out_pieces[1:]]
    out_pieces = [x for p, q in zip(out_pieces, out_sides) for x in spread(p, q, *packs[1:])]
    where = [member, parity] + [(mine + i) % fsdp for i in range(fsdp)] + out_places
    where = jnp.stack(where).astype(jnp.int32)
    partial = project(where, packs, out_pieces, fsdp)
    own, partner = partial[0], [along_both(partial[1], 1, 0)]
    for i in range(1, fsdp):
        own = own + along_fsdp(partial[2 * i], i).astype(jnp.float32)
        partner.append(along_both(partial[2 * i + 1], 1, i))
    other = sum(x.astype(jnp.float32) for x in partner)
    summed = jnp.where(
        parity == 0,
        jnp.concatenate([own, other], axis=1),
        jnp.concatenate([other, own], axis=1),
    )
    key_out, value_out = collect(member, [after(fresh[0], partial[0])] + fresh[1:])

    out_share = model_width // fsdp
    col_start = mine * out_share
    image_part = lax.dynamic_slice_in_dim(image, col_start, out_share, 1).astype(jnp.float32)
    gate_part = lax.dynamic_slice_in_dim(mod_gate, col_start, out_share, 0)
    hidden = (image_part + gate_part * summed).astype(jnp.bfloat16)
    return (hidden, key_out, value_out)


def solution(mesh):
    return jax.shard_map(
        on_device,
        mesh=mesh,
        in_specs=(
            P("patch", None),
            P(),
            P(),
            P(),
            P("patch", "fsdp"),
            P("patch", "fsdp"),
            P("patch", "fsdp"),
            P(),
            P(),
            P(None, "fsdp"),
            P(None, "fsdp"),
            P("patch", "fsdp"),
            P("patch", "fsdp"),
            P("fsdp", "patch"),
        ),
        out_specs=(P("patch", "fsdp"), P("patch", "fsdp"), P("patch", "fsdp")),
        check_vma=False,
    )
```

```python
import functools
import math

import jax
import jax.numpy as jnp
from jax import lax
from jax.experimental import pallas as pl
from jax.experimental.pallas import tpu as pltpu
from jax.sharding import PartitionSpec as P

INNER = 4
VMEM_BYTES = 60 * 1024 * 1024


def modulate(image, mod_shift, mod_scale):
    values = image.astype(jnp.float32)
    center = jnp.mean(values, axis=-1, keepdims=True)
    spread = jnp.mean(jnp.square(values - center), axis=-1, keepdims=True)
    normed = (values - center) * lax.rsqrt(spread + 1e-06)
    return ((1.0 + mod_scale) * normed + mod_shift).astype(jnp.bfloat16)


def after(x, *deps):
    return lax.optimization_barrier((x,) + deps)[0]


def nt_dot(a, b):
    return lax.dot_general(a, b, (((1,), (1,)), ((), ())), preferred_element_type=jnp.float32)


def norm_heads(x, gain):
    power = jnp.mean(x * x, axis=-1, keepdims=True)
    return (x * lax.rsqrt(power + 1e-06) * gain).astype(jnp.bfloat16)


def patch_kernel(depth, n_pieces, counts, where_ref, *refs):
    n_patches = len(counts)
    tk_ref, tv_ref, qg_ref, kg_ref = refs[:4]
    shares, refs = refs[4 : 4 + sum(counts)], refs[4 + sum(counts) :]
    pieces, refs = refs[:n_pieces], refs[n_pieces:]
    outs, (x_ref, held, scores, expos, x_sem, w_sem, k_sem) = refs[:n_patches], refs[n_patches:]
    rows, width = outs[0].shape[0] // 2, outs[0].shape[1] // 2
    head_size = qg_ref.shape[1]
    groups = [slice(g * rows, (g + 1) * rows) for g in range(n_patches)]
    owns, x_copies, at = [], [], 1 + n_pieces
    for g, count in enumerate(counts):
        owns.append(where_ref[at])
        for i in range(count):
            share = shares[len(x_copies)]
            first = pl.multiple_of(g * rows + where_ref[at + 1 + i], 16)
            x_copies.append(
                pltpu.make_async_copy(
                    share, x_ref.at[pl.ds(first, share.shape[0])], x_sem.at[len(x_copies)]
                )
            )
        at += 1 + count
    parts = ((pl.ds(0, 3 * depth), w_sem), (pl.ds(3 * depth, 2 * rows), k_sem))
    w_copies, k_copies = [
        [
            pltpu.make_async_copy(piece.at[part], held.at[where_ref[1 + i], part], sem.at[i])
            for i, piece in enumerate(pieces)
        ]
        for part, sem in parts
    ]
    for copy in x_copies + w_copies + k_copies:
        copy.start()
    for copy in x_copies:
        copy.wait()

    chunk = INNER * depth
    proj = [jnp.zeros((n_patches * rows, width), jnp.float32) for _ in range(3)]
    if chunk % 128 == 0:
        for first in range(0, n_pieces, INNER):
            for copy in w_copies[first : first + INNER]:
                copy.wait()
            place = where_ref[1 + first] // INNER
            part = x_ref[:, pl.ds(pl.multiple_of(place * chunk, 128), chunk)]
            for i in range(3):
                weight = held[pl.ds(place * INNER, INNER), i * depth : (i + 1) * depth, :]
                proj[i] += jnp.dot(
                    part, weight.reshape(chunk, width), preferred_element_type=jnp.float32
                )
    else:
        for copy in w_copies:
            copy.wait()
        for i in range(3):
            weight = held[:, i * depth : (i + 1) * depth, :]
            proj[i] += jnp.dot(
                x_ref[...],
                weight.reshape(n_pieces * depth, width),
                preferred_element_type=jnp.float32,
            )
    q_proj, k_proj, v_proj = proj
    for copy in k_copies:
        copy.wait()

    v_new = v_proj.astype(jnp.bfloat16)
    k0, v0 = 3 * depth, 3 * depth + rows
    scale = math.log2(math.e) / math.sqrt(head_size)
    own_cols = [pl.ds(pl.multiple_of(own * rows, 128), rows) for own in owns]
    for h in range(width // head_size):
        cols = slice(h * head_size, (h + 1) * head_size)
        beside = slice(width + cols.start, width + cols.stop)
        query = norm_heads(q_proj[:, cols], qg_ref[...])
        key = norm_heads(k_proj[:, cols], kg_ref[...])
        value = v_new[:, cols]
        keys = held[:, k0 : k0 + rows, cols].reshape(n_pieces * rows, head_size)
        values = held[:, v0 : v0 + rows, cols].reshape(n_pieces * rows, head_size)
        scores[h] = nt_dot(query, keys)
        for g, group in enumerate(groups):
            scores[h, group, own_cols[g]] = nt_dot(query[group], key[group])
            outs[g][:rows, beside] = key[group]
            outs[g][rows:, beside] = value[group]
        text_s = nt_dot(query, tk_ref[:, cols])
        image_s = scores[h]
        largest = jnp.maximum(
            jnp.max(text_s, axis=-1, keepdims=True), jnp.max(image_s, axis=-1, keepdims=True)
        )
        text_e = jnp.exp2((text_s - largest) * scale)
        image_e = jnp.exp2((image_s - largest) * scale)
        total = jnp.sum(text_e, axis=-1, keepdims=True) + jnp.sum(image_e, axis=-1, keepdims=True)
        expos[h] = image_e.astype(jnp.bfloat16)
        fresh_mix = []
        for g, group in enumerate(groups):
            fresh_mix.append(
                jnp.dot(
                    expos[h, group, own_cols[g]], value[group], preferred_element_type=jnp.float32
                )
            )
            expos[h, group, own_cols[g]] = jnp.zeros((rows, rows), jnp.bfloat16)
        mixture = (
            jnp.dot(text_e.astype(jnp.bfloat16), tv_ref[:, cols], preferred_element_type=jnp.float32)
            + jnp.dot(expos[h], values, preferred_element_type=jnp.float32)
            + jnp.concatenate(fresh_mix, axis=0)
        )
        attended = (mixture / total).astype(jnp.bfloat16)
        for g, group in enumerate(groups):
            first = pl.multiple_of(lax.rem(owns[g] // INNER, 2) * rows, 16)
            for out in outs[g // 2 * 2 : g // 2 * 2 + 2]:
                out[pl.ds(first, rows), cols] = attended[group]


def attend_patches(where, patches, text_keys, text_values, query_gain, key_gain, pieces, depth):
    shares = [x for patch in patches for x in patch]
    model_width, width = shares[0].shape[1], pieces[0].shape[1]
    rows = sum(x.shape[0] for x in patches[0])
    n, n_pieces, texts, head_size = len(patches), len(pieces), text_keys.shape[0], query_gain.shape[0]
    heads, n_keys = width // head_size, n_pieces * rows
    whole = lambda i, w: (0, 0)
    return pl.pallas_call(
        functools.partial(patch_kernel, depth, n_pieces, [len(x) for x in patches]),
        grid_spec=pltpu.PrefetchScalarGridSpec(
            num_scalar_prefetch=1,
            grid=(1,),
            in_specs=[pl.BlockSpec((texts, width), lambda i, w: (0, w[0]))] * 2
            + [pl.BlockSpec((1, head_size), whole)] * 2
            + [pl.BlockSpec(memory_space=pl.ANY)] * (len(shares) + n_pieces),
            out_specs=[pl.BlockSpec((2 * rows, 2 * width), whole)] * n,
            scratch_shapes=[
                pltpu.VMEM((n * rows, model_width), jnp.bfloat16),
                pltpu.VMEM((n_pieces,) + pieces[0].shape, jnp.bfloat16),
                pltpu.VMEM((heads, n * rows, n_keys), jnp.float32),
                pltpu.VMEM((heads, n * rows, n_keys), jnp.bfloat16),
                pltpu.SemaphoreType.DMA((len(shares),)),
                pltpu.SemaphoreType.DMA((n_pieces,)),
                pltpu.SemaphoreType.DMA((n_pieces,)),
            ],
        ),
        out_shape=[jax.ShapeDtypeStruct((2 * rows, 2 * width), jnp.bfloat16)] * n,
        compiler_params=pltpu.CompilerParams(vmem_limit_bytes=VMEM_BYTES),
        cost_estimate=pl.CostEstimate(
            flops=2 * n * rows * (model_width * 3 * width + 2 * (texts + n_keys) * width),
            bytes_accessed=2 * n_pieces * pieces[0].size,
            transcendentals=n * rows * (texts + n_keys) * heads,
        ),
    )(
        where,
        text_keys,
        text_values,
        query_gain.reshape(1, -1),
        key_gain.reshape(1, -1),
        *shares,
        *pieces,
    )


def deal_kernel(n_arrays, team, member_ref, *refs):
    arrays, outs = refs[:n_arrays], refs[n_arrays:]
    width = outs[0].shape[1]
    for k in range(team):
        at = member_ref[0] ^ k
        cols = pl.ds(pl.multiple_of(at * width, 128), width)
        first = 0
        for x in arrays:
            rows = x.shape[0]
            outs[k][first : first + rows, :] = x[:, cols]
            first += rows


def deal(member, arrays, team):
    width = arrays[0].shape[1] // team
    shape = jax.ShapeDtypeStruct((sum(x.shape[0] for x in arrays), width), jnp.bfloat16)
    return pl.pallas_call(
        functools.partial(deal_kernel, len(arrays), team),
        in_specs=[pl.BlockSpec(memory_space=pltpu.SMEM)]
        + [pl.BlockSpec(memory_space=pltpu.VMEM)] * len(arrays),
        out_specs=[pl.BlockSpec(memory_space=pltpu.VMEM)] * team,
        out_shape=[shape] * team,
        compiler_params=pltpu.CompilerParams(vmem_limit_bytes=VMEM_BYTES),
    )(member.reshape(1), *arrays)


def collect_kernel(team, member_ref, *refs):
    packs, (key_ref, value_ref) = refs[:team], refs[team:]
    rows, width = key_ref.shape[0], key_ref.shape[1] // team
    for s in range(team):
        at = member_ref[0] ^ s
        cols = pl.ds(pl.multiple_of(at * width, 128), width)
        key_ref[:, cols] = packs[s][:rows, width:]
        value_ref[:, cols] = packs[s][rows:, width:]


def collect(member, packs):
    team = len(packs)
    rows, width = packs[0].shape[0] // 2, packs[0].shape[1] // 2
    shape = jax.ShapeDtypeStruct((rows, width * team), jnp.bfloat16)
    return pl.pallas_call(
        functools.partial(collect_kernel, team),
        in_specs=[pl.BlockSpec(memory_space=pltpu.SMEM)]
        + [pl.BlockSpec(memory_space=pltpu.VMEM)] * team,
        out_specs=[pl.BlockSpec(memory_space=pltpu.VMEM)] * 2,
        out_shape=[shape, shape],
        compiler_params=pltpu.CompilerParams(vmem_limit_bytes=VMEM_BYTES),
    )(member.reshape(1), *packs)


def project_kernel(n_packs, n_pieces, n_shares, where_ref, *refs):
    packs, pieces = refs[:n_packs], refs[n_packs : n_packs + n_pieces]
    refs = refs[n_packs + n_pieces :]
    outs, held, sems = refs[:-2], refs[-2], refs[-1]
    rows, width = packs[0].shape[0] // 2, packs[0].shape[1]
    depth = held.shape[1]
    copies = [
        pltpu.make_async_copy(piece, held.at[where_ref[2 + n_shares + i]], sems.at[i])
        for i, piece in enumerate(pieces)
    ]
    for copy in copies:
        copy.start()
    own = pl.multiple_of(where_ref[1] * rows, 16)
    other = pl.multiple_of((1 - where_ref[1]) * rows, 16)
    attended = [
        jnp.concatenate([x[pl.ds(own, rows), :], x[pl.ds(other, rows), :]], axis=0) for x in packs
    ]
    for copy in copies:
        copy.wait()
    for i in reversed(range(n_shares)):
        block = pl.ds(where_ref[2 + i] * INNER, INNER)
        total = jnp.zeros((2 * rows, INNER * depth), jnp.float32)
        for s in range(n_packs):
            cols = pl.ds(pl.multiple_of((where_ref[0] ^ s) * width, 128), width)
            total += nt_dot(attended[s], held[block, :, cols].reshape(INNER * depth, width))
        outs[2 * i][...] = total[:rows].astype(outs[2 * i].dtype)
        outs[2 * i + 1][...] = total[rows:].astype(outs[2 * i + 1].dtype)


def project(where, packs, pieces, n_shares):
    rows, width = packs[0].shape[0] // 2, packs[0].shape[1] // 2
    depth, local_width = pieces[0].shape
    block = INNER * depth
    whole = lambda i, w: (0, 0)
    types = [jnp.float32] + [jnp.bfloat16] * (2 * n_shares - 1)
    return pl.pallas_call(
        functools.partial(project_kernel, len(packs), len(pieces), n_shares),
        grid_spec=pltpu.PrefetchScalarGridSpec(
            num_scalar_prefetch=1,
            grid=(1,),
            in_specs=[pl.BlockSpec((2 * rows, width), whole)] * len(packs)
            + [pl.BlockSpec(memory_space=pl.ANY)] * len(pieces),
            out_specs=[pl.BlockSpec((rows, block), whole)] * len(types),
            scratch_shapes=[
                pltpu.VMEM((len(pieces), depth, local_width), jnp.bfloat16),
                pltpu.SemaphoreType.DMA((len(pieces),)),
            ],
        ),
        out_shape=[jax.ShapeDtypeStruct((rows, block), t) for t in types],
        compiler_params=pltpu.CompilerParams(vmem_limit_bytes=VMEM_BYTES),
        cost_estimate=pl.CostEstimate(
            flops=4 * rows * block * n_shares * local_width,
            bytes_accessed=2 * block * n_shares * local_width,
            transcendentals=0,
        ),
    )(where, *packs, *pieces)


def on_device(
    image,
    mod_shift,
    mod_scale,
    mod_gate,
    w_query,
    w_key,
    w_value,
    query_gain,
    key_gain,
    text_keys,
    text_values,
    stale_keys,
    stale_values,
    w_out,
):
    head_size = query_gain.shape[0]
    rows, model_width = image.shape
    depth, local_width = w_query.shape
    heads = local_width // head_size
    patches = lax.axis_size("patch")
    fsdp = lax.axis_size("fsdp")
    outer = patches // INNER
    team = math.gcd(outer, heads)
    width = local_width // team
    assert outer == 2 * fsdp and team > 1 and team & (team - 1) == 0 and outer & (outer - 1) == 0
    me = lax.axis_index("patch")
    mine = lax.axis_index("fsdp")
    place, seat = me // INNER, me % INNER
    member, parity = place % team, place % 2
    def over_outer(x, pairs):
        pairs = [(a * INNER + k, b * INNER + k) for a, b in pairs for k in range(INNER)]
        return lax.ppermute(x, "patch", pairs)

    def to_partner(x, bits):
        return over_outer(x, [(z, z ^ bits) for z in range(outer)])

    def flip(x, bits):
        return lax.ppermute(x, "patch", [(p, p ^ bits) for p in range(patches)])

    def along_fsdp(x, step):
        return lax.ppermute(x, "fsdp", [(i, (i + step) % fsdp) for i in range(fsdp)])

    def along_both(x, bits, step):
        pairs = [
            (p * fsdp + f, (p ^ (bits * INNER)) * fsdp + (f + step) % fsdp)
            for p in range(patches)
            for f in range(fsdp)
        ]
        return lax.ppermute(x, ("patch", "fsdp"), pairs)

    def spread(piece, side, *deps):
        return [piece, side, flip(after(piece, *deps), 1), flip(after(side, *deps), 1)]

    def shares_of(got):
        return [got] + [along_fsdp(got, i) for i in range(1, fsdp)]

    def seats_of(position):
        return [position * INNER + (seat ^ bits) for bits in (0, 2, 1, 3)]

    modded = modulate(image, mod_shift, mod_scale)
    share = rows // fsdp
    part = lax.dynamic_slice_in_dim(modded, mine * share, share, axis=0)
    dealt = deal(member, (w_query, w_key, w_value, stale_keys, stale_values), team)
    pieces, sides = {0: dealt[0]}, {}
    row_shares = {}
    if outer == 4 and team == 4:
        ends = [(1, 0), (2, 3)]
        middle = [(1, 2), (2, 1)]
        inside = jnp.logical_or(place == 1, place == 2)
        near = to_partner(part, 1)
        across = over_outer(part, middle)
        sides[0] = flip(pieces[0], 2)
        far = over_outer(near, middle)
        pieces[2] = to_partner(after(dealt[2], near, across), 2)
        pieces[1] = to_partner(after(dealt[1], near, across), 1)
        end_across = over_outer(across, ends)
        end_far = over_outer(after(far, sides[0]), ends)
        sides[1] = flip(after(pieces[1], far), 2)
        pieces[3] = to_partner(after(dealt[3], far), 3)
        sides[2] = flip(after(pieces[2], end_far, sides[1]), 2)
        row_shares[1] = shares_of(after(near, pieces[1]))
        row_shares[2] = shares_of(jnp.where(inside, far, end_across))
        row_shares[3] = shares_of(jnp.where(inside, across, end_far))
        late = [sides[2], row_shares[1][-1]]
    else:
        for k in range(1, team):
            row_shares[k] = shares_of(to_partner(part, k))
        for k in range(1, outer):
            pieces[k] = to_partner(dealt[k % team], k)
        late = []
    for k in range(outer):
        if k not in sides:
            sides[k] = flip(pieces[k], 2)
    out_piece = after(w_out.T, sides[outer - 1])
    out_pieces = [out_piece] + [to_partner(out_piece, 2 * k) for k in range(1, fsdp)]

    origins = [o for k in range(outer) for o in seats_of(place ^ k)]
    pieces = [x for k in range(outer) for x in spread(pieces[k], sides[k], *late)]
    patch_rows = [[modded]] + [row_shares[k] for k in range(1, team)]
    where = [member] + origins
    for k in range(team):
        where.append((place ^ k) * INNER + seat)
        where += [((mine + (fsdp - i)) % fsdp) * share for i in range(fsdp)] if k else [0 * mine]
    messages = attend_patches(
        jnp.stack(where).astype(jnp.int32),
        patch_rows,
        text_keys,
        text_values,
        query_gain,
        key_gain,
        pieces,
        depth,
    )

    def give(x, bits):
        return lax.ppermute(x, "patch", [(p, p ^ (bits * INNER)) for p in range(patches)])

    packs = [messages[0]] + [give(messages[k], k) for k in range(1, team)]
    out_sides = [flip(out_pieces[0], 2)]
    out_sides += [flip(after(piece, messages[0]), 2) for piece in out_pieces[1:]]
    out_pieces = [x for p, q in zip(out_pieces, out_sides) for x in spread(p, q, *packs[1:])]
    out_places = [o for k in range(fsdp) for o in seats_of((place ^ (2 * k)) // 2)]
    where = [member, parity] + [(mine + i) % fsdp for i in range(fsdp)] + out_places
    where = jnp.stack(where).astype(jnp.int32)
    partial = project(where, packs, out_pieces, fsdp)
    own, partner = partial[0], [along_both(partial[1], 1, 0)]
    for i in range(1, fsdp):
        own = own + along_fsdp(partial[2 * i], i).astype(jnp.float32)
        partner.append(along_both(partial[2 * i + 1], 1, i))
    other = sum(x.astype(jnp.float32) for x in partner)
    summed = jnp.where(
        parity == 0,
        jnp.concatenate([own, other], axis=1),
        jnp.concatenate([other, own], axis=1),
    )
    key_out, value_out = collect(member, [after(packs[0], partial[0])] + packs[1:])

    out_share = model_width // fsdp
    col_start = mine * out_share
    image_part = lax.dynamic_slice_in_dim(image, col_start, out_share, 1).astype(jnp.float32)
    gate_part = lax.dynamic_slice_in_dim(mod_gate, col_start, out_share, 0)
    hidden = (image_part + gate_part * summed).astype(jnp.bfloat16)
    return (hidden, key_out, value_out)


def solution(mesh):
    return jax.shard_map(
        on_device,
        mesh=mesh,
        in_specs=(
            P("patch", None),
            P(),
            P(),
            P(),
            P("patch", "fsdp"),
            P("patch", "fsdp"),
            P("patch", "fsdp"),
            P(),
            P(),
            P(None, "fsdp"),
            P(None, "fsdp"),
            P("patch", "fsdp"),
            P("patch", "fsdp"),
            P("fsdp", "patch"),
        ),
        out_specs=(P("patch", "fsdp"), P("patch", "fsdp"), P("patch", "fsdp")),
        check_vma=False,
    )
```

```python
import functools
import math

import jax
import jax.numpy as jnp
from jax import lax
from jax.experimental import pallas as pl
from jax.experimental.pallas import tpu as pltpu
from jax.sharding import PartitionSpec as P

INNER = 4
VMEM_BYTES = 60 * 1024 * 1024


def modulate(image, mod_shift, mod_scale):
    values = image.astype(jnp.float32)
    center = jnp.mean(values, axis=-1, keepdims=True)
    spread = jnp.mean(jnp.square(values - center), axis=-1, keepdims=True)
    normed = (values - center) * lax.rsqrt(spread + 1e-06)
    return ((1.0 + mod_scale) * normed + mod_shift).astype(jnp.bfloat16)


def after(x, *deps):
    return lax.optimization_barrier((x,) + deps)[0]


def nt_dot(a, b):
    return lax.dot_general(a, b, (((1,), (1,)), ((), ())), preferred_element_type=jnp.float32)


def norm_heads(x, gain):
    power = jnp.mean(x * x, axis=-1, keepdims=True)
    return (x * lax.rsqrt(power + 1e-06) * gain).astype(jnp.bfloat16)


def patch_kernel(depth, n_pieces, cuts, where_ref, *refs):
    n_patches = len(cuts)
    tk_ref, tv_ref, qg_ref, kg_ref = refs[:4]
    n_rows = 1 + max(i for cut in cuts for i, _, _ in cut)
    arrays, refs = refs[4 : 4 + n_rows], refs[4 + n_rows :]
    pieces, refs = refs[:n_pieces], refs[n_pieces:]
    outs, (x_ref, held, scores, expos, x_sem, w_sem) = refs[:n_patches], refs[n_patches:]
    rows, width = outs[0].shape[0] // 2, outs[0].shape[1] // 2
    head_size = qg_ref.shape[1]
    groups = [slice(g * rows, (g + 1) * rows) for g in range(n_patches)]
    owns, x_copies, at = [], [], 1 + n_pieces
    for g, cut in enumerate(cuts):
        owns.append(where_ref[at])
        for i, (array, start, length) in enumerate(cut):
            first = pl.multiple_of(g * rows + where_ref[at + 1 + i], 16)
            x_copies.append(
                pltpu.make_async_copy(
                    arrays[array].at[pl.ds(start, length)],
                    x_ref.at[pl.ds(first, length)],
                    x_sem.at[len(x_copies)],
                )
            )
        at += 1 + len(cut)
    w_copies = [
        pltpu.make_async_copy(piece, held.at[where_ref[1 + i]], w_sem.at[i])
        for i, piece in enumerate(pieces)
    ]
    for copy in x_copies + w_copies:
        copy.start()
    for copy in x_copies:
        copy.wait()

    chunk = INNER * depth
    proj = [jnp.zeros((n_patches * rows, width), jnp.float32) for _ in range(3)]
    if chunk % 128 == 0:
        for first in range(0, n_pieces, INNER):
            for copy in w_copies[first : first + INNER]:
                copy.wait()
            place = where_ref[1 + first] // INNER
            part = x_ref[:, pl.ds(pl.multiple_of(place * chunk, 128), chunk)]
            for i in range(3):
                weight = held[pl.ds(place * INNER, INNER), i * depth : (i + 1) * depth, :]
                proj[i] += jnp.dot(
                    part, weight.reshape(chunk, width), preferred_element_type=jnp.float32
                )
    else:
        for copy in w_copies:
            copy.wait()
        for i in range(3):
            weight = held[:, i * depth : (i + 1) * depth, :]
            proj[i] += jnp.dot(
                x_ref[...],
                weight.reshape(n_pieces * depth, width),
                preferred_element_type=jnp.float32,
            )
    q_proj, k_proj, v_proj = proj

    v_new = v_proj.astype(jnp.bfloat16)
    k0, v0 = 3 * depth, 3 * depth + rows
    scale = math.log2(math.e) / math.sqrt(head_size)
    own_cols = [pl.ds(pl.multiple_of(own * rows, 128), rows) for own in owns]
    for h in range(width // head_size):
        cols = slice(h * head_size, (h + 1) * head_size)
        beside = slice(width + cols.start, width + cols.stop)
        query = norm_heads(q_proj[:, cols], qg_ref[...])
        key = norm_heads(k_proj[:, cols], kg_ref[...])
        value = v_new[:, cols]
        keys = held[:, k0 : k0 + rows, cols].reshape(n_pieces * rows, head_size)
        values = held[:, v0 : v0 + rows, cols].reshape(n_pieces * rows, head_size)
        scores[h] = nt_dot(query, keys)
        for g, group in enumerate(groups):
            scores[h, group, own_cols[g]] = nt_dot(query[group], key[group])
            outs[g][:rows, beside] = key[group]
            outs[g][rows:, beside] = value[group]
        text_s = nt_dot(query, tk_ref[:, cols])
        image_s = scores[h]
        largest = jnp.maximum(
            jnp.max(text_s, axis=-1, keepdims=True), jnp.max(image_s, axis=-1, keepdims=True)
        )
        text_e = jnp.exp2((text_s - largest) * scale)
        image_e = jnp.exp2((image_s - largest) * scale)
        total = jnp.sum(text_e, axis=-1, keepdims=True) + jnp.sum(image_e, axis=-1, keepdims=True)
        expos[h] = image_e.astype(jnp.bfloat16)
        fresh_mix = []
        for g, group in enumerate(groups):
            fresh_mix.append(
                jnp.dot(
                    expos[h, group, own_cols[g]], value[group], preferred_element_type=jnp.float32
                )
            )
            expos[h, group, own_cols[g]] = jnp.zeros((rows, rows), jnp.bfloat16)
        mixture = (
            jnp.dot(text_e.astype(jnp.bfloat16), tv_ref[:, cols], preferred_element_type=jnp.float32)
            + jnp.dot(expos[h], values, preferred_element_type=jnp.float32)
            + jnp.concatenate(fresh_mix, axis=0)
        )
        attended = (mixture / total).astype(jnp.bfloat16)
        for g, group in enumerate(groups):
            first = pl.multiple_of(lax.rem(owns[g] // INNER, 2) * rows, 16)
            for out in outs[g // 2 * 2 : g // 2 * 2 + 2]:
                out[pl.ds(first, rows), cols] = attended[group]


def attend_patches(where, patches, text_keys, text_values, query_gain, key_gain, pieces, depth):
    arrays, cuts, (rows, model_width), width = [], [], patches[0][0].shape, pieces[0].shape[1]
    for patch in patches:
        cuts.append([])
        for x in patch:
            x, start = x if isinstance(x, tuple) else (x, 0)
            held = [i for i, y in enumerate(arrays) if y is x]
            if not held:
                arrays.append(x)
            place = held[0] if held else len(arrays) - 1
            cuts[-1].append((place, start, rows // len(patch)))
    n, n_pieces, texts, head_size = len(patches), len(pieces), text_keys.shape[0], query_gain.shape[0]
    heads, n_keys = width // head_size, n_pieces * rows
    whole = lambda i, w: (0, 0)
    return pl.pallas_call(
        functools.partial(patch_kernel, depth, n_pieces, cuts),
        grid_spec=pltpu.PrefetchScalarGridSpec(
            num_scalar_prefetch=1,
            grid=(1,),
            in_specs=[pl.BlockSpec((texts, width), lambda i, w: (0, w[0]))] * 2
            + [pl.BlockSpec((1, head_size), whole)] * 2
            + [pl.BlockSpec(memory_space=pl.ANY)] * (len(arrays) + n_pieces),
            out_specs=[pl.BlockSpec((2 * rows, 2 * width), whole)] * n,
            scratch_shapes=[
                pltpu.VMEM((n * rows, model_width), jnp.bfloat16),
                pltpu.VMEM((n_pieces,) + pieces[0].shape, jnp.bfloat16),
                pltpu.VMEM((heads, n * rows, n_keys), jnp.float32),
                pltpu.VMEM((heads, n * rows, n_keys), jnp.bfloat16),
                pltpu.SemaphoreType.DMA((sum(len(cut) for cut in cuts),)),
                pltpu.SemaphoreType.DMA((n_pieces,)),
            ],
        ),
        out_shape=[jax.ShapeDtypeStruct((2 * rows, 2 * width), jnp.bfloat16)] * n,
        compiler_params=pltpu.CompilerParams(vmem_limit_bytes=VMEM_BYTES),
        cost_estimate=pl.CostEstimate(
            flops=2 * n * rows * (model_width * 3 * width + 2 * (texts + n_keys) * width),
            bytes_accessed=2 * n_pieces * pieces[0].size,
            transcendentals=n * rows * (texts + n_keys) * heads,
        ),
    )(
        where,
        text_keys,
        text_values,
        query_gain.reshape(1, -1),
        key_gain.reshape(1, -1),
        *arrays,
        *pieces,
    )


def deal_kernel(n_arrays, team, member_ref, *refs):
    arrays, outs = refs[:n_arrays], refs[n_arrays:]
    width = outs[0].shape[1]
    for k in range(team):
        at = member_ref[0] ^ k
        cols = pl.ds(pl.multiple_of(at * width, 128), width)
        first = 0
        for x in arrays:
            rows = x.shape[0]
            outs[k][first : first + rows, :] = x[:, cols]
            first += rows


def deal(member, arrays, team):
    width = arrays[0].shape[1] // team
    shape = jax.ShapeDtypeStruct((sum(x.shape[0] for x in arrays), width), jnp.bfloat16)
    return pl.pallas_call(
        functools.partial(deal_kernel, len(arrays), team),
        in_specs=[pl.BlockSpec(memory_space=pltpu.SMEM)]
        + [pl.BlockSpec(memory_space=pltpu.VMEM)] * len(arrays),
        out_specs=[pl.BlockSpec(memory_space=pltpu.VMEM)] * team,
        out_shape=[shape] * team,
        compiler_params=pltpu.CompilerParams(vmem_limit_bytes=VMEM_BYTES),
    )(member.reshape(1), *arrays)


def collect_kernel(team, member_ref, *refs):
    packs, (key_ref, value_ref) = refs[:team], refs[team:]
    rows, width = key_ref.shape[0], key_ref.shape[1] // team
    for s in range(team):
        at = member_ref[0] ^ s
        cols = pl.ds(pl.multiple_of(at * width, 128), width)
        key_ref[:, cols] = packs[s][:rows, width:]
        value_ref[:, cols] = packs[s][rows:, width:]


def collect(member, packs):
    team = len(packs)
    rows, width = packs[0].shape[0] // 2, packs[0].shape[1] // 2
    shape = jax.ShapeDtypeStruct((rows, width * team), jnp.bfloat16)
    return pl.pallas_call(
        functools.partial(collect_kernel, team),
        in_specs=[pl.BlockSpec(memory_space=pltpu.SMEM)]
        + [pl.BlockSpec(memory_space=pltpu.VMEM)] * team,
        out_specs=[pl.BlockSpec(memory_space=pltpu.VMEM)] * 2,
        out_shape=[shape, shape],
        compiler_params=pltpu.CompilerParams(vmem_limit_bytes=VMEM_BYTES),
    )(member.reshape(1), *packs)


def project_kernel(n_packs, n_pieces, n_shares, where_ref, *refs):
    packs, pieces = refs[:n_packs], refs[n_packs : n_packs + n_pieces]
    refs = refs[n_packs + n_pieces :]
    outs, held, sems = refs[:-2], refs[-2], refs[-1]
    rows, width = packs[0].shape[0] // 2, packs[0].shape[1]
    depth = held.shape[1]
    copies = [
        pltpu.make_async_copy(piece, held.at[where_ref[2 + n_shares + i]], sems.at[i])
        for i, piece in enumerate(pieces)
    ]
    for copy in copies:
        copy.start()
    own = pl.multiple_of(where_ref[1] * rows, 16)
    other = pl.multiple_of((1 - where_ref[1]) * rows, 16)
    attended = [
        jnp.concatenate([x[pl.ds(own, rows), :], x[pl.ds(other, rows), :]], axis=0) for x in packs
    ]
    for copy in copies:
        copy.wait()
    for i in reversed(range(n_shares)):
        block = pl.ds(where_ref[2 + i] * INNER, INNER)
        total = jnp.zeros((2 * rows, INNER * depth), jnp.float32)
        for s in range(n_packs):
            cols = pl.ds(pl.multiple_of((where_ref[0] ^ s) * width, 128), width)
            total += nt_dot(attended[s], held[block, :, cols].reshape(INNER * depth, width))
        outs[2 * i][...] = total[:rows].astype(outs[2 * i].dtype)
        outs[2 * i + 1][...] = total[rows:].astype(outs[2 * i + 1].dtype)


def project(where, packs, pieces, n_shares):
    rows, width = packs[0].shape[0] // 2, packs[0].shape[1] // 2
    depth, local_width = pieces[0].shape
    block = INNER * depth
    whole = lambda i, w: (0, 0)
    types = [jnp.float32] + [jnp.bfloat16] * (2 * n_shares - 1)
    return pl.pallas_call(
        functools.partial(project_kernel, len(packs), len(pieces), n_shares),
        grid_spec=pltpu.PrefetchScalarGridSpec(
            num_scalar_prefetch=1,
            grid=(1,),
            in_specs=[pl.BlockSpec((2 * rows, width), whole)] * len(packs)
            + [pl.BlockSpec(memory_space=pl.ANY)] * len(pieces),
            out_specs=[pl.BlockSpec((rows, block), whole)] * len(types),
            scratch_shapes=[
                pltpu.VMEM((len(pieces), depth, local_width), jnp.bfloat16),
                pltpu.SemaphoreType.DMA((len(pieces),)),
            ],
        ),
        out_shape=[jax.ShapeDtypeStruct((rows, block), t) for t in types],
        compiler_params=pltpu.CompilerParams(vmem_limit_bytes=VMEM_BYTES),
        cost_estimate=pl.CostEstimate(
            flops=4 * rows * block * n_shares * local_width,
            bytes_accessed=2 * block * n_shares * local_width,
            transcendentals=0,
        ),
    )(where, *packs, *pieces)


def on_device(
    image,
    mod_shift,
    mod_scale,
    mod_gate,
    w_query,
    w_key,
    w_value,
    query_gain,
    key_gain,
    text_keys,
    text_values,
    stale_keys,
    stale_values,
    w_out,
):
    head_size = query_gain.shape[0]
    rows, model_width = image.shape
    depth, local_width = w_query.shape
    heads = local_width // head_size
    patches = lax.axis_size("patch")
    fsdp = lax.axis_size("fsdp")
    outer = patches // INNER
    team = math.gcd(outer, heads)
    width = local_width // team
    assert outer == 2 * fsdp and team > 1 and team & (team - 1) == 0 and outer & (outer - 1) == 0
    me = lax.axis_index("patch")
    mine = lax.axis_index("fsdp")
    place, seat = me // INNER, me % INNER
    member, parity = place % team, place % 2
    def over_outer(x, pairs):
        pairs = [(a * INNER + k, b * INNER + k) for a, b in pairs for k in range(INNER)]
        return lax.ppermute(x, "patch", pairs)

    def to_partner(x, bits):
        return over_outer(x, [(z, z ^ bits) for z in range(outer)])

    def flip(x, bits):
        return lax.ppermute(x, "patch", [(p, p ^ bits) for p in range(patches)])

    def along_fsdp(x, step):
        return lax.ppermute(x, "fsdp", [(i, (i + step) % fsdp) for i in range(fsdp)])

    def along_both(x, bits, step):
        pairs = [
            (p * fsdp + f, (p ^ (bits * INNER)) * fsdp + (f + step) % fsdp)
            for p in range(patches)
            for f in range(fsdp)
        ]
        return lax.ppermute(x, ("patch", "fsdp"), pairs)

    def spread(piece, side, *deps):
        return [piece, side, flip(after(piece, *deps), 1), flip(after(side, *deps), 1)]

    def shares_of(got):
        return [got] + [along_fsdp(got, i) for i in range(1, fsdp)]

    def seats_of(position):
        return [position * INNER + (seat ^ bits) for bits in (0, 2, 1, 3)]

    modded = modulate(image, mod_shift, mod_scale)
    share = rows // fsdp
    part = lax.dynamic_slice_in_dim(modded, mine * share, share, axis=0)
    dealt = deal(member, (w_query, w_key, w_value, stale_keys, stale_values), team)
    pieces, sides = {0: dealt[0]}, {}
    row_shares = {}
    if outer == 4 and team == 4:
        ends = [(1, 0), (2, 3)]
        middle = [(1, 2), (2, 1)]
        inside = jnp.logical_or(place == 1, place == 2)
        near = to_partner(part, 1)
        across = over_outer(part, middle)
        sides[0] = flip(pieces[0], 2)
        far = over_outer(near, middle)
        pieces[2] = to_partner(after(dealt[2], near, across), 2)
        pieces[1] = to_partner(after(dealt[1], near, across), 1)
        row_shares[1] = shares_of(after(near, sides[0]))
        end_across = over_outer(after(across, pieces[1]), ends)
        end_far = over_outer(after(far, row_shares[1][-1]), ends)
        sides[1] = flip(after(pieces[1], far), 2)
        pieces[3] = to_partner(after(dealt[3], far), 3)
        row_shares[2] = shares_of(jnp.where(inside, far, end_across))
        row_shares[3] = shares_of(jnp.where(inside, across, end_far))
        sides[2] = flip(after(pieces[2], end_far, sides[1]), 2)
        late = [sides[2], row_shares[2][-1]]
        later = [row_shares[3][-1]]
    else:
        for k in range(1, team):
            row_shares[k] = shares_of(to_partner(part, k))
        for k in range(1, outer):
            pieces[k] = to_partner(dealt[k % team], k)
        late = later = []
    for k in range(outer):
        if k not in sides:
            sides[k] = flip(pieces[k], 2)
    out_piece = after(w_out.T, sides[outer - 1])
    out_pieces = [out_piece] + [to_partner(out_piece, 2 * k) for k in range(1, fsdp)]

    origins = [o for k in range(outer) for o in seats_of(place ^ k)]
    deps = lambda k: late if k < 2 else later
    pieces = [x for k in range(outer) for x in spread(pieces[k], sides[k], *deps(k))]
    patch_rows = [[modded]] + [row_shares[k] for k in range(1, team)]
    where = [member] + origins
    for k in range(team):
        where.append((place ^ k) * INNER + seat)
        where += [((mine + (fsdp - i)) % fsdp) * share for i in range(fsdp)] if k else [0 * mine]
    messages = attend_patches(
        jnp.stack(where).astype(jnp.int32),
        patch_rows,
        text_keys,
        text_values,
        query_gain,
        key_gain,
        pieces,
        depth,
    )

    def give(x, bits):
        return lax.ppermute(x, "patch", [(p, p ^ (bits * INNER)) for p in range(patches)])

    packs = [messages[0]] + [give(messages[k], k) for k in range(1, team)]
    out_sides = [flip(out_pieces[0], 2)]
    out_sides += [flip(after(piece, messages[0]), 2) for piece in out_pieces[1:]]
    out_pieces = [x for p, q in zip(out_pieces, out_sides) for x in spread(p, q, *packs[1:])]
    out_places = [o for k in range(fsdp) for o in seats_of((place ^ (2 * k)) // 2)]
    where = [member, parity] + [(mine + i) % fsdp for i in range(fsdp)] + out_places
    where = jnp.stack(where).astype(jnp.int32)
    partial = project(where, packs, out_pieces, fsdp)
    own, partner = partial[0], [along_both(partial[1], 1, 0)]
    for i in range(1, fsdp):
        own = own + along_fsdp(partial[2 * i], i).astype(jnp.float32)
        partner.append(along_both(partial[2 * i + 1], 1, i))
    other = sum(x.astype(jnp.float32) for x in partner)
    summed = jnp.where(
        parity == 0,
        jnp.concatenate([own, other], axis=1),
        jnp.concatenate([other, own], axis=1),
    )
    key_out, value_out = collect(member, [after(packs[0], partial[0])] + packs[1:])

    out_share = model_width // fsdp
    col_start = mine * out_share
    image_part = lax.dynamic_slice_in_dim(image, col_start, out_share, 1).astype(jnp.float32)
    gate_part = lax.dynamic_slice_in_dim(mod_gate, col_start, out_share, 0)
    hidden = (image_part + gate_part * summed).astype(jnp.bfloat16)
    return (hidden, key_out, value_out)


def solution(mesh):
    return jax.shard_map(
        on_device,
        mesh=mesh,
        in_specs=(
            P("patch", None),
            P(),
            P(),
            P(),
            P("patch", "fsdp"),
            P("patch", "fsdp"),
            P("patch", "fsdp"),
            P(),
            P(),
            P(None, "fsdp"),
            P(None, "fsdp"),
            P("patch", "fsdp"),
            P("patch", "fsdp"),
            P("fsdp", "patch"),
        ),
        out_specs=(P("patch", "fsdp"), P("patch", "fsdp"), P("patch", "fsdp")),
        check_vma=False,
    )
```

```python
import functools
import math

import jax
import jax.numpy as jnp
from jax import lax
from jax.experimental import pallas as pl
from jax.experimental.pallas import tpu as pltpu
from jax.sharding import PartitionSpec as P

INNER = 4
VMEM_BYTES = 60 * 1024 * 1024


def modulate(image, mod_shift, mod_scale):
    values = image.astype(jnp.float32)
    center = jnp.mean(values, axis=-1, keepdims=True)
    spread = jnp.mean(jnp.square(values - center), axis=-1, keepdims=True)
    normed = (values - center) * lax.rsqrt(spread + 1e-06)
    return ((1.0 + mod_scale) * normed + mod_shift).astype(jnp.bfloat16)


def after(x, *deps):
    return lax.optimization_barrier((x,) + deps)[0]


def nt_dot(a, b):
    return lax.dot_general(a, b, (((1,), (1,)), ((), ())), preferred_element_type=jnp.float32)


def norm_heads(x, gain):
    power = jnp.mean(x * x, axis=-1, keepdims=True)
    return (x * lax.rsqrt(power + 1e-06) * gain).astype(jnp.bfloat16)


def patch_kernel(depth, n_pieces, cuts, where_ref, *refs):
    n_patches = len(cuts)
    tk_ref, tv_ref, qg_ref, kg_ref = refs[:4]
    n_rows = 1 + max(i for cut in cuts for i, _, _ in cut)
    arrays, refs = refs[4 : 4 + n_rows], refs[4 + n_rows :]
    pieces, refs = refs[:n_pieces], refs[n_pieces:]
    outs, (x_ref, held, scores, expos, x_sem, w_sem) = refs[:n_patches], refs[n_patches:]
    rows, width = outs[0].shape[0] // 2, outs[0].shape[1] // 2
    head_size = qg_ref.shape[1]
    groups = [slice(g * rows, (g + 1) * rows) for g in range(n_patches)]
    owns, x_copies, at = [], [], 1 + n_pieces
    for g, cut in enumerate(cuts):
        owns.append(where_ref[at])
        for i, (array, start, length) in enumerate(cut):
            first = pl.multiple_of(g * rows + where_ref[at + 1 + i], 16)
            x_copies.append(
                pltpu.make_async_copy(
                    arrays[array].at[pl.ds(start, length)],
                    x_ref.at[pl.ds(first, length)],
                    x_sem.at[len(x_copies)],
                )
            )
        at += 1 + len(cut)
    w_copies = [
        pltpu.make_async_copy(piece, held.at[where_ref[1 + i]], w_sem.at[i])
        for i, piece in enumerate(pieces)
    ]
    for copy in x_copies + w_copies:
        copy.start()
    for copy in x_copies:
        copy.wait()

    chunk = INNER * depth
    proj = [jnp.zeros((n_patches * rows, width), jnp.float32) for _ in range(3)]
    if chunk % 128 == 0:
        for first in range(0, n_pieces, INNER):
            for copy in w_copies[first : first + INNER]:
                copy.wait()
            place = where_ref[1 + first] // INNER
            part = x_ref[:, pl.ds(pl.multiple_of(place * chunk, 128), chunk)]
            for i in range(3):
                weight = held[pl.ds(place * INNER, INNER), i * depth : (i + 1) * depth, :]
                proj[i] += jnp.dot(
                    part, weight.reshape(chunk, width), preferred_element_type=jnp.float32
                )
    else:
        for copy in w_copies:
            copy.wait()
        for i in range(3):
            weight = held[:, i * depth : (i + 1) * depth, :]
            proj[i] += jnp.dot(
                x_ref[...],
                weight.reshape(n_pieces * depth, width),
                preferred_element_type=jnp.float32,
            )
    q_proj, k_proj, v_proj = proj

    v_new = v_proj.astype(jnp.bfloat16)
    k0, v0 = 3 * depth, 3 * depth + rows
    scale = math.log2(math.e) / math.sqrt(head_size)
    own_cols = [pl.ds(pl.multiple_of(own * rows, 128), rows) for own in owns]
    for h in range(width // head_size):
        cols = slice(h * head_size, (h + 1) * head_size)
        beside = slice(width + cols.start, width + cols.stop)
        query = norm_heads(q_proj[:, cols], qg_ref[...])
        key = norm_heads(k_proj[:, cols], kg_ref[...])
        value = v_new[:, cols]
        keys = held[:, k0 : k0 + rows, cols].reshape(n_pieces * rows, head_size)
        values = held[:, v0 : v0 + rows, cols].reshape(n_pieces * rows, head_size)
        scores[h] = nt_dot(query, keys)
        for g, group in enumerate(groups):
            scores[h, group, own_cols[g]] = nt_dot(query[group], key[group])
            outs[g][:rows, beside] = key[group]
            outs[g][rows:, beside] = value[group]
        text_s = nt_dot(query, tk_ref[:, cols])
        image_s = scores[h]
        largest = jnp.maximum(
            jnp.max(text_s, axis=-1, keepdims=True), jnp.max(image_s, axis=-1, keepdims=True)
        )
        text_e = jnp.exp2((text_s - largest) * scale)
        image_e = jnp.exp2((image_s - largest) * scale)
        total = jnp.sum(text_e, axis=-1, keepdims=True) + jnp.sum(image_e, axis=-1, keepdims=True)
        expos[h] = image_e.astype(jnp.bfloat16)
        fresh_mix = []
        for g, group in enumerate(groups):
            fresh_mix.append(
                jnp.dot(
                    expos[h, group, own_cols[g]], value[group], preferred_element_type=jnp.float32
                )
            )
            expos[h, group, own_cols[g]] = jnp.zeros((rows, rows), jnp.bfloat16)
        mixture = (
            jnp.dot(text_e.astype(jnp.bfloat16), tv_ref[:, cols], preferred_element_type=jnp.float32)
            + jnp.dot(expos[h], values, preferred_element_type=jnp.float32)
            + jnp.concatenate(fresh_mix, axis=0)
        )
        attended = (mixture / total).astype(jnp.bfloat16)
        for g, group in enumerate(groups):
            first = pl.multiple_of(lax.rem(owns[g] // INNER, 2) * rows, 16)
            for out in outs[g // 2 * 2 : g // 2 * 2 + 2]:
                out[pl.ds(first, rows), cols] = attended[group]


def attend_patches(where, patches, text_keys, text_values, query_gain, key_gain, pieces, depth):
    arrays, cuts, (rows, model_width), width = [], [], patches[0][0].shape, pieces[0].shape[1]
    for patch in patches:
        cuts.append([])
        for x in patch:
            x, start = x if isinstance(x, tuple) else (x, 0)
            held = [i for i, y in enumerate(arrays) if y is x]
            if not held:
                arrays.append(x)
            place = held[0] if held else len(arrays) - 1
            cuts[-1].append((place, start, rows // len(patch)))
    n, n_pieces, texts, head_size = len(patches), len(pieces), text_keys.shape[0], query_gain.shape[0]
    heads, n_keys = width // head_size, n_pieces * rows
    whole = lambda i, w: (0, 0)
    return pl.pallas_call(
        functools.partial(patch_kernel, depth, n_pieces, cuts),
        grid_spec=pltpu.PrefetchScalarGridSpec(
            num_scalar_prefetch=1,
            grid=(1,),
            in_specs=[pl.BlockSpec((texts, width), lambda i, w: (0, w[0]))] * 2
            + [pl.BlockSpec((1, head_size), whole)] * 2
            + [pl.BlockSpec(memory_space=pl.ANY)] * (len(arrays) + n_pieces),
            out_specs=[pl.BlockSpec((2 * rows, 2 * width), whole)] * n,
            scratch_shapes=[
                pltpu.VMEM((n * rows, model_width), jnp.bfloat16),
                pltpu.VMEM((n_pieces,) + pieces[0].shape, jnp.bfloat16),
                pltpu.VMEM((heads, n * rows, n_keys), jnp.float32),
                pltpu.VMEM((heads, n * rows, n_keys), jnp.bfloat16),
                pltpu.SemaphoreType.DMA((sum(len(cut) for cut in cuts),)),
                pltpu.SemaphoreType.DMA((n_pieces,)),
            ],
        ),
        out_shape=[jax.ShapeDtypeStruct((2 * rows, 2 * width), jnp.bfloat16)] * n,
        compiler_params=pltpu.CompilerParams(vmem_limit_bytes=VMEM_BYTES),
        cost_estimate=pl.CostEstimate(
            flops=2 * n * rows * (model_width * 3 * width + 2 * (texts + n_keys) * width),
            bytes_accessed=2 * n_pieces * pieces[0].size,
            transcendentals=n * rows * (texts + n_keys) * heads,
        ),
    )(
        where,
        text_keys,
        text_values,
        query_gain.reshape(1, -1),
        key_gain.reshape(1, -1),
        *arrays,
        *pieces,
    )


def deal_kernel(n_arrays, team, member_ref, *refs):
    arrays, outs = refs[:n_arrays], refs[n_arrays:]
    width = outs[0].shape[1]
    for k in range(team):
        at = member_ref[0] ^ k
        cols = pl.ds(pl.multiple_of(at * width, 128), width)
        first = 0
        for x in arrays:
            rows = x.shape[0]
            outs[k][first : first + rows, :] = x[:, cols]
            first += rows


def deal(member, arrays, team):
    width = arrays[0].shape[1] // team
    shape = jax.ShapeDtypeStruct((sum(x.shape[0] for x in arrays), width), jnp.bfloat16)
    return pl.pallas_call(
        functools.partial(deal_kernel, len(arrays), team),
        in_specs=[pl.BlockSpec(memory_space=pltpu.SMEM)]
        + [pl.BlockSpec(memory_space=pltpu.VMEM)] * len(arrays),
        out_specs=[pl.BlockSpec(memory_space=pltpu.VMEM)] * team,
        out_shape=[shape] * team,
        compiler_params=pltpu.CompilerParams(vmem_limit_bytes=VMEM_BYTES),
    )(member.reshape(1), *arrays)


def collect_kernel(team, member_ref, *refs):
    packs, (key_ref, value_ref) = refs[:team], refs[team:]
    rows, width = key_ref.shape[0], key_ref.shape[1] // team
    for s in range(team):
        at = member_ref[0] ^ s
        cols = pl.ds(pl.multiple_of(at * width, 128), width)
        key_ref[:, cols] = packs[s][:rows, width:]
        value_ref[:, cols] = packs[s][rows:, width:]


def collect(member, packs):
    team = len(packs)
    rows, width = packs[0].shape[0] // 2, packs[0].shape[1] // 2
    shape = jax.ShapeDtypeStruct((rows, width * team), jnp.bfloat16)
    return pl.pallas_call(
        functools.partial(collect_kernel, team),
        in_specs=[pl.BlockSpec(memory_space=pltpu.SMEM)]
        + [pl.BlockSpec(memory_space=pltpu.VMEM)] * team,
        out_specs=[pl.BlockSpec(memory_space=pltpu.VMEM)] * 2,
        out_shape=[shape, shape],
        compiler_params=pltpu.CompilerParams(vmem_limit_bytes=VMEM_BYTES),
    )(member.reshape(1), *packs)


def project_kernel(n_packs, n_pieces, n_shares, where_ref, *refs):
    packs, pieces = refs[:n_packs], refs[n_packs : n_packs + n_pieces]
    refs = refs[n_packs + n_pieces :]
    outs, held, sems = refs[:-2], refs[-2], refs[-1]
    rows, width = packs[0].shape[0] // 2, packs[0].shape[1]
    depth = held.shape[1]
    copies = [
        pltpu.make_async_copy(piece, held.at[where_ref[2 + n_shares + i]], sems.at[i])
        for i, piece in enumerate(pieces)
    ]
    for copy in copies:
        copy.start()
    own = pl.multiple_of(where_ref[1] * rows, 16)
    other = pl.multiple_of((1 - where_ref[1]) * rows, 16)
    attended = [
        jnp.concatenate([x[pl.ds(own, rows), :], x[pl.ds(other, rows), :]], axis=0) for x in packs
    ]
    for copy in copies:
        copy.wait()
    for i in reversed(range(n_shares)):
        block = pl.ds(where_ref[2 + i] * INNER, INNER)
        total = jnp.zeros((2 * rows, INNER * depth), jnp.float32)
        for s in range(n_packs):
            cols = pl.ds(pl.multiple_of((where_ref[0] ^ s) * width, 128), width)
            total += nt_dot(attended[s], held[block, :, cols].reshape(INNER * depth, width))
        outs[2 * i][...] = total[:rows].astype(outs[2 * i].dtype)
        outs[2 * i + 1][...] = total[rows:].astype(outs[2 * i + 1].dtype)


def project(where, packs, pieces, n_shares):
    rows, width = packs[0].shape[0] // 2, packs[0].shape[1] // 2
    depth, local_width = pieces[0].shape
    block = INNER * depth
    whole = lambda i, w: (0, 0)
    types = [jnp.float32] + [jnp.bfloat16] * (2 * n_shares - 1)
    return pl.pallas_call(
        functools.partial(project_kernel, len(packs), len(pieces), n_shares),
        grid_spec=pltpu.PrefetchScalarGridSpec(
            num_scalar_prefetch=1,
            grid=(1,),
            in_specs=[pl.BlockSpec((2 * rows, width), whole)] * len(packs)
            + [pl.BlockSpec(memory_space=pl.ANY)] * len(pieces),
            out_specs=[pl.BlockSpec((rows, block), whole)] * len(types),
            scratch_shapes=[
                pltpu.VMEM((len(pieces), depth, local_width), jnp.bfloat16),
                pltpu.SemaphoreType.DMA((len(pieces),)),
            ],
        ),
        out_shape=[jax.ShapeDtypeStruct((rows, block), t) for t in types],
        compiler_params=pltpu.CompilerParams(vmem_limit_bytes=VMEM_BYTES),
        cost_estimate=pl.CostEstimate(
            flops=4 * rows * block * n_shares * local_width,
            bytes_accessed=2 * block * n_shares * local_width,
            transcendentals=0,
        ),
    )(where, *packs, *pieces)


def on_device(
    image,
    mod_shift,
    mod_scale,
    mod_gate,
    w_query,
    w_key,
    w_value,
    query_gain,
    key_gain,
    text_keys,
    text_values,
    stale_keys,
    stale_values,
    w_out,
):
    head_size = query_gain.shape[0]
    rows, model_width = image.shape
    depth, local_width = w_query.shape
    heads = local_width // head_size
    patches = lax.axis_size("patch")
    fsdp = lax.axis_size("fsdp")
    outer = patches // INNER
    team = math.gcd(outer, heads)
    width = local_width // team
    assert outer == 2 * fsdp and team > 1 and team & (team - 1) == 0 and outer & (outer - 1) == 0
    me = lax.axis_index("patch")
    mine = lax.axis_index("fsdp")
    place, seat = me // INNER, me % INNER
    member, parity = place % team, place % 2
    def over_outer(x, pairs):
        pairs = [(a * INNER + k, b * INNER + k) for a, b in pairs for k in range(INNER)]
        return lax.ppermute(x, "patch", pairs)

    def to_partner(x, bits):
        return over_outer(x, [(z, z ^ bits) for z in range(outer)])

    def flip(x, bits):
        return lax.ppermute(x, "patch", [(p, p ^ bits) for p in range(patches)])

    def along_fsdp(x, step):
        return lax.ppermute(x, "fsdp", [(i, (i + step) % fsdp) for i in range(fsdp)])

    def along_both(x, bits, step):
        pairs = [
            (p * fsdp + f, (p ^ (bits * INNER)) * fsdp + (f + step) % fsdp)
            for p in range(patches)
            for f in range(fsdp)
        ]
        return lax.ppermute(x, ("patch", "fsdp"), pairs)

    def spread(piece, side, *deps):
        return [piece, side, flip(after(piece, *deps), 1), flip(after(side, *deps), 1)]

    def shares_of(got):
        return [got] + [along_fsdp(got, i) for i in range(1, fsdp)]

    def seats_of(position):
        return [position * INNER + (seat ^ bits) for bits in (0, 2, 1, 3)]

    modded = modulate(image, mod_shift, mod_scale)
    share = rows // fsdp
    part = lax.dynamic_slice_in_dim(modded, mine * share, share, axis=0)
    dealt = deal(member, (w_query, w_key, w_value, stale_keys, stale_values), team)
    pieces, sides = {0: dealt[0]}, {}
    row_shares = {}
    if outer == 4 and team == 4:
        ends = [(1, 0), (2, 3)]
        middle = [(1, 2), (2, 1)]
        inside = jnp.logical_or(place == 1, place == 2)
        near = to_partner(part, 1)
        across = over_outer(part, middle)
        sides[0] = flip(pieces[0], 2)
        far = over_outer(near, middle)
        pieces[2] = to_partner(after(dealt[2], near, across), 2)
        pieces[1] = to_partner(after(dealt[1], near, across), 1)
        row_shares[1] = shares_of(after(near, sides[0]))
        end_across = over_outer(after(across, pieces[1]), ends)
        end_far = over_outer(after(far, row_shares[1][-1]), ends)
        sides[1] = flip(after(pieces[1], far), 2)
        pieces[3] = to_partner(after(dealt[3], far, pieces[2]), 3)
        row_shares[2] = shares_of(jnp.where(inside, far, end_across))
        row_shares[3] = shares_of(jnp.where(inside, across, end_far))
        sides[2] = flip(after(pieces[2], end_far, sides[1]), 2)
        late = [sides[2], row_shares[2][-1]]
        later = [row_shares[3][-1]]
    else:
        for k in range(1, team):
            row_shares[k] = shares_of(to_partner(part, k))
        for k in range(1, outer):
            pieces[k] = to_partner(dealt[k % team], k)
        late = later = []
    for k in range(outer):
        if k not in sides:
            sides[k] = flip(pieces[k], 2)
    out_piece = after(w_out.T, sides[outer - 1])
    out_pieces = [out_piece] + [to_partner(out_piece, 2 * k) for k in range(1, fsdp)]

    origins = [o for k in range(outer) for o in seats_of(place ^ k)]
    deps = lambda k: late if k < 2 else later
    pieces = [x for k in range(outer) for x in spread(pieces[k], sides[k], *deps(k))]
    patch_rows = [[modded]] + [row_shares[k] for k in range(1, team)]
    where = [member] + origins
    for k in range(team):
        where.append((place ^ k) * INNER + seat)
        where += [((mine + (fsdp - i)) % fsdp) * share for i in range(fsdp)] if k else [0 * mine]
    messages = attend_patches(
        jnp.stack(where).astype(jnp.int32),
        patch_rows,
        text_keys,
        text_values,
        query_gain,
        key_gain,
        pieces,
        depth,
    )

    def give(x, bits):
        return lax.ppermute(x, "patch", [(p, p ^ (bits * INNER)) for p in range(patches)])

    packs = [messages[0]] + [give(messages[k], k) for k in range(1, team)]
    out_sides = [flip(out_pieces[0], 2)]
    out_sides += [flip(after(piece, messages[0]), 2) for piece in out_pieces[1:]]
    out_pieces = [x for p, q in zip(out_pieces, out_sides) for x in spread(p, q, *packs[1:])]
    out_places = [o for k in range(fsdp) for o in seats_of((place ^ (2 * k)) // 2)]
    where = [member, parity] + [(mine + i) % fsdp for i in range(fsdp)] + out_places
    where = jnp.stack(where).astype(jnp.int32)
    partial = project(where, packs, out_pieces, fsdp)
    own, partner = partial[0], [along_both(partial[1], 1, 0)]
    for i in range(1, fsdp):
        own = own + along_fsdp(partial[2 * i], i).astype(jnp.float32)
        partner.append(along_both(partial[2 * i + 1], 1, i))
    other = sum(x.astype(jnp.float32) for x in partner)
    summed = jnp.where(
        parity == 0,
        jnp.concatenate([own, other], axis=1),
        jnp.concatenate([other, own], axis=1),
    )
    key_out, value_out = collect(member, [after(packs[0], partial[0])] + packs[1:])

    out_share = model_width // fsdp
    col_start = mine * out_share
    image_part = lax.dynamic_slice_in_dim(image, col_start, out_share, 1).astype(jnp.float32)
    gate_part = lax.dynamic_slice_in_dim(mod_gate, col_start, out_share, 0)
    hidden = (image_part + gate_part * summed).astype(jnp.bfloat16)
    return (hidden, key_out, value_out)


def solution(mesh):
    return jax.shard_map(
        on_device,
        mesh=mesh,
        in_specs=(
            P("patch", None),
            P(),
            P(),
            P(),
            P("patch", "fsdp"),
            P("patch", "fsdp"),
            P("patch", "fsdp"),
            P(),
            P(),
            P(None, "fsdp"),
            P(None, "fsdp"),
            P("patch", "fsdp"),
            P("patch", "fsdp"),
            P("fsdp", "patch"),
        ),
        out_specs=(P("patch", "fsdp"), P("patch", "fsdp"), P("patch", "fsdp")),
        check_vma=False,
    )
```

```python
import functools
import math

import jax
import jax.numpy as jnp
from jax import lax
from jax.experimental import pallas as pl
from jax.experimental.pallas import tpu as pltpu
from jax.sharding import PartitionSpec as P

INNER = 4
VMEM_BYTES = 60 * 1024 * 1024


def modulate(image, mod_shift, mod_scale):
    values = image.astype(jnp.float32)
    center = jnp.mean(values, axis=-1, keepdims=True)
    spread = jnp.mean(jnp.square(values - center), axis=-1, keepdims=True)
    normed = (values - center) * lax.rsqrt(spread + 1e-06)
    return ((1.0 + mod_scale) * normed + mod_shift).astype(jnp.bfloat16)


def after(x, *deps):
    return lax.optimization_barrier((x,) + deps)[0]


def nt_dot(a, b):
    return lax.dot_general(a, b, (((1,), (1,)), ((), ())), preferred_element_type=jnp.float32)


def norm_heads(x, gain):
    power = jnp.mean(x * x, axis=-1, keepdims=True)
    return (x * lax.rsqrt(power + 1e-06) * gain).astype(jnp.bfloat16)


def patch_kernel(depth, n_pieces, cuts, where_ref, *refs):
    n_patches = len(cuts)
    tk_ref, tv_ref, qg_ref, kg_ref = refs[:4]
    n_rows = 1 + max(i for cut in cuts for i, _, _ in cut)
    arrays, refs = refs[4 : 4 + n_rows], refs[4 + n_rows :]
    pieces, refs = refs[:n_pieces], refs[n_pieces:]
    outs, (x_ref, held, scores, expos, x_sem, w_sem) = refs[:n_patches], refs[n_patches:]
    rows, width = outs[0].shape[0] // 2, outs[0].shape[1] // 2
    head_size = qg_ref.shape[1]
    groups = [slice(g * rows, (g + 1) * rows) for g in range(n_patches)]
    owns, x_copies, at = [], [], 1 + n_pieces
    for g, cut in enumerate(cuts):
        owns.append(where_ref[at])
        for i, (array, start, length) in enumerate(cut):
            first = pl.multiple_of(g * rows + where_ref[at + 1 + i], 16)
            x_copies.append(
                pltpu.make_async_copy(
                    arrays[array].at[pl.ds(start, length)],
                    x_ref.at[pl.ds(first, length)],
                    x_sem.at[len(x_copies)],
                )
            )
        at += 1 + len(cut)
    w_copies = [
        pltpu.make_async_copy(piece, held.at[where_ref[1 + i]], w_sem.at[i])
        for i, piece in enumerate(pieces)
    ]
    for copy in x_copies + w_copies[:INNER]:
        copy.start()
    for copy in x_copies:
        copy.wait()
    for copy in w_copies[INNER:]:
        copy.start()

    chunk = INNER * depth
    proj = [jnp.zeros((n_patches * rows, width), jnp.float32) for _ in range(3)]
    if chunk % 128 == 0:
        for first in range(0, n_pieces, INNER):
            for copy in w_copies[first : first + INNER]:
                copy.wait()
            place = where_ref[1 + first] // INNER
            part = x_ref[:, pl.ds(pl.multiple_of(place * chunk, 128), chunk)]
            for i in range(3):
                weight = held[pl.ds(place * INNER, INNER), i * depth : (i + 1) * depth, :]
                proj[i] += jnp.dot(
                    part, weight.reshape(chunk, width), preferred_element_type=jnp.float32
                )
    else:
        for copy in w_copies:
            copy.wait()
        for i in range(3):
            weight = held[:, i * depth : (i + 1) * depth, :]
            proj[i] += jnp.dot(
                x_ref[...],
                weight.reshape(n_pieces * depth, width),
                preferred_element_type=jnp.float32,
            )
    q_proj, k_proj, v_proj = proj

    v_new = v_proj.astype(jnp.bfloat16)
    k0, v0 = 3 * depth, 3 * depth + rows
    scale = math.log2(math.e) / math.sqrt(head_size)
    own_cols = [pl.ds(pl.multiple_of(own * rows, 128), rows) for own in owns]
    for h in range(width // head_size):
        cols = slice(h * head_size, (h + 1) * head_size)
        beside = slice(width + cols.start, width + cols.stop)
        query = norm_heads(q_proj[:, cols], qg_ref[...])
        key = norm_heads(k_proj[:, cols], kg_ref[...])
        value = v_new[:, cols]
        keys = held[:, k0 : k0 + rows, cols].reshape(n_pieces * rows, head_size)
        values = held[:, v0 : v0 + rows, cols].reshape(n_pieces * rows, head_size)
        scores[h] = nt_dot(query, keys)
        for g, group in enumerate(groups):
            scores[h, group, own_cols[g]] = nt_dot(query[group], key[group])
            outs[g][:rows, beside] = key[group]
            outs[g][rows:, beside] = value[group]
        text_s = nt_dot(query, tk_ref[:, cols])
        image_s = scores[h]
        largest = jnp.maximum(
            jnp.max(text_s, axis=-1, keepdims=True), jnp.max(image_s, axis=-1, keepdims=True)
        )
        text_e = jnp.exp2((text_s - largest) * scale)
        image_e = jnp.exp2((image_s - largest) * scale)
        total = jnp.sum(text_e, axis=-1, keepdims=True) + jnp.sum(image_e, axis=-1, keepdims=True)
        expos[h] = image_e.astype(jnp.bfloat16)
        fresh_mix = []
        for g, group in enumerate(groups):
            fresh_mix.append(
                jnp.dot(
                    expos[h, group, own_cols[g]], value[group], preferred_element_type=jnp.float32
                )
            )
            expos[h, group, own_cols[g]] = jnp.zeros((rows, rows), jnp.bfloat16)
        mixture = (
            jnp.dot(text_e.astype(jnp.bfloat16), tv_ref[:, cols], preferred_element_type=jnp.float32)
            + jnp.dot(expos[h], values, preferred_element_type=jnp.float32)
            + jnp.concatenate(fresh_mix, axis=0)
        )
        attended = (mixture / total).astype(jnp.bfloat16)
        for g, group in enumerate(groups):
            first = pl.multiple_of(lax.rem(owns[g] // INNER, 2) * rows, 16)
            for out in outs[g // 2 * 2 : g // 2 * 2 + 2]:
                out[pl.ds(first, rows), cols] = attended[group]


def attend_patches(where, patches, text_keys, text_values, query_gain, key_gain, pieces, depth):
    arrays, cuts, (rows, model_width), width = [], [], patches[0][0].shape, pieces[0].shape[1]
    for patch in patches:
        cuts.append([])
        for x in patch:
            x, start = x if isinstance(x, tuple) else (x, 0)
            held = [i for i, y in enumerate(arrays) if y is x]
            if not held:
                arrays.append(x)
            place = held[0] if held else len(arrays) - 1
            cuts[-1].append((place, start, rows // len(patch)))
    n, n_pieces, texts, head_size = len(patches), len(pieces), text_keys.shape[0], query_gain.shape[0]
    heads, n_keys = width // head_size, n_pieces * rows
    whole = lambda i, w: (0, 0)
    return pl.pallas_call(
        functools.partial(patch_kernel, depth, n_pieces, cuts),
        grid_spec=pltpu.PrefetchScalarGridSpec(
            num_scalar_prefetch=1,
            grid=(1,),
            in_specs=[pl.BlockSpec((texts, width), lambda i, w: (0, w[0]))] * 2
            + [pl.BlockSpec((1, head_size), whole)] * 2
            + [pl.BlockSpec(memory_space=pl.ANY)] * (len(arrays) + n_pieces),
            out_specs=[pl.BlockSpec((2 * rows, 2 * width), whole)] * n,
            scratch_shapes=[
                pltpu.VMEM((n * rows, model_width), jnp.bfloat16),
                pltpu.VMEM((n_pieces,) + pieces[0].shape, jnp.bfloat16),
                pltpu.VMEM((heads, n * rows, n_keys), jnp.float32),
                pltpu.VMEM((heads, n * rows, n_keys), jnp.bfloat16),
                pltpu.SemaphoreType.DMA((sum(len(cut) for cut in cuts),)),
                pltpu.SemaphoreType.DMA((n_pieces,)),
            ],
        ),
        out_shape=[jax.ShapeDtypeStruct((2 * rows, 2 * width), jnp.bfloat16)] * n,
        compiler_params=pltpu.CompilerParams(vmem_limit_bytes=VMEM_BYTES),
        cost_estimate=pl.CostEstimate(
            flops=2 * n * rows * (model_width * 3 * width + 2 * (texts + n_keys) * width),
            bytes_accessed=2 * n_pieces * pieces[0].size,
            transcendentals=n * rows * (texts + n_keys) * heads,
        ),
    )(
        where,
        text_keys,
        text_values,
        query_gain.reshape(1, -1),
        key_gain.reshape(1, -1),
        *arrays,
        *pieces,
    )


def deal_kernel(n_arrays, team, member_ref, *refs):
    arrays, outs = refs[:n_arrays], refs[n_arrays:]
    width = outs[0].shape[1]
    for k in range(team):
        at = member_ref[0] ^ k
        cols = pl.ds(pl.multiple_of(at * width, 128), width)
        first = 0
        for x in arrays:
            rows = x.shape[0]
            outs[k][first : first + rows, :] = x[:, cols]
            first += rows


def deal(member, arrays, team):
    width = arrays[0].shape[1] // team
    shape = jax.ShapeDtypeStruct((sum(x.shape[0] for x in arrays), width), jnp.bfloat16)
    return pl.pallas_call(
        functools.partial(deal_kernel, len(arrays), team),
        in_specs=[pl.BlockSpec(memory_space=pltpu.SMEM)]
        + [pl.BlockSpec(memory_space=pltpu.VMEM)] * len(arrays),
        out_specs=[pl.BlockSpec(memory_space=pltpu.VMEM)] * team,
        out_shape=[shape] * team,
        compiler_params=pltpu.CompilerParams(vmem_limit_bytes=VMEM_BYTES),
    )(member.reshape(1), *arrays)


def collect_kernel(team, member_ref, *refs):
    packs, (key_ref, value_ref) = refs[:team], refs[team:]
    rows, width = key_ref.shape[0], key_ref.shape[1] // team
    for s in range(team):
        at = member_ref[0] ^ s
        cols = pl.ds(pl.multiple_of(at * width, 128), width)
        key_ref[:, cols] = packs[s][:rows, width:]
        value_ref[:, cols] = packs[s][rows:, width:]


def collect(member, packs):
    team = len(packs)
    rows, width = packs[0].shape[0] // 2, packs[0].shape[1] // 2
    shape = jax.ShapeDtypeStruct((rows, width * team), jnp.bfloat16)
    return pl.pallas_call(
        functools.partial(collect_kernel, team),
        in_specs=[pl.BlockSpec(memory_space=pltpu.SMEM)]
        + [pl.BlockSpec(memory_space=pltpu.VMEM)] * team,
        out_specs=[pl.BlockSpec(memory_space=pltpu.VMEM)] * 2,
        out_shape=[shape, shape],
        compiler_params=pltpu.CompilerParams(vmem_limit_bytes=VMEM_BYTES),
    )(member.reshape(1), *packs)


def project_kernel(n_packs, n_pieces, n_shares, where_ref, *refs):
    packs, pieces = refs[:n_packs], refs[n_packs : n_packs + n_pieces]
    refs = refs[n_packs + n_pieces :]
    outs, held, sems = refs[:-2], refs[-2], refs[-1]
    rows, width = packs[0].shape[0] // 2, packs[0].shape[1]
    depth = held.shape[1]
    copies = [
        pltpu.make_async_copy(piece, held.at[where_ref[2 + n_shares + i]], sems.at[i])
        for i, piece in enumerate(pieces)
    ]
    for copy in copies:
        copy.start()
    own = pl.multiple_of(where_ref[1] * rows, 16)
    other = pl.multiple_of((1 - where_ref[1]) * rows, 16)
    attended = [
        jnp.concatenate([x[pl.ds(own, rows), :], x[pl.ds(other, rows), :]], axis=0) for x in packs
    ]
    for copy in copies:
        copy.wait()
    for i in reversed(range(n_shares)):
        block = pl.ds(where_ref[2 + i] * INNER, INNER)
        total = jnp.zeros((2 * rows, INNER * depth), jnp.float32)
        for s in range(n_packs):
            cols = pl.ds(pl.multiple_of((where_ref[0] ^ s) * width, 128), width)
            total += nt_dot(attended[s], held[block, :, cols].reshape(INNER * depth, width))
        outs[2 * i][...] = total[:rows].astype(outs[2 * i].dtype)
        outs[2 * i + 1][...] = total[rows:].astype(outs[2 * i + 1].dtype)


def project(where, packs, pieces, n_shares):
    rows, width = packs[0].shape[0] // 2, packs[0].shape[1] // 2
    depth, local_width = pieces[0].shape
    block = INNER * depth
    whole = lambda i, w: (0, 0)
    types = [jnp.float32] + [jnp.bfloat16] * (2 * n_shares - 1)
    return pl.pallas_call(
        functools.partial(project_kernel, len(packs), len(pieces), n_shares),
        grid_spec=pltpu.PrefetchScalarGridSpec(
            num_scalar_prefetch=1,
            grid=(1,),
            in_specs=[pl.BlockSpec((2 * rows, width), whole)] * len(packs)
            + [pl.BlockSpec(memory_space=pl.ANY)] * len(pieces),
            out_specs=[pl.BlockSpec((rows, block), whole)] * len(types),
            scratch_shapes=[
                pltpu.VMEM((len(pieces), depth, local_width), jnp.bfloat16),
                pltpu.SemaphoreType.DMA((len(pieces),)),
            ],
        ),
        out_shape=[jax.ShapeDtypeStruct((rows, block), t) for t in types],
        compiler_params=pltpu.CompilerParams(vmem_limit_bytes=VMEM_BYTES),
        cost_estimate=pl.CostEstimate(
            flops=4 * rows * block * n_shares * local_width,
            bytes_accessed=2 * block * n_shares * local_width,
            transcendentals=0,
        ),
    )(where, *packs, *pieces)


def on_device(
    image,
    mod_shift,
    mod_scale,
    mod_gate,
    w_query,
    w_key,
    w_value,
    query_gain,
    key_gain,
    text_keys,
    text_values,
    stale_keys,
    stale_values,
    w_out,
):
    head_size = query_gain.shape[0]
    rows, model_width = image.shape
    depth, local_width = w_query.shape
    heads = local_width // head_size
    patches = lax.axis_size("patch")
    fsdp = lax.axis_size("fsdp")
    outer = patches // INNER
    team = math.gcd(outer, heads)
    width = local_width // team
    assert outer == 2 * fsdp and team > 1 and team & (team - 1) == 0 and outer & (outer - 1) == 0
    me = lax.axis_index("patch")
    mine = lax.axis_index("fsdp")
    place, seat = me // INNER, me % INNER
    member, parity = place % team, place % 2
    def over_outer(x, pairs):
        pairs = [(a * INNER + k, b * INNER + k) for a, b in pairs for k in range(INNER)]
        return lax.ppermute(x, "patch", pairs)

    def to_partner(x, bits):
        return over_outer(x, [(z, z ^ bits) for z in range(outer)])

    def flip(x, bits):
        return lax.ppermute(x, "patch", [(p, p ^ bits) for p in range(patches)])

    def along_fsdp(x, step):
        return lax.ppermute(x, "fsdp", [(i, (i + step) % fsdp) for i in range(fsdp)])

    def along_both(x, bits, step):
        pairs = [
            (p * fsdp + f, (p ^ (bits * INNER)) * fsdp + (f + step) % fsdp)
            for p in range(patches)
            for f in range(fsdp)
        ]
        return lax.ppermute(x, ("patch", "fsdp"), pairs)

    def spread(piece, side, *deps):
        return [piece, side, flip(after(piece, *deps), 1), flip(after(side, *deps), 1)]

    def shares_of(got):
        return [got] + [along_fsdp(got, i) for i in range(1, fsdp)]

    def seats_of(position):
        return [position * INNER + (seat ^ bits) for bits in (0, 2, 1, 3)]

    modded = modulate(image, mod_shift, mod_scale)
    share = rows // fsdp
    part = lax.dynamic_slice_in_dim(modded, mine * share, share, axis=0)
    dealt = deal(member, (w_query, w_key, w_value, stale_keys, stale_values), team)
    pieces, sides = {0: dealt[0]}, {}
    row_shares = {}
    if outer == 4 and team == 4:
        ends = [(1, 0), (2, 3)]
        middle = [(1, 2), (2, 1)]
        inside = jnp.logical_or(place == 1, place == 2)
        near = to_partner(part, 1)
        across = over_outer(part, middle)
        sides[0] = flip(pieces[0], 2)
        far = over_outer(near, middle)
        pieces[2] = to_partner(after(dealt[2], near, across), 2)
        pieces[1] = to_partner(after(dealt[1], near, across), 1)
        row_shares[1] = shares_of(after(near, sides[0]))
        end_across = over_outer(after(across, pieces[1]), ends)
        end_far = over_outer(after(far, row_shares[1][-1]), ends)
        sides[1] = flip(after(pieces[1], far), 2)
        pieces[3] = to_partner(after(dealt[3], far, pieces[2]), 3)
        row_shares[2] = shares_of(jnp.where(inside, far, end_across))
        row_shares[3] = shares_of(after(jnp.where(inside, across, end_far), row_shares[2][-1]))
        sides[2] = flip(pieces[2], 2)
        late = [sides[2], row_shares[2][-1]]
        later = [row_shares[3][-1]]
    else:
        for k in range(1, team):
            row_shares[k] = shares_of(to_partner(part, k))
        for k in range(1, outer):
            pieces[k] = to_partner(dealt[k % team], k)
        late = later = []
    for k in range(outer):
        if k not in sides:
            sides[k] = flip(pieces[k], 2)
    out_piece = after(w_out.T, sides[outer - 1])
    out_pieces = [out_piece] + [to_partner(out_piece, 2 * k) for k in range(1, fsdp)]

    origins = [o for k in range(outer) for o in seats_of(place ^ k)]
    deps = lambda k: late if k < 2 else later
    pieces = [x for k in range(outer) for x in spread(pieces[k], sides[k], *deps(k))]
    patch_rows = [[modded]] + [row_shares[k] for k in range(1, team)]
    where = [member] + origins
    for k in range(team):
        where.append((place ^ k) * INNER + seat)
        where += [((mine + (fsdp - i)) % fsdp) * share for i in range(fsdp)] if k else [0 * mine]
    messages = attend_patches(
        jnp.stack(where).astype(jnp.int32),
        patch_rows,
        text_keys,
        text_values,
        query_gain,
        key_gain,
        pieces,
        depth,
    )

    def give(x, bits):
        return lax.ppermute(x, "patch", [(p, p ^ (bits * INNER)) for p in range(patches)])

    packs = [messages[0]] + [give(messages[k], k) for k in range(1, team)]
    out_sides = [flip(out_pieces[0], 2)]
    out_sides += [flip(after(piece, messages[0]), 2) for piece in out_pieces[1:]]
    out_pieces = [x for p, q in zip(out_pieces, out_sides) for x in spread(p, q, *packs[1:])]
    out_places = [o for k in range(fsdp) for o in seats_of((place ^ (2 * k)) // 2)]
    where = [member, parity] + [(mine + i) % fsdp for i in range(fsdp)] + out_places
    where = jnp.stack(where).astype(jnp.int32)
    partial = project(where, packs, out_pieces, fsdp)
    own, partner = partial[0], [along_both(partial[1], 1, 0)]
    for i in range(1, fsdp):
        own = own + along_fsdp(partial[2 * i], i).astype(jnp.float32)
        partner.append(along_both(partial[2 * i + 1], 1, i))
    other = sum(x.astype(jnp.float32) for x in partner)
    summed = jnp.where(
        parity == 0,
        jnp.concatenate([own, other], axis=1),
        jnp.concatenate([other, own], axis=1),
    )
    key_out, value_out = collect(member, [after(packs[0], partial[0])] + packs[1:])

    out_share = model_width // fsdp
    col_start = mine * out_share
    image_part = lax.dynamic_slice_in_dim(image, col_start, out_share, 1).astype(jnp.float32)
    gate_part = lax.dynamic_slice_in_dim(mod_gate, col_start, out_share, 0)
    hidden = (image_part + gate_part * summed).astype(jnp.bfloat16)
    return (hidden, key_out, value_out)


def solution(mesh):
    return jax.shard_map(
        on_device,
        mesh=mesh,
        in_specs=(
            P("patch", None),
            P(),
            P(),
            P(),
            P("patch", "fsdp"),
            P("patch", "fsdp"),
            P("patch", "fsdp"),
            P(),
            P(),
            P(None, "fsdp"),
            P(None, "fsdp"),
            P("patch", "fsdp"),
            P("patch", "fsdp"),
            P("fsdp", "patch"),
        ),
        out_specs=(P("patch", "fsdp"), P("patch", "fsdp"), P("patch", "fsdp")),
        check_vma=False,
    )
```

```python
import functools
import math

import jax
import jax.numpy as jnp
from jax import lax
from jax.experimental import pallas as pl
from jax.experimental.pallas import tpu as pltpu
from jax.sharding import PartitionSpec as P

INNER = 4
VMEM_BYTES = 60 * 1024 * 1024


def modulate(image, mod_shift, mod_scale):
    values = image.astype(jnp.float32)
    center = jnp.mean(values, axis=-1, keepdims=True)
    spread = jnp.mean(jnp.square(values - center), axis=-1, keepdims=True)
    normed = (values - center) * lax.rsqrt(spread + 1e-06)
    return ((1.0 + mod_scale) * normed + mod_shift).astype(jnp.bfloat16)


def after(x, *deps):
    return lax.optimization_barrier((x,) + deps)[0]


def nt_dot(a, b):
    return lax.dot_general(a, b, (((1,), (1,)), ((), ())), preferred_element_type=jnp.float32)


def norm_heads(x, gain):
    power = jnp.mean(x * x, axis=-1, keepdims=True)
    return (x * lax.rsqrt(power + 1e-06) * gain).astype(jnp.bfloat16)


def patch_kernel(depth, n_pieces, cuts, where_ref, *refs):
    n_patches = len(cuts)
    tk_ref, tv_ref, qg_ref, kg_ref = refs[:4]
    n_rows = 1 + max(i for cut in cuts for i, _, _ in cut)
    arrays, refs = refs[4 : 4 + n_rows], refs[4 + n_rows :]
    pieces, refs = refs[:n_pieces], refs[n_pieces:]
    outs, (x_ref, held, scores, expos, x_sem, w_sem) = refs[:n_patches], refs[n_patches:]
    rows, width = outs[0].shape[0] // 2, outs[0].shape[1] // 2
    head_size = qg_ref.shape[1]
    groups = [slice(g * rows, (g + 1) * rows) for g in range(n_patches)]
    owns, x_copies, at = [], [], 1 + n_pieces
    for g, cut in enumerate(cuts):
        owns.append(where_ref[at])
        for i, (array, start, length) in enumerate(cut):
            first = pl.multiple_of(g * rows + where_ref[at + 1 + i], 16)
            x_copies.append(
                pltpu.make_async_copy(
                    arrays[array].at[pl.ds(start, length)],
                    x_ref.at[pl.ds(first, length)],
                    x_sem.at[len(x_copies)],
                )
            )
        at += 1 + len(cut)
    w_copies = [
        pltpu.make_async_copy(piece, held.at[where_ref[1 + i]], w_sem.at[i])
        for i, piece in enumerate(pieces)
    ]
    for copy in x_copies + w_copies[:INNER]:
        copy.start()
    for copy in x_copies:
        copy.wait()
    for copy in w_copies[INNER:]:
        copy.start()

    chunk = INNER * depth
    proj = [jnp.zeros((n_patches * rows, width), jnp.float32) for _ in range(3)]
    if chunk % 128 == 0:
        for first in range(0, n_pieces, INNER):
            for copy in w_copies[first : first + INNER]:
                copy.wait()
            place = where_ref[1 + first] // INNER
            part = x_ref[:, pl.ds(pl.multiple_of(place * chunk, 128), chunk)]
            for i in range(3):
                weight = held[pl.ds(place * INNER, INNER), i * depth : (i + 1) * depth, :]
                proj[i] += jnp.dot(
                    part, weight.reshape(chunk, width), preferred_element_type=jnp.float32
                )
    else:
        for copy in w_copies:
            copy.wait()
        for i in range(3):
            weight = held[:, i * depth : (i + 1) * depth, :]
            proj[i] += jnp.dot(
                x_ref[...],
                weight.reshape(n_pieces * depth, width),
                preferred_element_type=jnp.float32,
            )
    q_proj, k_proj, v_proj = proj

    v_new = v_proj.astype(jnp.bfloat16)
    k0, v0 = 3 * depth, 3 * depth + rows
    scale = math.log2(math.e) / math.sqrt(head_size)
    own_cols = [pl.ds(pl.multiple_of(own * rows, 128), rows) for own in owns]
    for h in range(width // head_size):
        cols = slice(h * head_size, (h + 1) * head_size)
        beside = slice(width + cols.start, width + cols.stop)
        query = norm_heads(q_proj[:, cols], qg_ref[...])
        key = norm_heads(k_proj[:, cols], kg_ref[...])
        value = v_new[:, cols]
        keys = held[:, k0 : k0 + rows, cols].reshape(n_pieces * rows, head_size)
        values = held[:, v0 : v0 + rows, cols].reshape(n_pieces * rows, head_size)
        scores[h] = nt_dot(query, keys)
        for g, group in enumerate(groups):
            scores[h, group, own_cols[g]] = nt_dot(query[group], key[group])
            outs[g][:rows, beside] = key[group]
            outs[g][rows:, beside] = value[group]
        text_s = nt_dot(query, tk_ref[:, cols])
        image_s = scores[h]
        largest = jnp.maximum(
            jnp.max(text_s, axis=-1, keepdims=True), jnp.max(image_s, axis=-1, keepdims=True)
        )
        text_e = jnp.exp2((text_s - largest) * scale)
        image_e = jnp.exp2((image_s - largest) * scale)
        total = jnp.sum(text_e, axis=-1, keepdims=True) + jnp.sum(image_e, axis=-1, keepdims=True)
        expos[h] = image_e.astype(jnp.bfloat16)
        fresh_mix = []
        for g, group in enumerate(groups):
            fresh_mix.append(
                jnp.dot(
                    expos[h, group, own_cols[g]], value[group], preferred_element_type=jnp.float32
                )
            )
            expos[h, group, own_cols[g]] = jnp.zeros((rows, rows), jnp.bfloat16)
        mixture = (
            jnp.dot(text_e.astype(jnp.bfloat16), tv_ref[:, cols], preferred_element_type=jnp.float32)
            + jnp.dot(expos[h], values, preferred_element_type=jnp.float32)
            + jnp.concatenate(fresh_mix, axis=0)
        )
        attended = (mixture / total).astype(jnp.bfloat16)
        for g, group in enumerate(groups):
            first = pl.multiple_of(lax.rem(owns[g] // INNER, 2) * rows, 16)
            for out in outs[g // 2 * 2 : g // 2 * 2 + 2]:
                out[pl.ds(first, rows), cols] = attended[group]


def attend_patches(where, patches, text_keys, text_values, query_gain, key_gain, pieces, depth):
    arrays, cuts, (rows, model_width), width = [], [], patches[0][0].shape, pieces[0].shape[1]
    for patch in patches:
        cuts.append([])
        for x in patch:
            x, start = x if isinstance(x, tuple) else (x, 0)
            held = [i for i, y in enumerate(arrays) if y is x]
            if not held:
                arrays.append(x)
            place = held[0] if held else len(arrays) - 1
            cuts[-1].append((place, start, rows // len(patch)))
    n, n_pieces, texts, head_size = len(patches), len(pieces), text_keys.shape[0], query_gain.shape[0]
    heads, n_keys = width // head_size, n_pieces * rows
    whole = lambda i, w: (0, 0)
    return pl.pallas_call(
        functools.partial(patch_kernel, depth, n_pieces, cuts),
        grid_spec=pltpu.PrefetchScalarGridSpec(
            num_scalar_prefetch=1,
            grid=(1,),
            in_specs=[pl.BlockSpec((texts, width), lambda i, w: (0, w[0]))] * 2
            + [pl.BlockSpec((1, head_size), whole)] * 2
            + [pl.BlockSpec(memory_space=pl.ANY)] * (len(arrays) + n_pieces),
            out_specs=[pl.BlockSpec((2 * rows, 2 * width), whole)] * n,
            scratch_shapes=[
                pltpu.VMEM((n * rows, model_width), jnp.bfloat16),
                pltpu.VMEM((n_pieces,) + pieces[0].shape, jnp.bfloat16),
                pltpu.VMEM((heads, n * rows, n_keys), jnp.float32),
                pltpu.VMEM((heads, n * rows, n_keys), jnp.bfloat16),
                pltpu.SemaphoreType.DMA((sum(len(cut) for cut in cuts),)),
                pltpu.SemaphoreType.DMA((n_pieces,)),
            ],
        ),
        out_shape=[jax.ShapeDtypeStruct((2 * rows, 2 * width), jnp.bfloat16)] * n,
        compiler_params=pltpu.CompilerParams(vmem_limit_bytes=VMEM_BYTES),
        cost_estimate=pl.CostEstimate(
            flops=2 * n * rows * (model_width * 3 * width + 2 * (texts + n_keys) * width),
            bytes_accessed=2 * n_pieces * pieces[0].size,
            transcendentals=n * rows * (texts + n_keys) * heads,
        ),
    )(
        where,
        text_keys,
        text_values,
        query_gain.reshape(1, -1),
        key_gain.reshape(1, -1),
        *arrays,
        *pieces,
    )


def deal_kernel(n_arrays, team, member_ref, *refs):
    arrays, outs = refs[:n_arrays], refs[n_arrays:]
    width = outs[0].shape[1]
    for k in range(team):
        at = member_ref[0] ^ k
        cols = pl.ds(pl.multiple_of(at * width, 128), width)
        first = 0
        for x in arrays:
            rows = x.shape[0]
            outs[k][first : first + rows, :] = x[:, cols]
            first += rows


def deal(member, arrays, team):
    width = arrays[0].shape[1] // team
    shape = jax.ShapeDtypeStruct((sum(x.shape[0] for x in arrays), width), jnp.bfloat16)
    return pl.pallas_call(
        functools.partial(deal_kernel, len(arrays), team),
        in_specs=[pl.BlockSpec(memory_space=pltpu.SMEM)]
        + [pl.BlockSpec(memory_space=pltpu.VMEM)] * len(arrays),
        out_specs=[pl.BlockSpec(memory_space=pltpu.VMEM)] * team,
        out_shape=[shape] * team,
        compiler_params=pltpu.CompilerParams(vmem_limit_bytes=VMEM_BYTES),
    )(member.reshape(1), *arrays)


def collect_kernel(team, member_ref, *refs):
    packs, (key_ref, value_ref) = refs[:team], refs[team:]
    rows, width = key_ref.shape[0], key_ref.shape[1] // team
    for s in range(team):
        at = member_ref[0] ^ s
        cols = pl.ds(pl.multiple_of(at * width, 128), width)
        key_ref[:, cols] = packs[s][:rows, width:]
        value_ref[:, cols] = packs[s][rows:, width:]


def collect(member, packs):
    team = len(packs)
    rows, width = packs[0].shape[0] // 2, packs[0].shape[1] // 2
    shape = jax.ShapeDtypeStruct((rows, width * team), jnp.bfloat16)
    return pl.pallas_call(
        functools.partial(collect_kernel, team),
        in_specs=[pl.BlockSpec(memory_space=pltpu.SMEM)]
        + [pl.BlockSpec(memory_space=pltpu.VMEM)] * team,
        out_specs=[pl.BlockSpec(memory_space=pltpu.VMEM)] * 2,
        out_shape=[shape, shape],
        compiler_params=pltpu.CompilerParams(vmem_limit_bytes=VMEM_BYTES),
    )(member.reshape(1), *packs)


def project_kernel(n_packs, n_pieces, n_shares, where_ref, *refs):
    packs, pieces = refs[:n_packs], refs[n_packs : n_packs + n_pieces]
    refs = refs[n_packs + n_pieces :]
    outs, held, sems = refs[:-2], refs[-2], refs[-1]
    rows, width = packs[0].shape[0] // 2, packs[0].shape[1]
    depth = held.shape[1]
    copies = [
        pltpu.make_async_copy(piece, held.at[where_ref[2 + n_shares + i]], sems.at[i])
        for i, piece in enumerate(pieces)
    ]
    for copy in copies:
        copy.start()
    own = pl.multiple_of(where_ref[1] * rows, 16)
    other = pl.multiple_of((1 - where_ref[1]) * rows, 16)
    attended = [
        jnp.concatenate([x[pl.ds(own, rows), :], x[pl.ds(other, rows), :]], axis=0) for x in packs
    ]
    for copy in copies:
        copy.wait()
    for i in reversed(range(n_shares)):
        block = pl.ds(where_ref[2 + i] * INNER, INNER)
        total = jnp.zeros((2 * rows, INNER * depth), jnp.float32)
        for s in range(n_packs):
            cols = pl.ds(pl.multiple_of((where_ref[0] ^ s) * width, 128), width)
            total += nt_dot(attended[s], held[block, :, cols].reshape(INNER * depth, width))
        outs[2 * i][...] = total[:rows].astype(outs[2 * i].dtype)
        outs[2 * i + 1][...] = total[rows:].astype(outs[2 * i + 1].dtype)


def project(where, packs, pieces, n_shares):
    rows, width = packs[0].shape[0] // 2, packs[0].shape[1] // 2
    depth, local_width = pieces[0].shape
    block = INNER * depth
    whole = lambda i, w: (0, 0)
    types = [jnp.float32] + [jnp.bfloat16] * (2 * n_shares - 1)
    return pl.pallas_call(
        functools.partial(project_kernel, len(packs), len(pieces), n_shares),
        grid_spec=pltpu.PrefetchScalarGridSpec(
            num_scalar_prefetch=1,
            grid=(1,),
            in_specs=[pl.BlockSpec((2 * rows, width), whole)] * len(packs)
            + [pl.BlockSpec(memory_space=pl.ANY)] * len(pieces),
            out_specs=[pl.BlockSpec((rows, block), whole)] * len(types),
            scratch_shapes=[
                pltpu.VMEM((len(pieces), depth, local_width), jnp.bfloat16),
                pltpu.SemaphoreType.DMA((len(pieces),)),
            ],
        ),
        out_shape=[jax.ShapeDtypeStruct((rows, block), t) for t in types],
        compiler_params=pltpu.CompilerParams(vmem_limit_bytes=VMEM_BYTES),
        cost_estimate=pl.CostEstimate(
            flops=4 * rows * block * n_shares * local_width,
            bytes_accessed=2 * block * n_shares * local_width,
            transcendentals=0,
        ),
    )(where, *packs, *pieces)


def on_device(
    image,
    mod_shift,
    mod_scale,
    mod_gate,
    w_query,
    w_key,
    w_value,
    query_gain,
    key_gain,
    text_keys,
    text_values,
    stale_keys,
    stale_values,
    w_out,
):
    head_size = query_gain.shape[0]
    rows, model_width = image.shape
    depth, local_width = w_query.shape
    heads = local_width // head_size
    patches = lax.axis_size("patch")
    fsdp = lax.axis_size("fsdp")
    outer = patches // INNER
    team = math.gcd(outer, heads)
    width = local_width // team
    assert outer == 2 * fsdp and team > 1 and team & (team - 1) == 0 and outer & (outer - 1) == 0
    me = lax.axis_index("patch")
    mine = lax.axis_index("fsdp")
    place, seat = me // INNER, me % INNER
    member, parity = place % team, place % 2
    def over_outer(x, pairs):
        pairs = [(a * INNER + k, b * INNER + k) for a, b in pairs for k in range(INNER)]
        return lax.ppermute(x, "patch", pairs)

    def to_partner(x, bits):
        return over_outer(x, [(z, z ^ bits) for z in range(outer)])

    def flip(x, bits):
        return lax.ppermute(x, "patch", [(p, p ^ bits) for p in range(patches)])

    def along_fsdp(x, step):
        return lax.ppermute(x, "fsdp", [(i, (i + step) % fsdp) for i in range(fsdp)])

    def along_both(x, bits, step):
        pairs = [
            (p * fsdp + f, (p ^ (bits * INNER)) * fsdp + (f + step) % fsdp)
            for p in range(patches)
            for f in range(fsdp)
        ]
        return lax.ppermute(x, ("patch", "fsdp"), pairs)

    def spread(piece, side, *deps):
        return [piece, side, flip(after(piece, *deps), 1), flip(after(side, *deps), 1)]

    def shares_of(got):
        return [got] + [along_fsdp(got, i) for i in range(1, fsdp)]

    def seats_of(position):
        return [position * INNER + (seat ^ bits) for bits in (0, 2, 1, 3)]

    modded = modulate(image, mod_shift, mod_scale)
    share = rows // fsdp
    part = lax.dynamic_slice_in_dim(modded, mine * share, share, axis=0)
    dealt = deal(member, (w_query, w_key, w_value, stale_keys, stale_values), team)
    pieces, sides = {0: dealt[0]}, {}
    row_shares = {}
    if outer == 4 and team == 4:
        ends = [(1, 0), (2, 3)]
        middle = [(1, 2), (2, 1)]
        inside = jnp.logical_or(place == 1, place == 2)
        near = to_partner(part, 1)
        across = over_outer(part, middle)
        sides[0] = flip(pieces[0], 2)
        far = over_outer(near, middle)
        pieces[2] = to_partner(after(dealt[2], far), 2)
        pieces[1] = to_partner(after(dealt[1], near, across), 1)
        row_shares[1] = shares_of(after(near, sides[0]))
        end_across = over_outer(after(across, pieces[1]), ends)
        end_far = over_outer(after(far, row_shares[1][-1]), ends)
        sides[1] = flip(after(pieces[1], far), 2)
        pieces[3] = to_partner(after(dealt[3], far, pieces[2]), 3)
        row_shares[2] = shares_of(jnp.where(inside, far, end_across))
        row_shares[3] = shares_of(after(jnp.where(inside, across, end_far), row_shares[2][-1]))
        sides[2] = flip(pieces[2], 2)
        late = [sides[2], row_shares[2][-1]]
        later = [row_shares[3][-1]]
    else:
        for k in range(1, team):
            row_shares[k] = shares_of(to_partner(part, k))
        for k in range(1, outer):
            pieces[k] = to_partner(dealt[k % team], k)
        late = later = []
    for k in range(outer):
        if k not in sides:
            sides[k] = flip(pieces[k], 2)
    out_piece = after(w_out.T, sides[outer - 1])
    out_pieces = [out_piece] + [to_partner(out_piece, 2 * k) for k in range(1, fsdp)]

    origins = [o for k in range(outer) for o in seats_of(place ^ k)]
    deps = lambda k: late if k < 2 else later
    pieces = [x for k in range(outer) for x in spread(pieces[k], sides[k], *deps(k))]
    patch_rows = [[modded]] + [row_shares[k] for k in range(1, team)]
    where = [member] + origins
    for k in range(team):
        where.append((place ^ k) * INNER + seat)
        where += [((mine + (fsdp - i)) % fsdp) * share for i in range(fsdp)] if k else [0 * mine]
    messages = attend_patches(
        jnp.stack(where).astype(jnp.int32),
        patch_rows,
        text_keys,
        text_values,
        query_gain,
        key_gain,
        pieces,
        depth,
    )

    def give(x, bits):
        return lax.ppermute(x, "patch", [(p, p ^ (bits * INNER)) for p in range(patches)])

    packs = [messages[0]] + [give(messages[k], k) for k in range(1, team)]
    out_sides = [flip(out_pieces[0], 2)]
    out_sides += [flip(after(piece, messages[0]), 2) for piece in out_pieces[1:]]
    out_pieces = [x for p, q in zip(out_pieces, out_sides) for x in spread(p, q, *packs[1:])]
    out_places = [o for k in range(fsdp) for o in seats_of((place ^ (2 * k)) // 2)]
    where = [member, parity] + [(mine + i) % fsdp for i in range(fsdp)] + out_places
    where = jnp.stack(where).astype(jnp.int32)
    partial = project(where, packs, out_pieces, fsdp)
    own, partner = partial[0], [along_both(partial[1], 1, 0)]
    for i in range(1, fsdp):
        own = own + along_fsdp(partial[2 * i], i).astype(jnp.float32)
        partner.append(along_both(partial[2 * i + 1], 1, i))
    other = sum(x.astype(jnp.float32) for x in partner)
    summed = jnp.where(
        parity == 0,
        jnp.concatenate([own, other], axis=1),
        jnp.concatenate([other, own], axis=1),
    )
    key_out, value_out = collect(member, [after(packs[0], partial[0])] + packs[1:])

    out_share = model_width // fsdp
    col_start = mine * out_share
    image_part = lax.dynamic_slice_in_dim(image, col_start, out_share, 1).astype(jnp.float32)
    gate_part = lax.dynamic_slice_in_dim(mod_gate, col_start, out_share, 0)
    hidden = (image_part + gate_part * summed).astype(jnp.bfloat16)
    return (hidden, key_out, value_out)


def solution(mesh):
    return jax.shard_map(
        on_device,
        mesh=mesh,
        in_specs=(
            P("patch", None),
            P(),
            P(),
            P(),
            P("patch", "fsdp"),
            P("patch", "fsdp"),
            P("patch", "fsdp"),
            P(),
            P(),
            P(None, "fsdp"),
            P(None, "fsdp"),
            P("patch", "fsdp"),
            P("patch", "fsdp"),
            P("fsdp", "patch"),
        ),
        out_specs=(P("patch", "fsdp"), P("patch", "fsdp"), P("patch", "fsdp")),
        check_vma=False,
    )
```

```python
import functools
import math

import jax
import jax.numpy as jnp
from jax import lax
from jax.experimental import pallas as pl
from jax.experimental.pallas import tpu as pltpu
from jax.sharding import PartitionSpec as P

INNER = 4
VMEM_BYTES = 60 * 1024 * 1024


def modulate(image, mod_shift, mod_scale):
    values = image.astype(jnp.float32)
    center = jnp.mean(values, axis=-1, keepdims=True)
    spread = jnp.mean(jnp.square(values - center), axis=-1, keepdims=True)
    normed = (values - center) * lax.rsqrt(spread + 1e-06)
    return ((1.0 + mod_scale) * normed + mod_shift).astype(jnp.bfloat16)


def after(x, *deps):
    return lax.optimization_barrier((x,) + deps)[0]


def nt_dot(a, b):
    return lax.dot_general(a, b, (((1,), (1,)), ((), ())), preferred_element_type=jnp.float32)


def norm_heads(x, gain):
    power = jnp.mean(x * x, axis=-1, keepdims=True)
    return (x * lax.rsqrt(power + 1e-06) * gain).astype(jnp.bfloat16)


def patch_kernel(depth, n_pieces, cuts, where_ref, *refs):
    n_patches = len(cuts)
    tk_ref, tv_ref, qg_ref, kg_ref = refs[:4]
    n_rows = 1 + max(i for cut in cuts for i, _, _ in cut)
    arrays, refs = refs[4 : 4 + n_rows], refs[4 + n_rows :]
    pieces, refs = refs[:n_pieces], refs[n_pieces:]
    outs, (x_ref, held, scores, expos, x_sem, w_sem) = refs[:n_patches], refs[n_patches:]
    rows, width = outs[0].shape[0] // 2, outs[0].shape[1] // 2
    head_size = qg_ref.shape[1]
    groups = [slice(g * rows, (g + 1) * rows) for g in range(n_patches)]
    owns, x_copies, at = [], [], 1 + n_pieces
    for g, cut in enumerate(cuts):
        owns.append(where_ref[at])
        for i, (array, start, length) in enumerate(cut):
            first = pl.multiple_of(g * rows + where_ref[at + 1 + i], 16)
            x_copies.append(
                pltpu.make_async_copy(
                    arrays[array].at[pl.ds(start, length)],
                    x_ref.at[pl.ds(first, length)],
                    x_sem.at[len(x_copies)],
                )
            )
        at += 1 + len(cut)
    w_copies = [
        pltpu.make_async_copy(piece, held.at[where_ref[1 + i]], w_sem.at[i])
        for i, piece in enumerate(pieces)
    ]
    for copy in x_copies + w_copies[:INNER]:
        copy.start()
    for copy in x_copies:
        copy.wait()
    for copy in w_copies[INNER:]:
        copy.start()

    chunk = INNER * depth
    proj = [jnp.zeros((n_patches * rows, width), jnp.float32) for _ in range(3)]
    if chunk % 128 == 0:
        for first in range(0, n_pieces, INNER):
            for copy in w_copies[first : first + INNER]:
                copy.wait()
            place = where_ref[1 + first] // INNER
            part = x_ref[:, pl.ds(pl.multiple_of(place * chunk, 128), chunk)]
            for i in range(3):
                weight = held[pl.ds(place * INNER, INNER), i * depth : (i + 1) * depth, :]
                proj[i] += jnp.dot(
                    part, weight.reshape(chunk, width), preferred_element_type=jnp.float32
                )
    else:
        for copy in w_copies:
            copy.wait()
        for i in range(3):
            weight = held[:, i * depth : (i + 1) * depth, :]
            proj[i] += jnp.dot(
                x_ref[...],
                weight.reshape(n_pieces * depth, width),
                preferred_element_type=jnp.float32,
            )
    q_proj, k_proj, v_proj = proj

    v_new = v_proj.astype(jnp.bfloat16)
    k0, v0 = 3 * depth, 3 * depth + rows
    scale = math.log2(math.e) / math.sqrt(head_size)
    own_cols = [pl.ds(pl.multiple_of(own * rows, 128), rows) for own in owns]
    for h in range(width // head_size):
        cols = slice(h * head_size, (h + 1) * head_size)
        beside = slice(width + cols.start, width + cols.stop)
        query = norm_heads(q_proj[:, cols], qg_ref[...])
        key = norm_heads(k_proj[:, cols], kg_ref[...])
        value = v_new[:, cols]
        keys = held[:, k0 : k0 + rows, cols].reshape(n_pieces * rows, head_size)
        values = held[:, v0 : v0 + rows, cols].reshape(n_pieces * rows, head_size)
        scores[h] = nt_dot(query, keys)
        for g, group in enumerate(groups):
            scores[h, group, own_cols[g]] = nt_dot(query[group], key[group])
            outs[g][:rows, beside] = key[group]
            outs[g][rows:, beside] = value[group]
        text_s = nt_dot(query, tk_ref[:, cols])
        image_s = scores[h]
        largest = jnp.maximum(
            jnp.max(text_s, axis=-1, keepdims=True), jnp.max(image_s, axis=-1, keepdims=True)
        )
        text_e = jnp.exp2((text_s - largest) * scale)
        image_e = jnp.exp2((image_s - largest) * scale)
        total = jnp.sum(text_e, axis=-1, keepdims=True) + jnp.sum(image_e, axis=-1, keepdims=True)
        expos[h] = image_e.astype(jnp.bfloat16)
        fresh_mix = []
        for g, group in enumerate(groups):
            fresh_mix.append(
                jnp.dot(
                    expos[h, group, own_cols[g]], value[group], preferred_element_type=jnp.float32
                )
            )
            expos[h, group, own_cols[g]] = jnp.zeros((rows, rows), jnp.bfloat16)
        mixture = (
            jnp.dot(text_e.astype(jnp.bfloat16), tv_ref[:, cols], preferred_element_type=jnp.float32)
            + jnp.dot(expos[h], values, preferred_element_type=jnp.float32)
            + jnp.concatenate(fresh_mix, axis=0)
        )
        attended = (mixture / total).astype(jnp.bfloat16)
        for g, group in enumerate(groups):
            first = pl.multiple_of(lax.rem(owns[g] // INNER, 2) * rows, 16)
            for out in outs[g // 2 * 2 : g // 2 * 2 + 2]:
                out[pl.ds(first, rows), cols] = attended[group]


def attend_patches(where, patches, text_keys, text_values, query_gain, key_gain, pieces, depth):
    arrays, cuts, (rows, model_width), width = [], [], patches[0][0].shape, pieces[0].shape[1]
    for patch in patches:
        cuts.append([])
        for x in patch:
            x, start = x if isinstance(x, tuple) else (x, 0)
            held = [i for i, y in enumerate(arrays) if y is x]
            if not held:
                arrays.append(x)
            place = held[0] if held else len(arrays) - 1
            cuts[-1].append((place, start, rows // len(patch)))
    n, n_pieces, texts, head_size = len(patches), len(pieces), text_keys.shape[0], query_gain.shape[0]
    heads, n_keys = width // head_size, n_pieces * rows
    whole = lambda i, w: (0, 0)
    return pl.pallas_call(
        functools.partial(patch_kernel, depth, n_pieces, cuts),
        grid_spec=pltpu.PrefetchScalarGridSpec(
            num_scalar_prefetch=1,
            grid=(1,),
            in_specs=[pl.BlockSpec((texts, width), lambda i, w: (0, w[0]))] * 2
            + [pl.BlockSpec((1, head_size), whole)] * 2
            + [pl.BlockSpec(memory_space=pl.ANY)] * (len(arrays) + n_pieces),
            out_specs=[pl.BlockSpec((2 * rows, 2 * width), whole)] * n,
            scratch_shapes=[
                pltpu.VMEM((n * rows, model_width), jnp.bfloat16),
                pltpu.VMEM((n_pieces,) + pieces[0].shape, jnp.bfloat16),
                pltpu.VMEM((heads, n * rows, n_keys), jnp.float32),
                pltpu.VMEM((heads, n * rows, n_keys), jnp.bfloat16),
                pltpu.SemaphoreType.DMA((sum(len(cut) for cut in cuts),)),
                pltpu.SemaphoreType.DMA((n_pieces,)),
            ],
        ),
        out_shape=[jax.ShapeDtypeStruct((2 * rows, 2 * width), jnp.bfloat16)] * n,
        compiler_params=pltpu.CompilerParams(vmem_limit_bytes=VMEM_BYTES),
        cost_estimate=pl.CostEstimate(
            flops=2 * n * rows * (model_width * 3 * width + 2 * (texts + n_keys) * width),
            bytes_accessed=2 * n_pieces * pieces[0].size,
            transcendentals=n * rows * (texts + n_keys) * heads,
        ),
    )(
        where,
        text_keys,
        text_values,
        query_gain.reshape(1, -1),
        key_gain.reshape(1, -1),
        *arrays,
        *pieces,
    )


def deal_kernel(n_arrays, team, member_ref, *refs):
    arrays, outs = refs[:n_arrays], refs[n_arrays:]
    width = outs[0].shape[1]
    for k in range(team):
        at = member_ref[0] ^ k
        cols = pl.ds(pl.multiple_of(at * width, 128), width)
        first = 0
        for x in arrays:
            rows = x.shape[0]
            outs[k][first : first + rows, :] = x[:, cols]
            first += rows


def deal(member, arrays, team):
    width = arrays[0].shape[1] // team
    shape = jax.ShapeDtypeStruct((sum(x.shape[0] for x in arrays), width), jnp.bfloat16)
    return pl.pallas_call(
        functools.partial(deal_kernel, len(arrays), team),
        in_specs=[pl.BlockSpec(memory_space=pltpu.SMEM)]
        + [pl.BlockSpec(memory_space=pltpu.VMEM)] * len(arrays),
        out_specs=[pl.BlockSpec(memory_space=pltpu.VMEM)] * team,
        out_shape=[shape] * team,
        compiler_params=pltpu.CompilerParams(vmem_limit_bytes=VMEM_BYTES),
    )(member.reshape(1), *arrays)


def collect_kernel(team, member_ref, *refs):
    packs, (key_ref, value_ref) = refs[:team], refs[team:]
    rows, width = key_ref.shape[0], key_ref.shape[1] // team
    for s in range(team):
        at = member_ref[0] ^ s
        cols = pl.ds(pl.multiple_of(at * width, 128), width)
        key_ref[:, cols] = packs[s][:rows, width:]
        value_ref[:, cols] = packs[s][rows:, width:]


def collect(member, packs):
    team = len(packs)
    rows, width = packs[0].shape[0] // 2, packs[0].shape[1] // 2
    shape = jax.ShapeDtypeStruct((rows, width * team), jnp.bfloat16)
    return pl.pallas_call(
        functools.partial(collect_kernel, team),
        in_specs=[pl.BlockSpec(memory_space=pltpu.SMEM)]
        + [pl.BlockSpec(memory_space=pltpu.VMEM)] * team,
        out_specs=[pl.BlockSpec(memory_space=pltpu.VMEM)] * 2,
        out_shape=[shape, shape],
        compiler_params=pltpu.CompilerParams(vmem_limit_bytes=VMEM_BYTES),
    )(member.reshape(1), *packs)


def project_kernel(n_packs, n_pieces, n_shares, where_ref, *refs):
    packs, pieces = refs[:n_packs], refs[n_packs : n_packs + n_pieces]
    refs = refs[n_packs + n_pieces :]
    outs, held, sems = refs[:-2], refs[-2], refs[-1]
    rows, width = packs[0].shape[0] // 2, packs[0].shape[1]
    depth = held.shape[1]
    copies = [
        pltpu.make_async_copy(piece, held.at[where_ref[2 + n_shares + i]], sems.at[i])
        for i, piece in enumerate(pieces)
    ]
    for copy in copies:
        copy.start()
    own = pl.multiple_of(where_ref[1] * rows, 16)
    other = pl.multiple_of((1 - where_ref[1]) * rows, 16)
    attended = [
        jnp.concatenate([x[pl.ds(own, rows), :], x[pl.ds(other, rows), :]], axis=0) for x in packs
    ]
    for copy in copies:
        copy.wait()
    for i in reversed(range(n_shares)):
        block = pl.ds(where_ref[2 + i] * INNER, INNER)
        total = jnp.zeros((2 * rows, INNER * depth), jnp.float32)
        for s in range(n_packs):
            cols = pl.ds(pl.multiple_of((where_ref[0] ^ s) * width, 128), width)
            total += nt_dot(attended[s], held[block, :, cols].reshape(INNER * depth, width))
        outs[2 * i][...] = total[:rows].astype(outs[2 * i].dtype)
        outs[2 * i + 1][...] = total[rows:].astype(outs[2 * i + 1].dtype)


def project(where, packs, pieces, n_shares):
    rows, width = packs[0].shape[0] // 2, packs[0].shape[1] // 2
    depth, local_width = pieces[0].shape
    block = INNER * depth
    whole = lambda i, w: (0, 0)
    types = [jnp.float32] + [jnp.bfloat16] * (2 * n_shares - 1)
    return pl.pallas_call(
        functools.partial(project_kernel, len(packs), len(pieces), n_shares),
        grid_spec=pltpu.PrefetchScalarGridSpec(
            num_scalar_prefetch=1,
            grid=(1,),
            in_specs=[pl.BlockSpec((2 * rows, width), whole)] * len(packs)
            + [pl.BlockSpec(memory_space=pl.ANY)] * len(pieces),
            out_specs=[pl.BlockSpec((rows, block), whole)] * len(types),
            scratch_shapes=[
                pltpu.VMEM((len(pieces), depth, local_width), jnp.bfloat16),
                pltpu.SemaphoreType.DMA((len(pieces),)),
            ],
        ),
        out_shape=[jax.ShapeDtypeStruct((rows, block), t) for t in types],
        compiler_params=pltpu.CompilerParams(vmem_limit_bytes=VMEM_BYTES),
        cost_estimate=pl.CostEstimate(
            flops=4 * rows * block * n_shares * local_width,
            bytes_accessed=2 * block * n_shares * local_width,
            transcendentals=0,
        ),
    )(where, *packs, *pieces)


def on_device(
    image,
    mod_shift,
    mod_scale,
    mod_gate,
    w_query,
    w_key,
    w_value,
    query_gain,
    key_gain,
    text_keys,
    text_values,
    stale_keys,
    stale_values,
    w_out,
):
    head_size = query_gain.shape[0]
    rows, model_width = image.shape
    depth, local_width = w_query.shape
    heads = local_width // head_size
    patches = lax.axis_size("patch")
    fsdp = lax.axis_size("fsdp")
    outer = patches // INNER
    team = math.gcd(outer, heads)
    width = local_width // team
    assert outer == 2 * fsdp and team > 1 and team & (team - 1) == 0 and outer & (outer - 1) == 0
    me = lax.axis_index("patch")
    mine = lax.axis_index("fsdp")
    place, seat = me // INNER, me % INNER
    member, parity = place % team, place % 2
    def over_outer(x, pairs):
        pairs = [(a * INNER + k, b * INNER + k) for a, b in pairs for k in range(INNER)]
        return lax.ppermute(x, "patch", pairs)

    def to_partner(x, bits):
        return over_outer(x, [(z, z ^ bits) for z in range(outer)])

    def flip(x, bits):
        return lax.ppermute(x, "patch", [(p, p ^ bits) for p in range(patches)])

    def along_fsdp(x, step):
        return lax.ppermute(x, "fsdp", [(i, (i + step) % fsdp) for i in range(fsdp)])

    def along_both(x, bits, step):
        pairs = [
            (p * fsdp + f, (p ^ (bits * INNER)) * fsdp + (f + step) % fsdp)
            for p in range(patches)
            for f in range(fsdp)
        ]
        return lax.ppermute(x, ("patch", "fsdp"), pairs)

    def spread(piece, side, *deps):
        return [piece, side, flip(after(piece, *deps), 1), flip(after(side, *deps), 1)]

    def shares_of(got):
        return [got] + [along_fsdp(got, i) for i in range(1, fsdp)]

    def seats_of(position):
        return [position * INNER + (seat ^ bits) for bits in (0, 2, 1, 3)]

    modded = modulate(image, mod_shift, mod_scale)
    share = rows // fsdp
    part = lax.dynamic_slice_in_dim(modded, mine * share, share, axis=0)
    dealt = deal(member, (w_query, w_key, w_value, stale_keys, stale_values), team)
    pieces, sides = {0: dealt[0]}, {}
    row_shares = {}
    if outer == 4 and team == 4:
        ends = [(1, 0), (2, 3)]
        middle = [(1, 2), (2, 1)]
        inside = jnp.logical_or(place == 1, place == 2)
        near = to_partner(part, 1)
        across = over_outer(part, middle)
        sides[0] = flip(pieces[0], 2)
        far = over_outer(near, middle)
        pieces[2] = to_partner(after(dealt[2], far), 2)
        pieces[1] = to_partner(after(dealt[1], near, across), 1)
        row_shares[1] = shares_of(after(near, sides[0]))
        end_across = over_outer(after(across, pieces[1]), ends)
        end_far = over_outer(after(far, row_shares[1][-1]), ends)
        sides[1] = flip(after(pieces[1], far), 2)
        pieces[3] = to_partner(after(dealt[3], far, pieces[2]), 3)
        row_shares[2] = shares_of(jnp.where(inside, far, end_across))
        row_shares[3] = shares_of(after(jnp.where(inside, across, end_far), row_shares[2][-1]))
        sides[2] = flip(pieces[2], 2)
        late = [sides[2], row_shares[2][-1]]
        later = [row_shares[3][-1]]
    else:
        for k in range(1, team):
            row_shares[k] = shares_of(to_partner(part, k))
        for k in range(1, outer):
            pieces[k] = to_partner(dealt[k % team], k)
        late = later = []
    for k in range(outer):
        if k not in sides:
            sides[k] = flip(pieces[k], 2)
    out_piece = after(w_out.T, sides[outer - 1])
    out_pieces = [out_piece] + [to_partner(out_piece, 2 * k) for k in range(1, fsdp)]

    origins = [o for k in range(outer) for o in seats_of(place ^ k)]
    deps = lambda k: late if k < 2 else later
    pieces = [x for k in range(outer) for x in spread(pieces[k], sides[k], *deps(k))]
    patch_rows = [[modded]] + [row_shares[k] for k in range(1, team)]
    where = [member] + origins
    for k in range(team):
        where.append((place ^ k) * INNER + seat)
        where += [((mine + (fsdp - i)) % fsdp) * share for i in range(fsdp)] if k else [0 * mine]
    messages = attend_patches(
        jnp.stack(where).astype(jnp.int32),
        patch_rows,
        text_keys,
        text_values,
        query_gain,
        key_gain,
        pieces,
        depth,
    )

    def give(x, bits):
        return lax.ppermute(x, "patch", [(p, p ^ (bits * INNER)) for p in range(patches)])

    packs = [messages[0]] + [give(messages[k], k) for k in range(1, team)]
    out_sides = [flip(out_pieces[0], 2)]
    out_sides += [flip(after(piece, messages[0]), 2) for piece in out_pieces[1:]]
    out_pieces = [x for p, q in zip(out_pieces, out_sides) for x in spread(p, q, *packs[1:3])]
    out_places = [o for k in range(fsdp) for o in seats_of((place ^ (2 * k)) // 2)]
    where = [member, parity] + [(mine + i) % fsdp for i in range(fsdp)] + out_places
    where = jnp.stack(where).astype(jnp.int32)
    partial = project(where, packs, out_pieces, fsdp)
    own, partner = partial[0], [along_both(partial[1], 1, 0)]
    for i in range(1, fsdp):
        own = own + along_fsdp(partial[2 * i], i).astype(jnp.float32)
        partner.append(along_both(partial[2 * i + 1], 1, i))
    other = sum(x.astype(jnp.float32) for x in partner)
    summed = jnp.where(
        parity == 0,
        jnp.concatenate([own, other], axis=1),
        jnp.concatenate([other, own], axis=1),
    )
    key_out, value_out = collect(member, [after(packs[0], partial[0])] + packs[1:])

    out_share = model_width // fsdp
    col_start = mine * out_share
    image_part = lax.dynamic_slice_in_dim(image, col_start, out_share, 1).astype(jnp.float32)
    gate_part = lax.dynamic_slice_in_dim(mod_gate, col_start, out_share, 0)
    hidden = (image_part + gate_part * summed).astype(jnp.bfloat16)
    return (hidden, key_out, value_out)


def solution(mesh):
    return jax.shard_map(
        on_device,
        mesh=mesh,
        in_specs=(
            P("patch", None),
            P(),
            P(),
            P(),
            P("patch", "fsdp"),
            P("patch", "fsdp"),
            P("patch", "fsdp"),
            P(),
            P(),
            P(None, "fsdp"),
            P(None, "fsdp"),
            P("patch", "fsdp"),
            P("patch", "fsdp"),
            P("fsdp", "patch"),
        ),
        out_specs=(P("patch", "fsdp"), P("patch", "fsdp"), P("patch", "fsdp")),
        check_vma=False,
    )
```
